32 devices in a mesh: groups: 2 (over y), gx: 4 (over z), gy: 4 (over x, core).
Axes of the slice: x: 2, y: 2, z: 4, core: 2. Of those that a mesh axis runs over, the one named last changes fastest.
Arguments:
- velocity: float32 [4, 64, 1024], P('groups', 'gx', 'gy'), parts along dimension 0, may hold values from -6 to 6
- kernel_in: bfloat16 [64, 2, 3, 3], replicated, may hold values from -1.5 to 1.5
- bias_in: float32 [64], replicated, may hold values from -3 to 3
- kernel_mid: bfloat16 [64, 64, 3, 3], replicated, may hold values from -0.25 to 0.25
- bias_mid: float32 [64], replicated, may hold values from -3 to 3
- kernel_out: bfloat16 [12, 64, 3, 3], replicated, may hold values from -0.07470703 to 0.07470703
- bias_out: float32 [12], replicated, may hold values from -3 to 3
- cotangent: float32 [4, 64, 1024], P('groups', 'gx', 'gy'), parts along dimension 0, may hold values from -6 to 6
Outputs:
- new_velocity: float32 [4, 64, 1024], P('groups', 'gx', 'gy'), parts along dimension 0
- grad_velocity: float32 [4, 64, 1024], P('groups', 'gx', 'gy'), parts along dimension 0
- grad_kernel_in: float32 [128, 2, 3, 3], P('groups'), parts along dimension 0
- grad_bias_in: float32 [128], P('groups'), parts along dimension 0
- grad_kernel_mid: float32 [128, 64, 3, 3], P('groups'), parts along dimension 0
- grad_bias_mid: float32 [128], P('groups'), parts along dimension 0
- grad_kernel_out: float32 [24, 64, 3, 3], P('groups'), parts along dimension 0
- grad_bias_out: float32 [24], P('groups'), parts along dimension 0
The draws below stay inside these ranges and needn't reach their ends.
There are 2 independent parts, one for each index of `groups`. The reference program is written for one: setup_inputs(seed, part) draws one part's arguments, and reference() takes and returns one part's arrays. A program takes and returns all parts, laid end to end along the dimension named above; an argument that names none is the same for every part. Nothing has to cross between parts.
All inputs are finite; a program needn't handle non-finite values.
Results may differ from the reference program's by a relative error of at most 0.017.
Values may be sent and summed in bfloat16 or wider, within the bound.
No kernel may reach another device: no remote copies, remote signals or barrier semaphores. Data moves between devices by JAX's collectives and lax.ppermute only.
A program may use at most 64 MiB of HBM per device.

```python
import math
import jax
import jax.numpy as jnp
from jax import lax

HID = 64
COEF = 12
NX = 64
NY = 1024


def levels(key, dims, split, smallest, top_value):
    gain = 1.0
    for axis_at, shards_of in split:
        draws = jax.random.uniform(jax.random.fold_in(jax.random.fold_in(key, 6), axis_at), (shards_of,), jnp.float32, smallest / len(split), top_value / len(split))
        gain = gain * jnp.repeat(jnp.exp(draws), dims[axis_at] // shards_of).reshape((-1,) + (1,) * (len(dims) - 1 - axis_at))
    return gain


def bell_draw(own_key, shape, spread, limit, pieces=(), kind=jnp.bfloat16):
    drawn = spread * jax.random.normal(own_key, shape, jnp.float32)
    if pieces:
        drawn = drawn * levels(own_key, shape, pieces, -0.22, 0.18)
    return jnp.clip(drawn, -limit, limit).astype(kind)


def setup_inputs(seed: int = 0, part: int = 0) -> dict:
    key_of = jax.random.split(jax.random.key(seed), 9)
    part_splits = jax.random.split(jax.random.fold_in(key_of[8], part), 9)
    return {
        "velocity": bell_draw(part_splits[0], (2, NX, NY), 1.0, 6.0, ((1, 4), (2, 4)), jnp.float32),
        "kernel_in": bell_draw(key_of[1], (HID, 2, 3, 3), 18 ** -0.5, 1.5),
        "bias_in": bell_draw(key_of[2], (HID,), 0.5, 3.0, (), jnp.float32),
        "kernel_mid": bell_draw(key_of[3], (HID, HID, 3, 3), (9 * HID) ** -0.5, 0.25),
        "bias_mid": bell_draw(key_of[4], (HID,), 0.5, 3.0, (), jnp.float32),
        "kernel_out": bell_draw(key_of[5], (COEF, HID, 3, 3), (0.3 / (9 * HID) ** 0.5), 0.07470703),
        "bias_out": bell_draw(key_of[6], (COEF,), 0.5, 3.0, (), jnp.float32),
        "cotangent": bell_draw(part_splits[7], (2, NX, NY), 1.0, 6.0, ((1, 4), (2, 4)), jnp.float32),
    }


rim_depth = 4
advection = 0.2
viscosity = 0.05
forcing_amp = 0.05
forcing_wave = 4
face_base = ((0.0, 0.5, 0.0, 0.0, 0.5, 0.0), (0.0, 0.0, 0.5, 0.5, 0.0, 0.0))

def convolve(inputs, kernel):
    return lax.conv_general_dilated(inputs.astype(jnp.float32)[None], kernel.astype(jnp.float32), (1, 1), 'VALID', dimension_numbers=('NCHW', 'OIHW', 'NCHW'), precision=lax.Precision.HIGHEST)[0]

def kernel_grad(inputs, rounded):
    out_rows = rounded.shape[1]
    out_cols = rounded.shape[2]
    flat_grad = rounded.astype(jnp.float32).reshape(rounded.shape[0], -1)
    blocks = []
    for offset_x in range(3):
        for offset_y in range(3):
            window = inputs[:, offset_x:offset_x + out_rows, offset_y:offset_y + out_cols].astype(jnp.float32)
            blocks.append(lax.dot_general(flat_grad, window.reshape(window.shape[0], -1), (((1,), (1,)), ((), ())), precision=lax.Precision.HIGHEST))
    stacked = jnp.stack(blocks, axis=2)
    return stacked.reshape(stacked.shape[0], stacked.shape[1], 3, 3)

def input_grad(rounded, kernel):
    flipped = jnp.transpose(kernel[:, :, ::-1, ::-1], (1, 0, 2, 3))
    padded = jnp.pad(rounded, ((0, 0), (2, 2), (2, 2)))
    return convolve(padded, flipped)

def silu_slope(linear):
    sigma = jax.nn.sigmoid(linear)
    return sigma * (1.0 + linear * (1.0 - sigma))

def layer_forward(inputs, kernel, layer_bias):
    linear = convolve(inputs, kernel) + layer_bias[:, None, None]
    return (linear, jax.nn.silu(linear).astype(jnp.bfloat16))

def layer_backward(inputs, linear, grad_act, kernel):
    grad_pre = grad_act * silu_slope(linear)
    rounded = grad_pre.astype(jnp.bfloat16)
    return (kernel_grad(inputs, rounded), lax.optimization_barrier(jnp.sum(grad_pre, axis=(1, 2))), input_grad(rounded, kernel))

def advect(padded_field, head_ext, col_start, ny_total):
    row_count = padded_field.shape[1] - 2
    col_count = padded_field.shape[2] - 2
    correction = head_ext.reshape(2, 6, row_count + 2, col_count + 2)
    correction = correction - lax.optimization_barrier(jnp.mean(correction, axis=1, keepdims=True))
    stencil = correction + jnp.array(face_base, jnp.float32)[:, :, None, None]
    face_x = jnp.zeros((2, row_count + 1, col_count), jnp.float32)
    for offset_x in range(2):
        for offset_y in range(-1, 2):
            weight_now = stencil[0, offset_x * 3 + offset_y + 1, :row_count + 1, 1:col_count + 1]
            face_x = face_x + weight_now * padded_field[:, offset_x:offset_x + row_count + 1, 1 + offset_y:1 + offset_y + col_count]
    normal_x = 0.5 * (padded_field[0, :row_count + 1, 1:col_count + 1] + padded_field[0, 1:row_count + 2, 1:col_count + 1])
    flux_x = normal_x * face_x
    face_y = jnp.zeros((2, row_count, col_count + 1), jnp.float32)
    for offset_x in range(-1, 2):
        for offset_y in range(2):
            weight_now = stencil[1, (offset_x + 1) * 2 + offset_y, 1:row_count + 1, :col_count + 1]
            face_y = face_y + weight_now * padded_field[:, 1 + offset_x:1 + offset_x + row_count, offset_y:offset_y + col_count + 1]
    normal_y = 0.5 * (padded_field[1, 1:row_count + 1, :col_count + 1] + padded_field[1, 1:row_count + 1, 1:col_count + 2])
    flux_y = normal_y * face_y
    divergence = flux_x[:, 1:, :] - flux_x[:, :-1, :] + flux_y[:, :, 1:] - flux_y[:, :, :-1]
    centre = padded_field[:, 1:-1, 1:-1]
    laplace_term = padded_field[:, 2:, 1:-1] + padded_field[:, :-2, 1:-1] + padded_field[:, 1:-1, 2:] + padded_field[:, 1:-1, :-2] - 4.0 * centre
    columns = (lax.iota(jnp.int32, col_count) + col_start).astype(jnp.float32)
    forcing = forcing_amp * jnp.sin(2.0 * math.pi * forcing_wave * columns / ny_total)
    forcing_field = jnp.stack([jnp.broadcast_to(forcing, (row_count, col_count)), jnp.zeros((row_count, col_count), jnp.float32)])
    return centre - advection * divergence + viscosity * laplace_term + forcing_field

def fold_wrap(grad_ext, rim_width):
    middle = grad_ext[:, rim_width:-rim_width, :]
    middle = middle.at[:, :rim_width].add(grad_ext[:, -rim_width:, :]).at[:, -rim_width:].add(grad_ext[:, :rim_width, :])
    interior = middle[:, :, rim_width:-rim_width]
    return interior.at[:, :, :rim_width].add(middle[:, :, -rim_width:]).at[:, :, -rim_width:].add(middle[:, :, :rim_width])

def reference(velocity, kernel_in, bias_in, kernel_mid, bias_mid, kernel_out, bias_out, cotangent):
    deep_ext = jnp.pad(velocity, ((0, 0), (rim_depth, rim_depth), (rim_depth, rim_depth)), mode='wrap')
    inputs = deep_ext.astype(jnp.bfloat16)
    pre_one, act_one = layer_forward(inputs, kernel_in, bias_in)
    pre_two, act_two = layer_forward(act_one, kernel_mid, bias_mid)
    head_out = convolve(act_two, kernel_out) + bias_out[:, None, None]
    state_ext = deep_ext[:, 3:-3, 3:-3]

    def advance(padded_field, head_ext):
        return advect(padded_field, head_ext, 0, NY)
    new_velocity, pullback = jax.vjp(advance, state_ext, head_out)
    grad_state, grad_head = pullback(cotangent)
    rounded = grad_head.astype(jnp.bfloat16)
    grad_kernel_out = kernel_grad(act_two, rounded)
    grad_bias_out = lax.optimization_barrier(jnp.sum(grad_head, axis=(1, 2)))
    grad_two = input_grad(rounded, kernel_out)
    grad_kernel_mid, grad_bias_mid, grad_one = layer_backward(act_one, pre_two, grad_two, kernel_mid)
    grad_kernel_in, grad_bias_in, grad_input = layer_backward(inputs, pre_one, grad_one, kernel_in)
    grad_total = grad_input + jnp.pad(grad_state, ((0, 0), (3, 3), (3, 3)))
    grad_velocity = fold_wrap(grad_total, rim_depth)
    grad_scale = 1.0 / math.sqrt(NX * NY)
    return (new_velocity, grad_velocity, grad_kernel_in * grad_scale, grad_bias_in * grad_scale, grad_kernel_mid * grad_scale, grad_bias_mid * grad_scale, grad_kernel_out * grad_scale, grad_bias_out * grad_scale)
```

```python
import math

import jax
import jax.numpy as jnp
from jax import lax
from jax.experimental import pallas as pl
from jax.experimental.pallas import tpu as pltpu
from jax.sharding import PartitionSpec as P

advection = 0.2
viscosity = 0.05
forcing_amp = 0.05
forcing_wave = 4
face_base = ((0.0, 0.5, 0.0, 0.0, 0.5, 0.0), (0.0, 0.0, 0.5, 0.5, 0.0, 0.0))
halo = 4
hid = 64
coef = 12
slot = 16
taps_x = [(a, b) for a in (0, 1) for b in (-1, 0, 1)]
taps_y = [(a, b) for a in (-1, 0, 1) for b in (0, 1)]
f32 = jnp.float32
bf16 = jnp.bfloat16


def shift(value, rows, cols):
    if rows:
        value = pltpu.roll(value, (-rows) % value.shape[-2], value.ndim - 2)
    if cols:
        value = pltpu.roll(value, (-cols) % value.shape[-1], value.ndim - 1)
    return value


def mm(lhs, rhs):
    return lax.dot_general(lhs, rhs, (((1,), (0,)), ((), ())), preferred_element_type=f32)


def mm_nt(lhs, rhs):
    return lax.dot_general(lhs, rhs, (((1,), (1,)), ((), ())), preferred_element_type=f32)


def sigma_of(linear):
    return 0.5 * jnp.tanh(0.5 * linear) + 0.5


def store_shifted(refs, at, value):
    rows = value.shape[0]
    for b in range(3):
        refs[b, at : at + rows, :] = shift(value, 0, b - 1).astype(refs.dtype)


def put_plane(planes, k, stride, value):
    for j in range(planes.shape[0]):
        planes[j, pl.ds(k, value.shape[0], stride=stride), :] = value[:, 128 * j : 128 * j + 128]


def take_plane(planes, k, count, stride):
    tiles = [planes[j, pl.ds(k, count, stride=stride), :] for j in range(planes.shape[0])]
    return jnp.concatenate(tiles, axis=1)


def take_rows(planes, at, size):
    return jnp.concatenate([planes[j, at : at + size, :] for j in range(planes.shape[0])], axis=1)


def put_rows(planes, at, value):
    for j in range(planes.shape[0]):
        planes[j, at : at + value.shape[0], :] = value[:, 128 * j : 128 * j + 128]


def faces(w0, w1):
    normal_x = 0.5 * (w0 + shift(w0, 1, 0))
    normal_y = 0.5 * (w1 + shift(w1, 0, 1))
    return normal_x, normal_y


def shifted_fields(w):
    table = {}
    for b in (-1, 0, 1):
        col = shift(w, 0, b)
        for a in (-1, 0, 1):
            table[a, b] = shift(col, a, 0)
    return table


def lane_sums(total):
    lanes = total.shape[1]
    part = total[:, :128]
    for k in range(1, lanes // 128):
        part = part + total[:, 128 * k : 128 * k + 128]
    return jnp.sum(part.T, axis=0, keepdims=True)


def backward_kernel(
    rows,
    cols,
    ext_ref,
    w_in_ref,
    w_mid_ref,
    w_mid_t_ref,
    w_out_t_ref,
    b_in_ref,
    b_mid_ref,
    pay_ref,
    act_two_ref,
    grad_one_ref,
    stage,
    state_in,
    head_in,
    act_one,
    slope_one,
    grad_two,
    acc_mid,
    acc_small,
    bias_acc,
):
    height, width = stage.shape[1], stage.shape[2]
    deep = rows + 2 * halo
    stage[...] = jnp.zeros(stage.shape, f32)
    stage[:, 0:deep, 0 : cols + 2 * halo] = ext_ref[...]
    w0, w1, c0, c1 = stage[0], stage[1], stage[2], stage[3]
    lane = lax.broadcasted_iota(jnp.int32, (1, width), 1)
    own_cols = (lane >= halo) & (lane < halo + cols)

    planes = head_in
    planes[...] = jnp.zeros(planes.shape, f32)
    put_plane(planes, 0, slot, w0)
    put_plane(planes, 1, slot, w1)
    for r in range(0, deep, 2):
        store_shifted(state_in.at[0], r * slot, take_rows(planes, r * slot, 2 * slot))

    normal_x, normal_y = faces(w0, w1)
    t0, t1 = shifted_fields(w0), shifted_fields(w1)
    fx0 = -advection * (c0 - shift(c0, 1, 0)) * normal_x
    fx1 = -advection * (c1 - shift(c1, 1, 0)) * normal_x
    fy0 = -advection * (c0 - shift(c0, 0, 1)) * normal_y
    fy1 = -advection * (c1 - shift(c1, 0, 1)) * normal_y
    row_id = lax.broadcasted_iota(jnp.int32, (height, width), 0)
    own = own_cols & (row_id >= halo) & (row_id < halo + rows)
    sums = []
    for at, taps, g0, g1 in ((0, taps_x, fx0, fx1), (6, taps_y, fy0, fy1)):
        raw = [g0 * t0[tap] + g1 * t1[tap] for tap in taps]
        mean = sum(raw[1:], raw[0]) * (1.0 / 6.0)
        for k in range(6):
            value = raw[k] - mean
            put_plane(planes, at + k, slot, value)
            sums.append(jnp.sum(jnp.where(own, value, 0.0), axis=0, keepdims=True))
    for r in range(0, deep, 2):
        store_shifted(state_in.at[1], r * slot, take_rows(planes, r * slot, 2 * slot))
    bias_out = jnp.concatenate(sums + [jnp.zeros((128 - coef, width), f32)], axis=0)

    w_in = w_in_ref[...]
    b_in = b_in_ref[...]
    for r in range(1, deep - 1, 2):
        fed = jnp.concatenate(
            [state_in[0, b, (r - 1) * slot : (r + 3) * slot, :] for b in range(3)], axis=0
        )
        linear = mm(w_in, fed) + b_in
        sigma = sigma_of(linear)
        act = linear * sigma
        store_shifted(act_one, (r - 1) * hid, act)
        slope_one[(r - 1) * hid : (r + 1) * hid, :] = sigma + act * (1.0 - sigma)

    b_mid = b_mid_ref[...]
    w_out_t = w_out_t_ref[...]
    bias_acc[...] = jnp.zeros(bias_acc.shape, f32)
    acc_mid[...] = jnp.zeros(acc_mid.shape, f32)
    acc_small[...] = jnp.zeros(acc_small.shape, f32)
    for r in range(2, deep - 2, 2):
        mine = halo <= r < halo + rows
        linear = b_mid
        window = [act_one[b, (r - 2) * hid : (r + 2) * hid, :] for b in range(3)]
        for b in range(3):
            linear = linear + mm(w_mid_ref[b], window[b])
        sigma = sigma_of(linear)
        act = linear * sigma
        act_short = act.astype(bf16)
        act_two_ref[(r - 2) * hid : r * hid, :] = act_short
        fed = jnp.concatenate(
            [state_in[1, b, (r - 1) * slot : (r + 3) * slot, :] for b in range(3)], axis=0
        )
        grad = mm(w_out_t, fed) * (sigma + act * (1.0 - sigma))
        store_shifted(grad_two, (r - 2) * hid, grad)
        if mine:
            kept = jnp.where(own_cols, grad, 0.0)
            bias_acc[0] += kept
            kept = kept.astype(bf16)
            for b in range(3):
                acc_mid[b] += mm_nt(kept, window[b])
            acc_small[0] += mm_nt(fed, jnp.where(own_cols, act, 0.0).astype(bf16))

    for r in range(3, deep - 3, 2):
        grad = mm(w_mid_t_ref[0], grad_two[0, (r - 3) * hid : (r + 1) * hid, :])
        for b in (1, 2):
            grad = grad + mm(w_mid_t_ref[b], grad_two[b, (r - 3) * hid : (r + 1) * hid, :])
        grad = grad * slope_one[(r - 1) * hid : (r + 1) * hid, :]
        grad_one_ref[(r - 3) * hid : (r - 1) * hid, :] = grad.astype(bf16)
        kept = jnp.where(own_cols, grad, 0.0)
        if r == 3:
            bias_acc[1, hid:, :] += kept[hid:, :]
        elif r == deep - 5:
            bias_acc[1, :hid, :] += kept[:hid, :]
        else:
            bias_acc[1] += kept
    for r in range(halo, halo + rows, 2):
        kept = grad_one_ref[(r - 3) * hid : (r - 1) * hid, :]
        kept = jnp.where(own_cols, kept, jnp.zeros((), bf16))
        fed = jnp.concatenate(
            [state_in[0, b, (r - 1) * slot : (r + 3) * slot, :] for b in range(3)], axis=0
        )
        acc_small[1] += mm_nt(fed, kept)

    pay_ref[...] = jnp.zeros(pay_ref.shape, pay_ref.dtype)
    for b in range(3):
        total = acc_mid[b, :hid, : 3 * hid] + acc_mid[b, hid:, hid:]
        for a in range(3):
            t = 3 * a + b
            pay_ref[:hid, t * hid : (t + 1) * hid] = total[:, a * hid : (a + 1) * hid].astype(bf16)
    for a in range(3):
        for b in range(3):
            t = 3 * a + b
            at = (2 - b) * 4 * slot + (2 - a) * slot
            block = (
                acc_small[0, at : at + slot, :hid] + acc_small[0, at + slot : at + 2 * slot, hid:]
            )
            pay_ref[hid:, t * hid : (t + 1) * hid] = block.astype(bf16)
    pieces = []
    for a in range(3):
        for b in range(3):
            at = b * 4 * slot + a * slot
            pieces.append(acc_small[1, at : at + 2, :hid] + acc_small[1, at + slot : at + slot + 2, hid:])
    sums_in, sums_mid = lane_sums(bias_acc[1]), lane_sums(bias_acc[0])
    pieces.append(sums_in[:, :hid] + sums_in[:, hid:])
    pieces.append(sums_mid[:, :hid] + sums_mid[:, hid:])
    pieces.append(lane_sums(bias_out)[:, :hid])
    pieces.append(jnp.zeros((hid - 21, hid), f32))
    pay_ref[:hid, 9 * hid :] = jnp.concatenate(pieces, axis=0).astype(bf16)


def advance_kernel(
    rows,
    cols,
    ext_ref,
    forcing_ref,
    w_head_ref,
    b_head_ref,
    w_in_t_ref,
    act_two_ref,
    grad_one_ref,
    new_ref,
    grad_ref,
    stage,
    head,
    back,
):
    height, width = stage.shape[1], stage.shape[2]
    deep = rows + 2 * halo
    stage[...] = jnp.zeros(stage.shape, f32)
    stage[:, 0:deep, 0 : cols + 2 * halo] = ext_ref[...]
    w0, w1, c0, c1 = stage[0], stage[1], stage[2], stage[3]
    head[...] = jnp.zeros(head.shape, f32)
    back[...] = jnp.zeros(back.shape, f32)
    w_head = w_head_ref[...]
    b_head = b_head_ref[...]
    for r in range(3, deep - 3, 2):
        part = mm(w_head, act_two_ref[(r - 3) * hid : (r + 1) * hid, :])
        size = 2 * slot
        out = b_head
        for b in range(3):
            out = out + shift(part[b * size : (b + 1) * size], 0, b - 1)
        put_rows(head, r * slot, out)
    w_in_t = w_in_t_ref[...]
    for r in range(halo, halo + rows, 2):
        part = mm(w_in_t, grad_one_ref[(r - 4) * hid : r * hid, :])
        out = part[16:32]
        for b in (0, 2):
            out = out + shift(part[b * 16 : (b + 1) * 16], 0, b - 1)
        put_rows(back, r * 8, out)

    coefs = [take_plane(head, k, deep, slot) for k in range(coef)]
    mean_x = sum(coefs[1:6], coefs[0]) * (1.0 / 6.0)
    mean_y = sum(coefs[7:12], coefs[6]) * (1.0 / 6.0)
    sx = [coefs[k] - mean_x + face_base[0][k] for k in range(6)]
    sy = [coefs[6 + k] - mean_y + face_base[1][k] for k in range(6)]
    normal_x, normal_y = faces(w0, w1)
    grad_x = [-advection * (c - shift(c, 1, 0)) for c in (c0, c1)]
    grad_y = [-advection * (c - shift(c, 0, 1)) for c in (c0, c1)]
    normal_grad_x, normal_grad_y = 0.0, 0.0
    for c, (w, cot) in enumerate(((w0, c0), (w1, c1))):
        table = shifted_fields(w)
        face_x = sum(s * table[tap] for s, tap in zip(sx, taps_x))
        face_y = sum(s * table[tap] for s, tap in zip(sy, taps_y))
        flux_x = normal_x * face_x
        flux_y = normal_y * face_y
        normal_grad_x = normal_grad_x + grad_x[c] * face_x
        normal_grad_y = normal_grad_y + grad_y[c] * face_y
        around = table[1, 0] + table[-1, 0] + table[0, 1] + table[0, -1]
        new = (
            w
            - advection
            * (flux_x - shift(flux_x, -1, 0) + flux_y - shift(flux_y, 0, -1))
            + viscosity * (around - 4.0 * w)
        )
        if c == 0:
            new = new + forcing_ref[...]
        new_ref[c] = new[halo : halo + rows, halo : halo + cols]
    for c, cot in enumerate((c0, c1)):
        around = shift(cot, 1, 0) + shift(cot, -1, 0) + shift(cot, 0, 1) + shift(cot, 0, -1)
        total = cot + viscosity * (around - 4.0 * cot)
        flow_x = normal_x * grad_x[c]
        flow_y = normal_y * grad_y[c]
        by_col = {-1: {}, 0: {}, 1: {}}
        for s, (a, b) in zip(sx, taps_x):
            by_col[b][a] = by_col[b].get(a, 0.0) + flow_x * s
        for s, (a, b) in zip(sy, taps_y):
            by_col[b][a] = by_col[b].get(a, 0.0) + flow_y * s
        for b, column in by_col.items():
            part = sum(shift(value, -a, 0) for a, value in column.items())
            total = total + shift(part, 0, -b)
        if c == 0:
            total = total + 0.5 * (normal_grad_x + shift(normal_grad_x, -1, 0))
        else:
            total = total + 0.5 * (normal_grad_y + shift(normal_grad_y, 0, -1))
        total = total + take_plane(back, c, deep, 8)
        grad_ref[c] = total[halo : halo + rows, halo : halo + cols]


def finish_kernel(scale, one_ref, two_ref, in_ref, b_in_ref, mid_ref, b_mid_ref, out_ref, b_out_ref):
    total = (one_ref[...].astype(f32) + two_ref[...].astype(f32)) * scale
    for t in range(9):
        mid_ref[t] = total[:hid, t * hid : (t + 1) * hid]
        out_ref[:, t, :] = total[hid : hid + coef, t * hid : (t + 1) * hid]
    tail = total[:hid, 9 * hid :]
    for t in range(9):
        in_ref[t] = tail[2 * t : 2 * t + 2]
    b_in_ref[...] = tail[18:19]
    b_mid_ref[...] = tail[19:20]
    b_out_ref[...] = tail[20:21, :coef]


def banded(blocks):
    lower = jnp.pad(blocks, ((0, 0), (0, 1), (0, 0), (0, 0)))
    upper = jnp.pad(blocks, ((0, 0), (1, 0), (0, 0), (0, 0)))
    both = jnp.stack([lower, upper], axis=1)
    both = jnp.transpose(both, (0, 1, 3, 2, 4))
    return both.reshape(3, 2 * blocks.shape[2], 4 * blocks.shape[3])


def pad_dim(array, dim, size):
    pads = [(0, 0)] * array.ndim
    pads[dim] = (0, size - array.shape[dim])
    return jnp.pad(array, pads)


def across(stacked):
    return jnp.transpose(stacked, (1, 0, 2)).reshape(stacked.shape[1], -1)


def weights(kernel_in, kernel_mid, kernel_out):
    k_in = jnp.transpose(kernel_in, (3, 2, 0, 1))
    k_mid = jnp.transpose(kernel_mid, (3, 2, 0, 1))
    k_out = jnp.transpose(kernel_out, (3, 2, 0, 1))

    def turned(k):
        return jnp.transpose(k[::-1, ::-1], (0, 1, 3, 2))

    w_in = across(banded(pad_dim(k_in, 3, slot)))
    w_mid = banded(k_mid)
    w_mid_t = banded(turned(k_mid))
    w_out_t = across(banded(pad_dim(turned(k_out), 3, slot)))
    w_head = banded(pad_dim(k_out, 2, slot)).reshape(6 * slot, 4 * hid)
    w_in_t = banded(pad_dim(turned(k_in), 2, 8)).reshape(48, 4 * hid)
    return w_in, w_mid, w_mid_t, w_out_t, w_head, w_in_t


def ring(count, step):
    return [(i, (i + step) % count) for i in range(count)]


def extended(fields):
    short = fields.astype(bf16)
    for axis, dim in (("gy", 2), ("gx", 1)):
        count = lax.axis_size(axis)
        size = short.shape[dim]
        low = lax.ppermute(lax.slice_in_dim(short, size - halo, size, axis=dim), axis, ring(count, 1))
        high = lax.ppermute(lax.slice_in_dim(short, 0, halo, axis=dim), axis, ring(count, -1))
        short = jnp.concatenate([low, short, high], axis=dim)
        fields = jnp.concatenate([low.astype(f32), fields, high.astype(f32)], axis=dim)
    return fields


def per_device(velocity, kernel_in, bias_in, kernel_mid, bias_mid, kernel_out, bias_out, cotangent):
    rows, cols = velocity.shape[1], velocity.shape[2]
    ny_total = lax.axis_size("gy") * cols
    cell_count = lax.axis_size("gx") * rows * ny_total
    deep = rows + 2 * halo
    height = deep
    width = -(-(cols + 2 * halo) // 128) * 128
    vmem = pl.BlockSpec(memory_space=pltpu.VMEM)
    params = pltpu.CompilerParams(vmem_limit_bytes=48 << 20)

    w_in, w_mid, w_mid_t, w_out_t, w_head, w_in_t = weights(kernel_in, kernel_mid, kernel_out)
    b_in = jnp.tile(bias_in, 2)[:, None]
    b_mid = jnp.tile(bias_mid, 2)[:, None]
    b_head = jnp.tile(pad_dim(bias_out, 0, slot), 2)[:, None]
    columns = lax.iota(jnp.int32, width) - halo + lax.axis_index("gy") * cols
    forcing = forcing_amp * jnp.sin(2.0 * math.pi * forcing_wave * columns.astype(f32) / ny_total)
    ext = extended(jnp.concatenate([velocity, cotangent], axis=0))

    payload, act_two, grad_one = pl.pallas_call(
        lambda *refs: backward_kernel(rows, cols, *refs),
        out_shape=(
            jax.ShapeDtypeStruct((hid + slot, 10 * hid), bf16),
            jax.ShapeDtypeStruct(((deep - 4) * hid, width), bf16),
            jax.ShapeDtypeStruct(((deep - 6) * hid, width), bf16),
        ),
        in_specs=[vmem] * 7,
        out_specs=(vmem,) * 3,
        scratch_shapes=[
            pltpu.VMEM((4, height, width), f32),
            pltpu.VMEM((2, 3, deep * slot, width), bf16),
            pltpu.VMEM((width // 128, deep * slot, 128), f32),
            pltpu.VMEM((3, (deep - 2) * hid, width), bf16),
            pltpu.VMEM(((deep - 2) * hid, width), f32),
            pltpu.VMEM((3, (deep - 4) * hid, width), bf16),
            pltpu.VMEM((3, 2 * hid, 4 * hid), f32),
            pltpu.VMEM((2, 12 * slot, 2 * hid), f32),
            pltpu.VMEM((2, 2 * hid, width), f32),
        ],
        compiler_params=params,
        name="backward",
    )(ext, w_in, w_mid, w_mid_t, w_out_t, b_in, b_mid)

    new_velocity, grad_velocity = pl.pallas_call(
        lambda *refs: advance_kernel(rows, cols, *refs),
        out_shape=(jax.ShapeDtypeStruct(velocity.shape, f32),) * 2,
        in_specs=[vmem] * 7,
        out_specs=(vmem,) * 2,
        scratch_shapes=[
            pltpu.VMEM((4, height, width), f32),
            pltpu.VMEM((width // 128, deep * slot, 128), f32),
            pltpu.VMEM((width // 128, deep * 8, 128), f32),
        ],
        compiler_params=params,
        name="advance",
    )(ext, forcing[None, :], w_head, b_head, w_in_t, act_two, grad_one)

    steps = []
    for axis in ("gy", "gx"):
        count = lax.axis_size(axis)
        steps += [(axis, count, 1 << k) for k in range(count.bit_length() - 1)]
    for at, (axis, count, bit) in enumerate(steps):
        arrived = lax.ppermute(payload, axis, [(i, i ^ bit) for i in range(count)])
        if at < len(steps) - 1:
            payload = (payload.astype(f32) + arrived.astype(f32)).astype(bf16)

    g_in, gb_in, g_mid, gb_mid, g_out, gb_out = pl.pallas_call(
        lambda *refs: finish_kernel(1.0 / math.sqrt(cell_count), *refs),
        out_shape=(
            jax.ShapeDtypeStruct((9, 2, hid), f32),
            jax.ShapeDtypeStruct((1, hid), f32),
            jax.ShapeDtypeStruct((9, hid, hid), f32),
            jax.ShapeDtypeStruct((1, hid), f32),
            jax.ShapeDtypeStruct((coef, 9, hid), f32),
            jax.ShapeDtypeStruct((1, coef), f32),
        ),
        in_specs=[vmem] * 2,
        out_specs=(vmem,) * 6,
        compiler_params=params,
        name="finish",
    )(payload, arrived)

    return (
        new_velocity,
        grad_velocity,
        jnp.transpose(g_in.reshape(3, 3, 2, hid), (3, 2, 0, 1)),
        gb_in.reshape(hid),
        jnp.transpose(g_mid.reshape(3, 3, hid, hid), (2, 3, 0, 1)),
        gb_mid.reshape(hid),
        jnp.transpose(g_out.reshape(coef, 3, 3, hid), (0, 3, 1, 2)),
        gb_out.reshape(coef),
    )


def solution(mesh):
    in_specs = (P("groups", "gx", "gy"), P(), P(), P(), P(), P(), P(), P("groups", "gx", "gy"))
    out_specs = (
        P("groups", "gx", "gy"),
        P("groups", "gx", "gy"),
        P("groups", None, None, None),
        P("groups"),
        P("groups", None, None, None),
        P("groups"),
        P("groups", None, None, None),
        P("groups"),
    )
    return jax.shard_map(
        per_device, mesh=mesh, in_specs=in_specs, out_specs=out_specs, check_vma=False
    )
```

```python
import math

import jax
import jax.numpy as jnp
from jax import lax
from jax.experimental import pallas as pl
from jax.experimental.pallas import tpu as pltpu
from jax.sharding import PartitionSpec as P

advection = 0.2
viscosity = 0.05
forcing_amp = 0.05
forcing_wave = 4
face_base = ((0.0, 0.5, 0.0, 0.0, 0.5, 0.0), (0.0, 0.0, 0.5, 0.5, 0.0, 0.0))
halo = 4
hid = 64
coef = 12
slot = 16
taps_x = [(a, b) for a in (0, 1) for b in (-1, 0, 1)]
taps_y = [(a, b) for a in (-1, 0, 1) for b in (0, 1)]
f32 = jnp.float32
bf16 = jnp.bfloat16


def shift(value, rows, cols):
    if rows:
        value = pltpu.roll(value, (-rows) % value.shape[-2], value.ndim - 2)
    if cols:
        value = pltpu.roll(value, (-cols) % value.shape[-1], value.ndim - 1)
    return value


def mm(lhs, rhs):
    return lax.dot_general(lhs, rhs, (((1,), (0,)), ((), ())), preferred_element_type=f32)


def mm_nt(lhs, rhs):
    return lax.dot_general(lhs, rhs, (((1,), (1,)), ((), ())), preferred_element_type=f32)


def sigma_of(linear):
    return 0.5 * jnp.tanh(0.5 * linear) + 0.5


def store_shifted(refs, at, value):
    rows = value.shape[0]
    for b in range(3):
        refs[b, at : at + rows, :] = shift(value, 0, b - 1).astype(refs.dtype)


def put_plane(planes, k, stride, value):
    for j in range(planes.shape[0]):
        planes[j, pl.ds(k, value.shape[0], stride=stride), :] = value[:, 128 * j : 128 * j + 128]


def take_plane(planes, k, count, stride):
    tiles = [planes[j, pl.ds(k, count, stride=stride), :] for j in range(planes.shape[0])]
    return jnp.concatenate(tiles, axis=1)


def take_rows(planes, at, size):
    return jnp.concatenate([planes[j, at : at + size, :] for j in range(planes.shape[0])], axis=1)


def put_rows(planes, at, value):
    for j in range(planes.shape[0]):
        planes[j, at : at + value.shape[0], :] = value[:, 128 * j : 128 * j + 128]


def faces(w0, w1):
    normal_x = 0.5 * (w0 + shift(w0, 1, 0))
    normal_y = 0.5 * (w1 + shift(w1, 0, 1))
    return normal_x, normal_y


def shifted_fields(w):
    table = {}
    for b in (-1, 0, 1):
        col = shift(w, 0, b)
        for a in (-1, 0, 1):
            table[a, b] = shift(col, a, 0)
    return table


def lane_sums(total):
    lanes = total.shape[1]
    part = total[:, :128]
    for k in range(1, lanes // 128):
        part = part + total[:, 128 * k : 128 * k + 128]
    return jnp.sum(part.T, axis=0, keepdims=True)


def backward_kernel(
    rows,
    cols,
    ext_ref,
    w_in_ref,
    w_mid_ref,
    w_mid_t_ref,
    w_out_t_ref,
    b_in_ref,
    b_mid_ref,
    core_ref,
    keep_ref,
    send_ref,
    act_two_ref,
    grad_one_ref,
    pay,
    stage,
    state_in,
    head_in,
    act_one,
    slope_one,
    grad_two,
    acc_mid,
    acc_small,
    bias_acc,
):
    height, width = stage.shape[1], stage.shape[2]
    deep = rows + 2 * halo
    stage[...] = jnp.zeros(stage.shape, f32)
    stage[:, 0:deep, 0 : cols + 2 * halo] = ext_ref[...]
    w0, w1, c0, c1 = stage[0], stage[1], stage[2], stage[3]
    lane = lax.broadcasted_iota(jnp.int32, (1, width), 1)
    own_cols = (lane >= halo) & (lane < halo + cols)

    planes = head_in
    planes[...] = jnp.zeros(planes.shape, f32)
    put_plane(planes, 0, slot, w0)
    put_plane(planes, 1, slot, w1)
    for r in range(0, deep, 2):
        store_shifted(state_in.at[0], r * slot, take_rows(planes, r * slot, 2 * slot))

    normal_x, normal_y = faces(w0, w1)
    t0, t1 = shifted_fields(w0), shifted_fields(w1)
    fx0 = -advection * (c0 - shift(c0, 1, 0)) * normal_x
    fx1 = -advection * (c1 - shift(c1, 1, 0)) * normal_x
    fy0 = -advection * (c0 - shift(c0, 0, 1)) * normal_y
    fy1 = -advection * (c1 - shift(c1, 0, 1)) * normal_y
    row_id = lax.broadcasted_iota(jnp.int32, (height, width), 0)
    own = own_cols & (row_id >= halo) & (row_id < halo + rows)
    sums = []
    for at, taps, g0, g1 in ((0, taps_x, fx0, fx1), (6, taps_y, fy0, fy1)):
        raw = [g0 * t0[tap] + g1 * t1[tap] for tap in taps]
        mean = sum(raw[1:], raw[0]) * (1.0 / 6.0)
        for k in range(6):
            value = raw[k] - mean
            put_plane(planes, at + k, slot, value)
            sums.append(jnp.sum(jnp.where(own, value, 0.0), axis=0, keepdims=True))
    for r in range(0, deep, 2):
        store_shifted(state_in.at[1], r * slot, take_rows(planes, r * slot, 2 * slot))
    bias_out = jnp.concatenate(sums + [jnp.zeros((128 - coef, width), f32)], axis=0)

    w_in = w_in_ref[...]
    b_in = b_in_ref[:, 0:1]
    for r in range(1, deep - 1, 2):
        fed = jnp.concatenate(
            [state_in[0, b, (r - 1) * slot : (r + 3) * slot, :] for b in range(3)], axis=0
        )
        linear = mm(w_in, fed) + b_in
        sigma = sigma_of(linear)
        act = linear * sigma
        store_shifted(act_one, (r - 1) * hid, act)
        slope_one[(r - 1) * hid : (r + 1) * hid, :] = sigma + act * (1.0 - sigma)

    b_mid = b_mid_ref[:, 0:1]
    w_out_t = w_out_t_ref[...]
    bias_acc[...] = jnp.zeros(bias_acc.shape, f32)
    acc_mid[...] = jnp.zeros(acc_mid.shape, f32)
    acc_small[...] = jnp.zeros(acc_small.shape, f32)
    for r in range(2, deep - 2, 2):
        mine = halo <= r < halo + rows
        linear = b_mid
        window = [act_one[b, (r - 2) * hid : (r + 2) * hid, :] for b in range(3)]
        for b in range(3):
            linear = linear + mm(w_mid_ref[b], window[b])
        sigma = sigma_of(linear)
        act = linear * sigma
        act_short = act.astype(bf16)
        act_two_ref[(r - 2) * hid : r * hid, :] = act_short
        fed = jnp.concatenate(
            [state_in[1, b, (r - 1) * slot : (r + 3) * slot, :] for b in range(3)], axis=0
        )
        grad = mm(w_out_t, fed) * (sigma + act * (1.0 - sigma))
        store_shifted(grad_two, (r - 2) * hid, grad)
        if mine:
            kept = jnp.where(own_cols, grad, 0.0)
            bias_acc[0] += kept
            kept = kept.astype(bf16)
            for b in range(3):
                acc_mid[b] += mm_nt(kept, window[b])
            acc_small[0] += mm_nt(fed, jnp.where(own_cols, act, 0.0).astype(bf16))

    for r in range(3, deep - 3, 2):
        grad = mm(w_mid_t_ref[0], grad_two[0, (r - 3) * hid : (r + 1) * hid, :])
        for b in (1, 2):
            grad = grad + mm(w_mid_t_ref[b], grad_two[b, (r - 3) * hid : (r + 1) * hid, :])
        grad = grad * slope_one[(r - 1) * hid : (r + 1) * hid, :]
        grad_one_ref[(r - 3) * hid : (r - 1) * hid, :] = grad.astype(bf16)
        kept = jnp.where(own_cols, grad, 0.0)
        if r == 3:
            bias_acc[1, hid:, :] += kept[hid:, :]
        elif r == deep - 5:
            bias_acc[1, :hid, :] += kept[:hid, :]
        else:
            bias_acc[1] += kept
    for r in range(halo, halo + rows, 2):
        kept = grad_one_ref[(r - 3) * hid : (r - 1) * hid, :]
        kept = jnp.where(own_cols, kept, jnp.zeros((), bf16))
        fed = jnp.concatenate(
            [state_in[0, b, (r - 1) * slot : (r + 3) * slot, :] for b in range(3)], axis=0
        )
        acc_small[1] += mm_nt(fed, kept)

    for b in range(3):
        total = acc_mid[b, :hid, : 3 * hid] + acc_mid[b, hid:, hid:]
        for a in range(3):
            t = 3 * a + b
            block = total[:, a * hid : (a + 1) * hid].astype(bf16)
            for h in range(2):
                pay[h, :, t * hid : (t + 1) * hid] = block[32 * h : 32 * h + 32]
    slots = []
    pieces = []
    for a in range(3):
        for b in range(3):
            at = (2 - b) * 4 * slot + (2 - a) * slot
            slots.append(
                acc_small[0, at : at + slot, :hid] + acc_small[0, at + slot : at + 2 * slot, hid:]
            )
            at = b * 4 * slot + a * slot
            pieces.append(
                acc_small[1, at : at + 2, :hid] + acc_small[1, at + slot : at + slot + 2, hid:]
            )
    sums_in, sums_mid = lane_sums(bias_acc[1]), lane_sums(bias_acc[0])
    pieces.append(sums_in[:, :hid] + sums_in[:, hid:])
    pieces.append(sums_mid[:, :hid] + sums_mid[:, hid:])
    pieces.append(lane_sums(bias_out)[:, :hid])
    pieces.append(jnp.zeros((11, hid), f32))
    rest = jnp.concatenate(pieces, axis=0)
    slots += [rest[:slot], rest[slot:], jnp.zeros((slot, hid), f32)]
    for h in range(2):
        for q in range(3):
            at = 6 * h + 2 * q
            block = jnp.concatenate(slots[at : at + 2], axis=0).astype(bf16)
            pay[h, :, (9 + q) * hid : (10 + q) * hid] = block
    core = core_ref[0]
    keep_ref[...] = pay[core]
    send_ref[...] = pay[1 - core]


def advance_kernel(
    rows,
    cols,
    ext_ref,
    forcing_ref,
    w_head_ref,
    b_head_ref,
    w_in_t_ref,
    act_two_ref,
    grad_one_ref,
    new_ref,
    grad_ref,
    stage,
    head,
    back,
):
    height, width = stage.shape[1], stage.shape[2]
    deep = rows + 2 * halo
    stage[...] = jnp.zeros(stage.shape, f32)
    stage[:, 0:deep, 0 : cols + 2 * halo] = ext_ref[...]
    w0, w1, c0, c1 = stage[0], stage[1], stage[2], stage[3]
    head[...] = jnp.zeros(head.shape, f32)
    back[...] = jnp.zeros(back.shape, f32)
    w_head = w_head_ref[...]
    b_head = b_head_ref[:, 0:1]
    for r in range(3, deep - 3, 2):
        part = mm(w_head, act_two_ref[(r - 3) * hid : (r + 1) * hid, :])
        size = 2 * slot
        out = b_head
        for b in range(3):
            out = out + shift(part[b * size : (b + 1) * size], 0, b - 1)
        put_rows(head, r * slot, out)
    w_in_t = w_in_t_ref[...]
    for r in range(halo, halo + rows, 2):
        part = mm(w_in_t, grad_one_ref[(r - 4) * hid : r * hid, :])
        out = part[16:32]
        for b in (0, 2):
            out = out + shift(part[b * 16 : (b + 1) * 16], 0, b - 1)
        put_rows(back, r * 8, out)

    coefs = [take_plane(head, k, deep, slot) for k in range(coef)]
    mean_x = sum(coefs[1:6], coefs[0]) * (1.0 / 6.0)
    mean_y = sum(coefs[7:12], coefs[6]) * (1.0 / 6.0)
    sx = [coefs[k] - mean_x + face_base[0][k] for k in range(6)]
    sy = [coefs[6 + k] - mean_y + face_base[1][k] for k in range(6)]
    normal_x, normal_y = faces(w0, w1)
    grad_x = [-advection * (c - shift(c, 1, 0)) for c in (c0, c1)]
    grad_y = [-advection * (c - shift(c, 0, 1)) for c in (c0, c1)]
    normal_grad_x, normal_grad_y = 0.0, 0.0
    for c, (w, cot) in enumerate(((w0, c0), (w1, c1))):
        table = shifted_fields(w)
        face_x = sum(s * table[tap] for s, tap in zip(sx, taps_x))
        face_y = sum(s * table[tap] for s, tap in zip(sy, taps_y))
        flux_x = normal_x * face_x
        flux_y = normal_y * face_y
        normal_grad_x = normal_grad_x + grad_x[c] * face_x
        normal_grad_y = normal_grad_y + grad_y[c] * face_y
        around = table[1, 0] + table[-1, 0] + table[0, 1] + table[0, -1]
        new = (
            w
            - advection
            * (flux_x - shift(flux_x, -1, 0) + flux_y - shift(flux_y, 0, -1))
            + viscosity * (around - 4.0 * w)
        )
        if c == 0:
            new = new + forcing_ref[...]
        new_ref[c] = new[halo : halo + rows, halo : halo + cols]
    for c, cot in enumerate((c0, c1)):
        around = shift(cot, 1, 0) + shift(cot, -1, 0) + shift(cot, 0, 1) + shift(cot, 0, -1)
        total = cot + viscosity * (around - 4.0 * cot)
        flow_x = normal_x * grad_x[c]
        flow_y = normal_y * grad_y[c]
        by_col = {-1: {}, 0: {}, 1: {}}
        for s, (a, b) in zip(sx, taps_x):
            by_col[b][a] = by_col[b].get(a, 0.0) + flow_x * s
        for s, (a, b) in zip(sy, taps_y):
            by_col[b][a] = by_col[b].get(a, 0.0) + flow_y * s
        for b, column in by_col.items():
            part = sum(shift(value, -a, 0) for a, value in column.items())
            total = total + shift(part, 0, -b)
        if c == 0:
            total = total + 0.5 * (normal_grad_x + shift(normal_grad_x, -1, 0))
        else:
            total = total + 0.5 * (normal_grad_y + shift(normal_grad_y, 0, -1))
        total = total + take_plane(back, c, deep, 8)
        grad_ref[c] = total[halo : halo + rows, halo : halo + cols]


def finish_kernel(
    scale, mine_ref, other_ref, core_ref, in_ref, b_in_ref, mid_ref, b_mid_ref, out_ref, b_out_ref
):
    mine = mine_ref[...].astype(f32) * scale
    other = other_ref[...].astype(f32) * scale
    first = core_ref[0] == 0
    halves = (jnp.where(first, mine, other), jnp.where(first, other, mine))
    slots = []
    for h, half in enumerate(halves):
        for t in range(9):
            mid_ref[t, 32 * h : 32 * h + 32, :] = half[:, t * hid : (t + 1) * hid]
        for q in range(3):
            block = half[:, (9 + q) * hid : (10 + q) * hid]
            slots += [block[:slot], block[slot:]]
    for a in range(3):
        for b in range(3):
            out_ref[:, a, b, :] = slots[3 * a + b][:coef]
    for t in range(9):
        in_ref[t] = slots[9 + t // 8][2 * t % 16 : 2 * t % 16 + 2]
    b_in_ref[...] = slots[10][2:3]
    b_mid_ref[...] = slots[10][3:4]
    b_out_ref[...] = slots[10][4:5, :coef]


def weights_kernel(
    k_in_ref,
    k_mid_ref,
    k_out_ref,
    b_in_ref,
    b_mid_ref,
    b_out_ref,
    w_in_ref,
    w_mid_ref,
    w_mid_t_ref,
    w_out_t_ref,
    w_head_ref,
    w_in_t_ref,
    c_in_ref,
    c_mid_ref,
    c_head_ref,
):
    def band(block, upper):
        none = jnp.zeros(block[0].shape, f32)
        return jnp.concatenate([none, *block] if upper else [*block, none], axis=1)

    def tall(block, rows):
        return jnp.concatenate(
            [block, jnp.zeros((rows - block.shape[0], block.shape[1]), f32)], axis=0
        )

    k_mid = [k_mid_ref[t].astype(f32) for t in range(9)]
    k_mid_t = [k.T for k in k_mid]
    k_out = [k_out_ref[:, t // 3, t % 3, :].astype(f32) for t in range(9)]
    k_in = [k_in_ref[t].astype(f32) for t in range(9)]
    in_rows = []
    out_rows = []
    zero = jnp.zeros((slot, hid), f32)
    for b in range(3):
        forward = [3 * a + b for a in range(3)]
        backward = [8 - t for t in forward]
        for u in range(2):
            at = slice(u * hid, (u + 1) * hid)
            w_mid_ref[b, at, :] = band([k_mid[t] for t in forward], u).astype(bf16)
            w_mid_t_ref[b, at, :] = band([k_mid_t[t] for t in backward], u).astype(bf16)
        head = [band([tall(k_out[t], slot) for t in forward], u) for u in range(2)]
        w_head_ref[2 * slot * b : 2 * slot * (b + 1), :] = jnp.concatenate(head, 0).astype(bf16)
        back = [band([tall(k_in[t], 8) for t in backward], u) for u in range(2)]
        w_in_t_ref[16 * b : 16 * (b + 1), :] = jnp.concatenate(back, 0).astype(bf16)
        for rows, blocks in (
            (in_rows, [tall(k_in[t], slot) for t in forward]),
            (out_rows, [tall(k_out[t], slot) for t in backward]),
        ):
            lower = jnp.concatenate(blocks + [zero], axis=0)
            upper = jnp.concatenate([zero] + blocks, axis=0)
            rows.append(jnp.concatenate([lower, upper], axis=1))
    w_in_ref[...] = jnp.concatenate(in_rows, axis=0).T.astype(bf16)
    w_out_t_ref[...] = jnp.concatenate(out_rows, axis=0).T.astype(bf16)
    for ref, bias in ((c_in_ref, b_in_ref[...]), (c_mid_ref, b_mid_ref[...])):
        ref[...] = jnp.broadcast_to(jnp.concatenate([bias, bias], axis=1), (128, 128)).T
    bias = jnp.concatenate([b_out_ref[...], jnp.zeros((1, slot - coef), f32)], axis=1)
    bias = jnp.concatenate([bias, bias, jnp.zeros((1, 128 - 2 * slot), f32)], axis=1)
    c_head_ref[...] = jnp.broadcast_to(bias, (128, 128)).T[: 2 * slot]


def extended(fields):
    short = fields.astype(bf16)
    for axis, dim in (("gy", 2), ("gx", 1)):
        count = lax.axis_size(axis)
        size = short.shape[dim]
        even = lax.axis_index(axis) % 2 == 0
        first = lax.slice_in_dim(short, 0, halo, axis=dim)
        last = lax.slice_in_dim(short, size - halo, size, axis=dim)
        far_pairs = [(i, (i + 1 if i % 2 else i - 1) % count) for i in range(count)]
        far = lax.ppermute(jnp.where(even, first, last), axis, far_pairs)
        near = lax.ppermute(jnp.where(even, last, first), axis, [(i, i ^ 1) for i in range(count)])
        low = jnp.where(even, far, near)
        high = jnp.where(even, near, far)
        short = jnp.concatenate([low, short, high], axis=dim)
        fields = jnp.concatenate([low.astype(f32), fields, high.astype(f32)], axis=dim)
    return fields


def swap(value, rows, cols):
    height, width = lax.axis_size("gx"), lax.axis_size("gy")
    pairs = [
        (i * width + j, (i ^ rows) * width + (j ^ cols)) for i in range(height) for j in range(width)
    ]
    return lax.ppermute(value, ("gx", "gy"), pairs)


def added(*values):
    sums = [v.astype(f32) for v in values]
    while len(sums) > 1:
        sums = [sums[k] + sums[k + 1] for k in range(0, len(sums), 2)]
    return sums[0].astype(bf16)


def summed(keep, send):
    half = added(keep, swap(send, 0, 1))
    steps = [(0, 1 << k) for k in range(1, lax.axis_size("gy").bit_length() - 1)]
    steps += [(1 << k, 0) for k in range(lax.axis_size("gx").bit_length() - 1)]
    while steps:
        if len(steps) >= 2 and steps[0][0] == 0 and steps[1][1] == 0:
            (_, cols), (rows, _) = steps[:2]
            half = added(
                half,
                swap(half, 0, cols),
                swap(half, rows, 0),
                swap(half, rows, cols),
            )
            steps = steps[2:]
        else:
            half = added(half, swap(half, *steps[0]))
            steps = steps[1:]
    return half, swap(half, 0, 1)


def per_device(velocity, kernel_in, bias_in, kernel_mid, bias_mid, kernel_out, bias_out, cotangent):
    rows, cols = velocity.shape[1], velocity.shape[2]
    ny_total = lax.axis_size("gy") * cols
    cell_count = lax.axis_size("gx") * rows * ny_total
    deep = rows + 2 * halo
    height = deep
    width = -(-(cols + 2 * halo) // 128) * 128
    vmem = pl.BlockSpec(memory_space=pltpu.VMEM)
    params = pltpu.CompilerParams(vmem_limit_bytes=48 << 20)

    core = (lax.axis_index("gy") % 2).astype(jnp.int32).reshape(1)
    smem = pl.BlockSpec(memory_space=pltpu.SMEM)
    w_in, w_mid, w_mid_t, w_out_t, w_head, w_in_t, b_in, b_mid, b_head = pl.pallas_call(
        weights_kernel,
        out_shape=(
            jax.ShapeDtypeStruct((2 * hid, 12 * slot), bf16),
            jax.ShapeDtypeStruct((3, 2 * hid, 4 * hid), bf16),
            jax.ShapeDtypeStruct((3, 2 * hid, 4 * hid), bf16),
            jax.ShapeDtypeStruct((2 * hid, 12 * slot), bf16),
            jax.ShapeDtypeStruct((6 * slot, 4 * hid), bf16),
            jax.ShapeDtypeStruct((48, 4 * hid), bf16),
            jax.ShapeDtypeStruct((128, 128), f32),
            jax.ShapeDtypeStruct((128, 128), f32),
            jax.ShapeDtypeStruct((2 * slot, 128), f32),
        ),
        in_specs=[vmem] * 6,
        out_specs=(vmem,) * 9,
        compiler_params=params,
        name="weights",
    )(
        jnp.transpose(kernel_in, (2, 3, 1, 0)).reshape(9, 2, hid),
        jnp.transpose(kernel_mid, (2, 3, 0, 1)).reshape(9, hid, hid),
        jnp.transpose(kernel_out, (0, 2, 3, 1)),
        bias_in[None, :],
        bias_mid[None, :],
        bias_out[None, :],
    )
    columns = lax.iota(jnp.int32, width) - halo + lax.axis_index("gy") * cols
    forcing = forcing_amp * jnp.sin(2.0 * math.pi * forcing_wave * columns.astype(f32) / ny_total)
    ext = extended(jnp.concatenate([velocity, cotangent], axis=0))

    keep, send, act_two, grad_one = pl.pallas_call(
        lambda *refs: backward_kernel(rows, cols, *refs),
        out_shape=(
            jax.ShapeDtypeStruct((hid // 2, 12 * hid), bf16),
            jax.ShapeDtypeStruct((hid // 2, 12 * hid), bf16),
            jax.ShapeDtypeStruct(((deep - 4) * hid, width), bf16),
            jax.ShapeDtypeStruct(((deep - 6) * hid, width), bf16),
        ),
        in_specs=[vmem] * 7 + [smem],
        out_specs=(vmem,) * 4,
        scratch_shapes=[
            pltpu.VMEM((2, hid // 2, 12 * hid), bf16),
            pltpu.VMEM((4, height, width), f32),
            pltpu.VMEM((2, 3, deep * slot, width), bf16),
            pltpu.VMEM((width // 128, deep * slot, 128), f32),
            pltpu.VMEM((3, (deep - 2) * hid, width), bf16),
            pltpu.VMEM(((deep - 2) * hid, width), f32),
            pltpu.VMEM((3, (deep - 4) * hid, width), bf16),
            pltpu.VMEM((3, 2 * hid, 4 * hid), f32),
            pltpu.VMEM((2, 12 * slot, 2 * hid), f32),
            pltpu.VMEM((2, 2 * hid, width), f32),
        ],
        compiler_params=params,
        name="backward",
    )(ext, w_in, w_mid, w_mid_t, w_out_t, b_in, b_mid, core)

    new_velocity, grad_velocity = pl.pallas_call(
        lambda *refs: advance_kernel(rows, cols, *refs),
        out_shape=(jax.ShapeDtypeStruct(velocity.shape, f32),) * 2,
        in_specs=[vmem] * 7,
        out_specs=(vmem,) * 2,
        scratch_shapes=[
            pltpu.VMEM((4, height, width), f32),
            pltpu.VMEM((width // 128, deep * slot, 128), f32),
            pltpu.VMEM((width // 128, deep * 8, 128), f32),
        ],
        compiler_params=params,
        name="advance",
    )(ext, forcing[None, :], w_head, b_head, w_in_t, act_two, grad_one)

    mine, other = summed(keep, send)
    g_in, gb_in, g_mid, gb_mid, g_out, gb_out = pl.pallas_call(
        lambda *refs: finish_kernel(1.0 / math.sqrt(cell_count), *refs),
        out_shape=(
            jax.ShapeDtypeStruct((9, 2, hid), f32),
            jax.ShapeDtypeStruct((1, hid), f32),
            jax.ShapeDtypeStruct((9, hid, hid), f32),
            jax.ShapeDtypeStruct((1, hid), f32),
            jax.ShapeDtypeStruct((coef, 3, 3, hid), f32),
            jax.ShapeDtypeStruct((1, coef), f32),
        ),
        in_specs=[vmem] * 2 + [smem],
        out_specs=(vmem,) * 6,
        compiler_params=params,
        name="finish",
    )(mine, other, core)

    return (
        new_velocity,
        grad_velocity,
        jnp.transpose(g_in.reshape(3, 3, 2, hid), (3, 2, 0, 1)),
        gb_in.reshape(hid),
        jnp.transpose(g_mid.reshape(3, 3, hid, hid), (2, 3, 0, 1)),
        gb_mid.reshape(hid),
        jnp.transpose(g_out, (0, 3, 1, 2)),
        gb_out.reshape(coef),
    )


def solution(mesh):
    in_specs = (P("groups", "gx", "gy"), P(), P(), P(), P(), P(), P(), P("groups", "gx", "gy"))
    out_specs = (
        P("groups", "gx", "gy"),
        P("groups", "gx", "gy"),
        P("groups", None, None, None),
        P("groups"),
        P("groups", None, None, None),
        P("groups"),
        P("groups", None, None, None),
        P("groups"),
    )
    return jax.shard_map(
        per_device, mesh=mesh, in_specs=in_specs, out_specs=out_specs, check_vma=False
    )
```

```python
import math

import jax
import jax.numpy as jnp
from jax import lax
from jax.experimental import pallas as pl
from jax.experimental.pallas import tpu as pltpu
from jax.sharding import PartitionSpec as P

advection = 0.2
viscosity = 0.05
forcing_amp = 0.05
forcing_wave = 4
face_base = ((0.0, 0.5, 0.0, 0.0, 0.5, 0.0), (0.0, 0.0, 0.5, 0.5, 0.0, 0.0))
halo = 4
hid = 64
coef = 12
slot = 16
taps_x = [(a, b) for a in (0, 1) for b in (-1, 0, 1)]
taps_y = [(a, b) for a in (-1, 0, 1) for b in (0, 1)]
f32 = jnp.float32
bf16 = jnp.bfloat16


def shift(value, rows, cols):
    if rows:
        value = pltpu.roll(value, (-rows) % value.shape[-2], value.ndim - 2)
    if cols:
        value = pltpu.roll(value, (-cols) % value.shape[-1], value.ndim - 1)
    return value


def mm(lhs, rhs):
    return lax.dot_general(lhs, rhs, (((1,), (0,)), ((), ())), preferred_element_type=f32)


def mm_nt(lhs, rhs):
    return lax.dot_general(lhs, rhs, (((1,), (1,)), ((), ())), preferred_element_type=f32)


def sigma_of(linear):
    return 0.5 * jnp.tanh(0.5 * linear) + 0.5


class Rows:
    def __init__(self, size, *pieces):
        self.size = size
        self.pieces = pieces

    def get(self, lo, hi, lead=()):
        parts = []
        for start, stop, ref in self.pieces:
            first, last = max(lo, start), min(hi, stop)
            if first < last:
                rows = slice((first - start) * self.size, (last - start) * self.size)
                parts.append((first, ref[(*lead, rows, slice(None))]))
        parts = [part for _, part in sorted(parts, key=lambda item: item[0])]
        return parts[0] if len(parts) == 1 else jnp.concatenate(parts, axis=0)

    def put(self, lo, value, lead=()):
        for start, stop, ref in self.pieces:
            if start <= lo < stop:
                rows = slice((lo - start) * self.size, (lo - start) * self.size + value.shape[0])
                ref[(*lead, rows, slice(None))] = value

    def put_shifted(self, lo, value, lead=()):
        value = value.astype(bf16)
        for b in range(3):
            self.put(lo, shift(value, 0, b - 1), (*lead, b))

    def window(self, lo, hi, lead=()):
        return jnp.concatenate([self.get(lo, hi, (*lead, b)) for b in range(3)], axis=0)


def put_plane(planes, k, stride, value):
    for j in range(planes.shape[0]):
        planes[j, pl.ds(k, value.shape[0], stride=stride), :] = value[:, 128 * j : 128 * j + 128]


def take_plane(planes, k, count, stride):
    tiles = [planes[j, pl.ds(k, count, stride=stride), :] for j in range(planes.shape[0])]
    return jnp.concatenate(tiles, axis=1)


def take_rows(planes, at, size):
    return jnp.concatenate([planes[j, at : at + size, :] for j in range(planes.shape[0])], axis=1)


def put_rows(planes, at, value):
    for j in range(planes.shape[0]):
        planes[j, at : at + value.shape[0], :] = value[:, 128 * j : 128 * j + 128]


def faces(w0, w1):
    normal_x = 0.5 * (w0 + shift(w0, 1, 0))
    normal_y = 0.5 * (w1 + shift(w1, 0, 1))
    return normal_x, normal_y


def shifted_fields(w):
    table = {}
    for b in (-1, 0, 1):
        col = shift(w, 0, b)
        for a in (-1, 0, 1):
            table[a, b] = shift(col, a, 0)
    return table


def lane_sums(total):
    lanes = total.shape[1]
    part = total[:, :128]
    for k in range(1, lanes // 128):
        part = part + total[:, 128 * k : 128 * k + 128]
    return jnp.sum(part.T, axis=0, keepdims=True)


def prepare(first, rows, cols, ext_ref, stage, planes, state_in, state_rows, head_rows):
    count = ext_ref.shape[1]
    height, width = stage.shape[1], stage.shape[2]
    stage[...] = jnp.zeros(stage.shape, f32)
    stage[:, 0:count, 0 : cols + 2 * halo] = ext_ref[...]
    w0, w1, c0, c1 = stage[0], stage[1], stage[2], stage[3]

    planes[...] = jnp.zeros(planes.shape, f32)
    put_plane(planes, 0, slot, w0)
    put_plane(planes, 1, slot, w1)
    for r in state_rows:
        state_in.put_shifted(r, take_rows(planes, (r - first) * slot, 2 * slot), (0,))

    normal_x, normal_y = faces(w0, w1)
    t0, t1 = shifted_fields(w0), shifted_fields(w1)
    fx0 = -advection * (c0 - shift(c0, 1, 0)) * normal_x
    fx1 = -advection * (c1 - shift(c1, 1, 0)) * normal_x
    fy0 = -advection * (c0 - shift(c0, 0, 1)) * normal_y
    fy1 = -advection * (c1 - shift(c1, 0, 1)) * normal_y
    lane = lax.broadcasted_iota(jnp.int32, (height, width), 1)
    row_id = lax.broadcasted_iota(jnp.int32, (height, width), 0) + first
    own = (lane >= halo) & (lane < halo + cols) & (row_id >= halo) & (row_id < halo + rows)
    sums = []
    for at, taps, g0, g1 in ((0, taps_x, fx0, fx1), (6, taps_y, fy0, fy1)):
        raw = [g0 * t0[tap] + g1 * t1[tap] for tap in taps]
        mean = sum(raw[1:], raw[0]) * (1.0 / 6.0)
        for k in range(6):
            value = raw[k] - mean
            put_plane(planes, at + k, slot, value)
            sums.append(jnp.sum(jnp.where(own, value, 0.0), axis=0, keepdims=True))
    for r in head_rows:
        state_in.put_shifted(r, take_rows(planes, (r - first) * slot, 2 * slot), (1,))
    return sums


def layers(
    rows,
    cols,
    groups,
    refs,
    state_in,
    act_one,
    slope_one,
    grad_two,
    act_two,
    grad_one,
    acc_mid,
    acc_small,
    bias_acc,
):
    w_in_ref, w_mid_ref, w_mid_t_ref, w_out_t_ref, b_in_ref, b_mid_ref = refs
    width = bias_acc.shape[2]
    lane = lax.broadcasted_iota(jnp.int32, (1, width), 1)
    own_cols = (lane >= halo) & (lane < halo + cols)
    groups_one, groups_two, groups_back, groups_in = groups

    w_in = w_in_ref[...]
    b_in = b_in_ref[:, 0:1]
    for r in groups_one:
        linear = mm(w_in, state_in.window(r - 1, r + 3, (0,))) + b_in
        sigma = sigma_of(linear)
        act = linear * sigma
        act_one.put_shifted(r, act)
        slope_one.put(r, sigma + act * (1.0 - sigma))

    b_mid = b_mid_ref[:, 0:1]
    w_out_t = w_out_t_ref[...]
    w_mid = jnp.concatenate([w_mid_ref[b] for b in range(3)], axis=1)
    w_mid_t = jnp.concatenate([w_mid_t_ref[b] for b in range(3)], axis=1)
    for r in groups_two:
        window = [act_one.get(r - 1, r + 3, (b,)) for b in range(3)]
        linear = mm(w_mid, jnp.concatenate(window, axis=0)) + b_mid
        sigma = sigma_of(linear)
        act = linear * sigma
        act_two.put(r, act.astype(bf16))
        fed = state_in.window(r - 1, r + 3, (1,))
        grad = mm(w_out_t, fed) * (sigma + act * (1.0 - sigma))
        grad_two.put_shifted(r, grad)
        if halo <= r < halo + rows:
            kept = jnp.where(own_cols, grad, 0.0)
            bias_acc[0] += kept
            kept = kept.astype(bf16)
            for b in range(3):
                acc_mid[b] += mm_nt(kept, window[b])
            acc_small[0] += mm_nt(fed, jnp.where(own_cols, act, 0.0).astype(bf16))

    for r in groups_back:
        grad = mm(w_mid_t, grad_two.window(r - 1, r + 3)) * slope_one.get(r, r + 2)
        grad_one.put(r, grad.astype(bf16))
        kept = jnp.where(own_cols, grad, 0.0)
        if r < halo:
            bias_acc[1, hid:, :] += kept[hid:, :]
        elif r + 2 > halo + rows:
            bias_acc[1, :hid, :] += kept[:hid, :]
        else:
            bias_acc[1] += kept
    for r in groups_in:
        kept = jnp.where(own_cols, grad_one.get(r, r + 2), jnp.zeros((), bf16))
        acc_small[1] += mm_nt(state_in.window(r - 1, r + 3, (0,)), kept)


def inner_kernel(rows, cols, ext_ref, *refs):
    weight_refs, refs = refs[:6], refs[6:]
    act_one, slope_one, grad_two, act_two, grad_one, acc_mid, acc_small, bias_acc, *refs = refs
    stage, planes, state_in = refs
    low, high = halo, halo + rows
    state_in = Rows(slot, (low, high, state_in))
    acc_mid[...] = jnp.zeros(acc_mid.shape, f32)
    acc_small[...] = jnp.zeros(acc_small.shape, f32)
    bias_acc[...] = jnp.zeros(bias_acc.shape, f32)
    pairs = range(low, high, 2)
    prepare(low, rows, cols, ext_ref, stage, planes, state_in, pairs, pairs)
    groups = [range(low + k, high - k, 2) for k in (1, 2, 3, 4)]
    layers(
        rows,
        cols,
        groups,
        weight_refs,
        state_in,
        Rows(hid, (low + 1, high - 1, act_one)),
        Rows(hid, (low + 1, high - 1, slope_one)),
        Rows(hid, (low + 2, high - 2, grad_two)),
        Rows(hid, (low + 2, high - 2, act_two)),
        Rows(hid, (low + 3, high - 3, grad_one)),
        acc_mid,
        acc_small,
        bias_acc,
    )


def split_rows(size, first, low, high, last, lower_ref, inner_ref, upper_ref):
    return Rows(size, (first, low, lower_ref), (low, high, inner_ref), (high, last, upper_ref))


def outer_kernel(rows, cols, ext_ref, *refs):
    weight_refs, core_ref, refs = refs[:6], refs[6], refs[7:]
    act_one_in, slope_one_in, grad_two_in, grad_one_in, acc_mid_in, acc_small_in, bias_in, *refs = refs
    keep_ref, send_ref, act_two, grad_one, *refs = refs
    pay, stage, planes, state_in, act_one, slope_one, grad_two, acc_mid, acc_small, bias_acc = refs
    low, high, deep = halo, halo + rows, rows + 2 * halo
    acc_mid[...] = acc_mid_in[...]
    acc_small[...] = acc_small_in[...]
    bias_acc[...] = bias_in[...]
    state_in = Rows(slot, (0, deep, state_in))
    state_rows = [r for r in range(0, deep, 2) if r < low + 6 or r + 2 > high - 6]
    head_rows = [r for r in range(0, deep, 2) if r < low + 4 or r + 2 > high - 4]
    sums = prepare(0, rows, cols, ext_ref, stage, planes, state_in, state_rows, head_rows)
    bias_out = jnp.concatenate(sums + [jnp.zeros((128 - coef, stage.shape[2]), f32)], axis=0)
    groups = [
        [*range(k, low + k, 2), *range(high - k, deep - k, 2)] for k in (1, 2, 3)
    ]
    groups.append([low, low + 2, high - 4, high - 2])

    def both(k, edge, inner):
        edges = [edge.at[i] for i in range(2)]
        return split_rows(hid, k, low + k, high - k, deep - k, edges[0], inner, edges[1])

    layers(
        rows,
        cols,
        groups,
        weight_refs,
        state_in,
        both(1, act_one, act_one_in),
        both(1, slope_one, slope_one_in),
        both(2, grad_two, grad_two_in),
        Rows(hid, (2, low + 2, act_two.at[0]), (high - 2, deep - 2, act_two.at[1])),
        both(3, grad_one, grad_one_in),
        acc_mid,
        acc_small,
        bias_acc,
    )

    for b in range(3):
        total = acc_mid[b, :hid, : 3 * hid] + acc_mid[b, hid:, hid:]
        for a in range(3):
            t = 3 * a + b
            block = total[:, a * hid : (a + 1) * hid].astype(bf16)
            for h in range(2):
                pay[h, :, t * hid : (t + 1) * hid] = block[32 * h : 32 * h + 32]
    slots = []
    pieces = []
    for a in range(3):
        for b in range(3):
            at = (2 - b) * 4 * slot + (2 - a) * slot
            slots.append(
                acc_small[0, at : at + slot, :hid] + acc_small[0, at + slot : at + 2 * slot, hid:]
            )
            at = b * 4 * slot + a * slot
            pieces.append(
                acc_small[1, at : at + 2, :hid] + acc_small[1, at + slot : at + slot + 2, hid:]
            )
    sums_in, sums_mid = lane_sums(bias_acc[1]), lane_sums(bias_acc[0])
    pieces.append(sums_in[:, :hid] + sums_in[:, hid:])
    pieces.append(sums_mid[:, :hid] + sums_mid[:, hid:])
    pieces.append(lane_sums(bias_out)[:, :hid])
    pieces.append(jnp.zeros((11, hid), f32))
    rest = jnp.concatenate(pieces, axis=0)
    slots += [rest[:slot], rest[slot:], jnp.zeros((slot, hid), f32)]
    for h in range(2):
        for q in range(3):
            at = 6 * h + 2 * q
            block = jnp.concatenate(slots[at : at + 2], axis=0).astype(bf16)
            pay[h, :, (9 + q) * hid : (10 + q) * hid] = block
    core = core_ref[0]
    keep_ref[...] = pay[core]
    send_ref[...] = pay[1 - core]


def advance_kernel(
    rows,
    cols,
    ext_ref,
    forcing_ref,
    w_head_ref,
    b_head_ref,
    w_in_t_ref,
    act_two_in,
    act_two_edge,
    grad_one_in,
    grad_one_edge,
    new_ref,
    grad_ref,
    stage,
    head,
    back,
):
    low, high, deep = halo, halo + rows, rows + 2 * halo
    act_two, grad_one = (
        split_rows(hid, k, low + k, high - k, deep - k, edge.at[0], inner, edge.at[1])
        for k, inner, edge in ((2, act_two_in, act_two_edge), (3, grad_one_in, grad_one_edge))
    )
    stage[...] = jnp.zeros(stage.shape, f32)
    stage[:, 0:deep, 0 : cols + 2 * halo] = ext_ref[...]
    w0, w1, c0, c1 = stage[0], stage[1], stage[2], stage[3]
    head[...] = jnp.zeros(head.shape, f32)
    back[...] = jnp.zeros(back.shape, f32)
    w_head = w_head_ref[...]
    b_head = b_head_ref[:, 0:1]
    for r in range(3, deep - 3, 2):
        part = mm(w_head, act_two.get(r - 1, r + 3))
        size = 2 * slot
        out = b_head
        for b in range(3):
            out = out + shift(part[b * size : (b + 1) * size], 0, b - 1)
        put_rows(head, r * slot, out)
    w_in_t = w_in_t_ref[...]
    for r in range(halo, halo + rows, 2):
        part = mm(w_in_t, grad_one.get(r - 1, r + 3))
        out = part[16:32]
        for b in (0, 2):
            out = out + shift(part[b * 16 : (b + 1) * 16], 0, b - 1)
        put_rows(back, r * 8, out)

    coefs = [take_plane(head, k, deep, slot) for k in range(coef)]
    mean_x = sum(coefs[1:6], coefs[0]) * (1.0 / 6.0)
    mean_y = sum(coefs[7:12], coefs[6]) * (1.0 / 6.0)
    sx = [coefs[k] - mean_x + face_base[0][k] for k in range(6)]
    sy = [coefs[6 + k] - mean_y + face_base[1][k] for k in range(6)]
    normal_x, normal_y = faces(w0, w1)
    grad_x = [-advection * (c - shift(c, 1, 0)) for c in (c0, c1)]
    grad_y = [-advection * (c - shift(c, 0, 1)) for c in (c0, c1)]
    normal_grad_x, normal_grad_y = 0.0, 0.0
    for c, (w, cot) in enumerate(((w0, c0), (w1, c1))):
        table = shifted_fields(w)
        face_x = sum(s * table[tap] for s, tap in zip(sx, taps_x))
        face_y = sum(s * table[tap] for s, tap in zip(sy, taps_y))
        flux_x = normal_x * face_x
        flux_y = normal_y * face_y
        normal_grad_x = normal_grad_x + grad_x[c] * face_x
        normal_grad_y = normal_grad_y + grad_y[c] * face_y
        around = table[1, 0] + table[-1, 0] + table[0, 1] + table[0, -1]
        new = (
            w
            - advection
            * (flux_x - shift(flux_x, -1, 0) + flux_y - shift(flux_y, 0, -1))
            + viscosity * (around - 4.0 * w)
        )
        if c == 0:
            new = new + forcing_ref[...]
        new_ref[c] = new[halo : halo + rows, halo : halo + cols]
    for c, cot in enumerate((c0, c1)):
        around = shift(cot, 1, 0) + shift(cot, -1, 0) + shift(cot, 0, 1) + shift(cot, 0, -1)
        total = cot + viscosity * (around - 4.0 * cot)
        flow_x = normal_x * grad_x[c]
        flow_y = normal_y * grad_y[c]
        by_col = {-1: {}, 0: {}, 1: {}}
        for s, (a, b) in zip(sx, taps_x):
            by_col[b][a] = by_col[b].get(a, 0.0) + flow_x * s
        for s, (a, b) in zip(sy, taps_y):
            by_col[b][a] = by_col[b].get(a, 0.0) + flow_y * s
        for b, column in by_col.items():
            part = sum(shift(value, -a, 0) for a, value in column.items())
            total = total + shift(part, 0, -b)
        if c == 0:
            total = total + 0.5 * (normal_grad_x + shift(normal_grad_x, -1, 0))
        else:
            total = total + 0.5 * (normal_grad_y + shift(normal_grad_y, 0, -1))
        total = total + take_plane(back, c, deep, 8)
        grad_ref[c] = total[halo : halo + rows, halo : halo + cols]


def finish_kernel(
    scale, mine_ref, other_ref, core_ref, in_ref, b_in_ref, mid_ref, b_mid_ref, out_ref, b_out_ref
):
    mine = mine_ref[...].astype(f32) * scale
    other = other_ref[...].astype(f32) * scale
    first = core_ref[0] == 0
    halves = (jnp.where(first, mine, other), jnp.where(first, other, mine))
    slots = []
    for h, half in enumerate(halves):
        for t in range(9):
            mid_ref[t, 32 * h : 32 * h + 32, :] = half[:, t * hid : (t + 1) * hid]
        for q in range(3):
            block = half[:, (9 + q) * hid : (10 + q) * hid]
            slots += [block[:slot], block[slot:]]
    for a in range(3):
        for b in range(3):
            out_ref[:, a, b, :] = slots[3 * a + b][:coef]
    for t in range(9):
        in_ref[t] = slots[9 + t // 8][2 * t % 16 : 2 * t % 16 + 2]
    b_in_ref[...] = slots[10][2:3]
    b_mid_ref[...] = slots[10][3:4]
    b_out_ref[...] = slots[10][4:5, :coef]


def in_hbm(array):
    return pltpu.with_memory_space_constraint(array, pltpu.HBM)


def fetched(sources, targets, sems):
    copies = [
        pltpu.make_async_copy(source, target, sems.at[k])
        for k, (source, target) in enumerate(zip(sources, targets))
    ]
    for copy in copies:
        copy.start()
    for copy in copies:
        copy.wait()


def pack_kernel(even_ref, velocity_ref, cotangent_ref, fields_ref, far_ref, near_ref, sems):
    cols = fields_ref.shape[2]
    fetched(
        (velocity_ref, cotangent_ref), (fields_ref.at[0:2], fields_ref.at[2:4]), sems
    )
    first = fields_ref[:, :, 0:halo].astype(bf16)
    last = fields_ref[:, :, cols - halo : cols].astype(bf16)
    even = even_ref[0] == 1
    far_ref[...] = jnp.where(even, first, last)
    near_ref[...] = jnp.where(even, last, first)


def weights_kernel(*refs):
    sources, refs = refs[:6], refs[6:]
    outs, (*inputs, sems) = refs[:9], refs[9:]
    fetched(sources, inputs, sems)
    k_in_ref, k_mid_ref, k_out_ref, b_in_ref, b_mid_ref, b_out_ref = inputs
    w_in_ref, w_mid_ref, w_mid_t_ref, w_out_t_ref, w_head_ref, w_in_t_ref, *outs = outs
    c_in_ref, c_mid_ref, c_head_ref = outs

    def band(block, upper):
        none = jnp.zeros(block[0].shape, f32)
        return jnp.concatenate([none, *block] if upper else [*block, none], axis=1)

    def tall(block, rows):
        return jnp.concatenate(
            [block, jnp.zeros((rows - block.shape[0], block.shape[1]), f32)], axis=0
        )

    k_mid = [k_mid_ref[t].astype(f32) for t in range(9)]
    k_mid_t = [k.T for k in k_mid]
    k_out = [k_out_ref[:, t // 3, t % 3, :].astype(f32) for t in range(9)]
    k_in = [k_in_ref[t].astype(f32) for t in range(9)]
    in_rows = []
    out_rows = []
    zero = jnp.zeros((slot, hid), f32)
    for b in range(3):
        forward = [3 * a + b for a in range(3)]
        backward = [8 - t for t in forward]
        for u in range(2):
            at = slice(u * hid, (u + 1) * hid)
            w_mid_ref[b, at, :] = band([k_mid[t] for t in forward], u).astype(bf16)
            w_mid_t_ref[b, at, :] = band([k_mid_t[t] for t in backward], u).astype(bf16)
        head = [band([tall(k_out[t], slot) for t in forward], u) for u in range(2)]
        w_head_ref[2 * slot * b : 2 * slot * (b + 1), :] = jnp.concatenate(head, 0).astype(bf16)
        back = [band([tall(k_in[t], 8) for t in backward], u) for u in range(2)]
        w_in_t_ref[16 * b : 16 * (b + 1), :] = jnp.concatenate(back, 0).astype(bf16)
        for rows, blocks in (
            (in_rows, [tall(k_in[t], slot) for t in forward]),
            (out_rows, [tall(k_out[t], slot) for t in backward]),
        ):
            lower = jnp.concatenate(blocks + [zero], axis=0)
            upper = jnp.concatenate([zero] + blocks, axis=0)
            rows.append(jnp.concatenate([lower, upper], axis=1))
    w_in_ref[...] = jnp.concatenate(in_rows, axis=0).T.astype(bf16)
    w_out_t_ref[...] = jnp.concatenate(out_rows, axis=0).T.astype(bf16)
    for ref, bias in ((c_in_ref, b_in_ref[...]), (c_mid_ref, b_mid_ref[...])):
        ref[...] = jnp.broadcast_to(jnp.concatenate([bias, bias], axis=1), (128, 128)).T
    bias = jnp.concatenate([b_out_ref[...], jnp.zeros((1, slot - coef), f32)], axis=1)
    bias = jnp.concatenate([bias, bias, jnp.zeros((1, 128 - 2 * slot), f32)], axis=1)
    c_head_ref[...] = jnp.broadcast_to(bias, (128, 128)).T[: 2 * slot]


def edges(fields, axis, dim):
    size = fields.shape[dim]
    even = lax.axis_index(axis) % 2 == 0
    first = lax.slice_in_dim(fields, 0, halo, axis=dim).astype(bf16)
    last = lax.slice_in_dim(fields, size - halo, size, axis=dim).astype(bf16)
    return jnp.where(even, first, last), jnp.where(even, last, first)


def widened(fields, far, near, axis, dim):
    count = lax.axis_size(axis)
    even = lax.axis_index(axis) % 2 == 0
    far_pairs = [(i, (i + 1 if i % 2 else i - 1) % count) for i in range(count)]
    far = lax.ppermute(far, axis, far_pairs)
    near = lax.ppermute(near, axis, [(i, i ^ 1) for i in range(count)])
    low = jnp.where(even, far, near).astype(f32)
    high = jnp.where(even, near, far).astype(f32)
    return jnp.concatenate([low, fields, high], axis=dim)


def swap(value, rows, cols):
    height, width = lax.axis_size("gx"), lax.axis_size("gy")
    pairs = [
        (i * width + j, (i ^ rows) * width + (j ^ cols)) for i in range(height) for j in range(width)
    ]
    return lax.ppermute(value, ("gx", "gy"), pairs)


def added(*values):
    sums = [v.astype(f32) for v in values]
    while len(sums) > 1:
        sums = [sums[k] + sums[k + 1] for k in range(0, len(sums), 2)]
    return sums[0].astype(bf16)


def summed(keep, send, beside):
    half = added(keep, swap(send, 0, 1))
    steps = [(0, 1 << k) for k in range(1, lax.axis_size("gy").bit_length() - 1)]
    steps += [(1 << k, 0) for k in range(lax.axis_size("gx").bit_length() - 1)]
    while steps:
        if len(steps) >= 2 and steps[0][0] == 0 and steps[1][1] == 0:
            (_, cols), (rows, _) = steps[:2]
            half = added(
                half,
                swap(half, 0, cols),
                swap(half, rows, 0),
                swap(half, rows, cols),
            )
            steps = steps[2:]
        else:
            arrived = swap(half, *steps[0])
            steps = steps[1:]
            if not steps:
                arrived, beside = lax.optimization_barrier((arrived, beside))
            half = added(half, arrived)
    return half, swap(half, 0, 1), beside


def per_device(velocity, kernel_in, bias_in, kernel_mid, bias_mid, kernel_out, bias_out, cotangent):
    rows, cols = velocity.shape[1], velocity.shape[2]
    ny_total = lax.axis_size("gy") * cols
    cell_count = lax.axis_size("gx") * rows * ny_total
    deep = rows + 2 * halo
    height = deep
    width = -(-(cols + 2 * halo) // 128) * 128
    vmem = pl.BlockSpec(memory_space=pltpu.VMEM)
    params = pltpu.CompilerParams(vmem_limit_bytes=18 << 20)

    core = (lax.axis_index("gy") % 2).astype(jnp.int32).reshape(1)
    smem = pl.BlockSpec(memory_space=pltpu.SMEM)
    hbm = pl.BlockSpec(memory_space=pltpu.HBM)
    w_in, w_mid, w_mid_t, w_out_t, w_head, w_in_t, b_in, b_mid, b_head = pl.pallas_call(
        weights_kernel,
        out_shape=(
            jax.ShapeDtypeStruct((2 * hid, 12 * slot), bf16),
            jax.ShapeDtypeStruct((3, 2 * hid, 4 * hid), bf16),
            jax.ShapeDtypeStruct((3, 2 * hid, 4 * hid), bf16),
            jax.ShapeDtypeStruct((2 * hid, 12 * slot), bf16),
            jax.ShapeDtypeStruct((6 * slot, 4 * hid), bf16),
            jax.ShapeDtypeStruct((48, 4 * hid), bf16),
            jax.ShapeDtypeStruct((128, 128), f32),
            jax.ShapeDtypeStruct((128, 128), f32),
            jax.ShapeDtypeStruct((2 * slot, 128), f32),
        ),
        in_specs=[hbm] * 6,
        out_specs=(vmem,) * 9,
        scratch_shapes=[
            pltpu.VMEM((9, 2, hid), bf16),
            pltpu.VMEM((9, hid, hid), bf16),
            pltpu.VMEM((coef, 3, 3, hid), bf16),
            pltpu.VMEM((1, hid), f32),
            pltpu.VMEM((1, hid), f32),
            pltpu.VMEM((1, coef), f32),
            pltpu.SemaphoreType.DMA((6,)),
        ],
        compiler_params=params,
        name="weights",
    )(
        in_hbm(jnp.transpose(kernel_in, (2, 3, 1, 0)).reshape(9, 2, hid)),
        in_hbm(jnp.transpose(kernel_mid, (2, 3, 0, 1)).reshape(9, hid, hid)),
        in_hbm(jnp.transpose(kernel_out, (0, 2, 3, 1))),
        in_hbm(bias_in[None, :]),
        in_hbm(bias_mid[None, :]),
        in_hbm(bias_out[None, :]),
    )
    columns = lax.iota(jnp.int32, width) - halo + lax.axis_index("gy") * cols
    forcing = forcing_amp * jnp.sin(2.0 * math.pi * forcing_wave * columns.astype(f32) / ny_total)
    even = (lax.axis_index("gy") % 2 == 0).astype(jnp.int32).reshape(1)
    edge = jax.ShapeDtypeStruct((4, rows, halo), bf16)
    fields, far, near = pl.pallas_call(
        pack_kernel,
        out_shape=(jax.ShapeDtypeStruct((4, rows, cols), f32), edge, edge),
        in_specs=[smem, hbm, hbm],
        out_specs=(vmem,) * 3,
        scratch_shapes=[pltpu.SemaphoreType.DMA((2,))],
        compiler_params=params,
        name="pack",
    )(even, in_hbm(velocity), in_hbm(cotangent))
    wide = widened(fields, far, near, "gy", 2)
    maps = (w_in, w_mid, w_mid_t, w_out_t, b_in, b_mid)
    far_near, maps = lax.optimization_barrier((edges(wide, "gx", 1), maps))
    ext = widened(wide, *far_near, "gx", 1)

    accs = (
        jax.ShapeDtypeStruct((3, 2 * hid, 4 * hid), f32),
        jax.ShapeDtypeStruct((2, 12 * slot, 2 * hid), f32),
        jax.ShapeDtypeStruct((2, 2 * hid, width), f32),
    )
    act_one, slope_one, grad_two, act_two_in, grad_one_in, *totals = pl.pallas_call(
        lambda *refs: inner_kernel(rows, cols, *refs),
        out_shape=(
            jax.ShapeDtypeStruct((3, (rows - 2) * hid, width), bf16),
            jax.ShapeDtypeStruct(((rows - 2) * hid, width), f32),
            jax.ShapeDtypeStruct((3, (rows - 4) * hid, width), bf16),
            jax.ShapeDtypeStruct(((rows - 4) * hid, width), bf16),
            jax.ShapeDtypeStruct(((rows - 6) * hid, width), bf16),
            *accs,
        ),
        in_specs=[vmem] * 7,
        out_specs=(vmem,) * 8,
        scratch_shapes=[
            pltpu.VMEM((4, rows, width), f32),
            pltpu.VMEM((width // 128, rows * slot, 128), f32),
            pltpu.VMEM((2, 3, rows * slot, width), bf16),
        ],
        compiler_params=params,
        name="inner",
    )(wide, *maps)

    keep, send, act_two_edge, grad_one_edge = pl.pallas_call(
        lambda *refs: outer_kernel(rows, cols, *refs),
        out_shape=(
            jax.ShapeDtypeStruct((hid // 2, 12 * hid), bf16),
            jax.ShapeDtypeStruct((hid // 2, 12 * hid), bf16),
            jax.ShapeDtypeStruct((2, halo * hid, width), bf16),
            jax.ShapeDtypeStruct((2, halo * hid, width), bf16),
        ),
        in_specs=[vmem] * 7 + [smem] + [vmem] * 7,
        out_specs=(vmem,) * 4,
        scratch_shapes=[
            pltpu.VMEM((2, hid // 2, 12 * hid), bf16),
            pltpu.VMEM((4, deep, width), f32),
            pltpu.VMEM((width // 128, deep * slot, 128), f32),
            pltpu.VMEM((2, 3, deep * slot, width), bf16),
            pltpu.VMEM((2, 3, halo * hid, width), bf16),
            pltpu.VMEM((2, halo * hid, width), f32),
            pltpu.VMEM((2, 3, halo * hid, width), bf16),
            *(pltpu.VMEM(acc.shape, f32) for acc in accs),
        ],
        compiler_params=params,
        name="outer",
    )(ext, *maps, core, act_one, slope_one, grad_two, grad_one_in, *totals)

    new_velocity, grad_velocity = pl.pallas_call(
        lambda *refs: advance_kernel(rows, cols, *refs),
        out_shape=(jax.ShapeDtypeStruct(velocity.shape, f32),) * 2,
        in_specs=[vmem] * 9,
        out_specs=(vmem,) * 2,
        scratch_shapes=[
            pltpu.VMEM((4, height, width), f32),
            pltpu.VMEM((width // 128, deep * slot, 128), f32),
            pltpu.VMEM((width // 128, deep * 8, 128), f32),
        ],
        compiler_params=params,
        name="advance",
    )(ext, forcing[None, :], w_head, b_head, w_in_t, act_two_in, act_two_edge, grad_one_in, grad_one_edge)

    mine, other, (new_velocity, grad_velocity) = summed(
        keep, send, (new_velocity, grad_velocity)
    )
    g_in, gb_in, g_mid, gb_mid, g_out, gb_out = pl.pallas_call(
        lambda *refs: finish_kernel(1.0 / math.sqrt(cell_count), *refs),
        out_shape=(
            jax.ShapeDtypeStruct((9, 2, hid), f32),
            jax.ShapeDtypeStruct((1, hid), f32),
            jax.ShapeDtypeStruct((9, hid, hid), f32),
            jax.ShapeDtypeStruct((1, hid), f32),
            jax.ShapeDtypeStruct((coef, 3, 3, hid), f32),
            jax.ShapeDtypeStruct((1, coef), f32),
        ),
        in_specs=[vmem] * 2 + [smem],
        out_specs=(vmem,) * 6,
        compiler_params=params,
        name="finish",
    )(mine, other, core)

    return (
        new_velocity,
        grad_velocity,
        jnp.transpose(g_in.reshape(3, 3, 2, hid), (3, 2, 0, 1)),
        gb_in.reshape(hid),
        jnp.transpose(g_mid.reshape(3, 3, hid, hid), (2, 3, 0, 1)),
        gb_mid.reshape(hid),
        jnp.transpose(g_out, (0, 3, 1, 2)),
        gb_out.reshape(coef),
    )


def solution(mesh):
    in_specs = (P("groups", "gx", "gy"), P(), P(), P(), P(), P(), P(), P("groups", "gx", "gy"))
    out_specs = (
        P("groups", "gx", "gy"),
        P("groups", "gx", "gy"),
        P("groups", None, None, None),
        P("groups"),
        P("groups", None, None, None),
        P("groups"),
        P("groups", None, None, None),
        P("groups"),
    )
    return jax.shard_map(
        per_device, mesh=mesh, in_specs=in_specs, out_specs=out_specs, check_vma=False
    )
```

```python
import math

import jax
import jax.numpy as jnp
from jax import lax
from jax.experimental import pallas as pl
from jax.experimental.pallas import tpu as pltpu
from jax.sharding import PartitionSpec as P

advection = 0.2
viscosity = 0.05
forcing_amp = 0.05
forcing_wave = 4
face_base = ((0.0, 0.5, 0.0, 0.0, 0.5, 0.0), (0.0, 0.0, 0.5, 0.5, 0.0, 0.0))
halo = 4
hid = 64
coef = 12
slot = 16
taps_x = [(a, b) for a in (0, 1) for b in (-1, 0, 1)]
taps_y = [(a, b) for a in (-1, 0, 1) for b in (0, 1)]
f32 = jnp.float32
bf16 = jnp.bfloat16


def shift(value, rows, cols):
    if rows:
        value = pltpu.roll(value, (-rows) % value.shape[-2], value.ndim - 2)
    if cols:
        value = pltpu.roll(value, (-cols) % value.shape[-1], value.ndim - 1)
    return value


def mm(lhs, rhs):
    return lax.dot_general(lhs, rhs, (((1,), (0,)), ((), ())), preferred_element_type=f32)


def mm_nt(lhs, rhs):
    return lax.dot_general(lhs, rhs, (((1,), (1,)), ((), ())), preferred_element_type=f32)


def sigma_of(linear):
    return 0.5 * jnp.tanh(0.5 * linear) + 0.5


class Rows:
    def __init__(self, size, *pieces):
        self.size = size
        self.pieces = pieces

    def get(self, lo, hi, lead=()):
        parts = []
        for start, stop, ref in self.pieces:
            first, last = max(lo, start), min(hi, stop)
            if first < last:
                rows = slice((first - start) * self.size, (last - start) * self.size)
                parts.append((first, ref[(*lead, rows, slice(None))]))
        parts = [part for _, part in sorted(parts, key=lambda item: item[0])]
        return parts[0] if len(parts) == 1 else jnp.concatenate(parts, axis=0)

    def put(self, lo, value, lead=()):
        for start, stop, ref in self.pieces:
            if start <= lo < stop:
                rows = slice((lo - start) * self.size, (lo - start) * self.size + value.shape[0])
                ref[(*lead, rows, slice(None))] = value

    def put_shifted(self, lo, value, lead=()):
        value = value.astype(bf16)
        for b in range(3):
            self.put(lo, shift(value, 0, b - 1), (*lead, b))

    def window(self, lo, hi, lead=()):
        return jnp.concatenate([self.get(lo, hi, (*lead, b)) for b in range(3)], axis=0)


def put_plane(planes, k, stride, value):
    for j in range(planes.shape[0]):
        planes[j, pl.ds(k, value.shape[0], stride=stride), :] = value[:, 128 * j : 128 * j + 128]


def take_plane(planes, k, count, stride):
    tiles = [planes[j, pl.ds(k, count, stride=stride), :] for j in range(planes.shape[0])]
    return jnp.concatenate(tiles, axis=1)


def take_rows(planes, at, size):
    return jnp.concatenate([planes[j, at : at + size, :] for j in range(planes.shape[0])], axis=1)


def put_rows(planes, at, value):
    for j in range(planes.shape[0]):
        planes[j, at : at + value.shape[0], :] = value[:, 128 * j : 128 * j + 128]


def faces(w0, w1):
    normal_x = 0.5 * (w0 + shift(w0, 1, 0))
    normal_y = 0.5 * (w1 + shift(w1, 0, 1))
    return normal_x, normal_y


def shifted_fields(w):
    table = {}
    for b in (-1, 0, 1):
        col = shift(w, 0, b)
        for a in (-1, 0, 1):
            table[a, b] = shift(col, a, 0)
    return table


def lane_sums(total):
    lanes = total.shape[1]
    part = total[:, :128]
    for k in range(1, lanes // 128):
        part = part + total[:, 128 * k : 128 * k + 128]
    return jnp.sum(part.T, axis=0, keepdims=True)


def prepare(first, rows, cols, ext_ref, stage, planes, state_in, state_rows, head_rows):
    count = ext_ref.shape[1]
    height, width = stage.shape[1], stage.shape[2]
    stage[...] = jnp.zeros(stage.shape, f32)
    stage[:, 0:count, 0 : cols + 2 * halo] = ext_ref[...]
    w0, w1, c0, c1 = stage[0], stage[1], stage[2], stage[3]

    planes[...] = jnp.zeros(planes.shape, f32)
    put_plane(planes, 0, slot, w0)
    put_plane(planes, 1, slot, w1)
    for r in state_rows:
        state_in.put_shifted(r, take_rows(planes, (r - first) * slot, 2 * slot), (0,))

    normal_x, normal_y = faces(w0, w1)
    t0, t1 = shifted_fields(w0), shifted_fields(w1)
    fx0 = -advection * (c0 - shift(c0, 1, 0)) * normal_x
    fx1 = -advection * (c1 - shift(c1, 1, 0)) * normal_x
    fy0 = -advection * (c0 - shift(c0, 0, 1)) * normal_y
    fy1 = -advection * (c1 - shift(c1, 0, 1)) * normal_y
    lane = lax.broadcasted_iota(jnp.int32, (height, width), 1)
    row_id = lax.broadcasted_iota(jnp.int32, (height, width), 0) + first
    own = (lane >= halo) & (lane < halo + cols) & (row_id >= halo) & (row_id < halo + rows)
    sums = []
    for at, taps, g0, g1 in ((0, taps_x, fx0, fx1), (6, taps_y, fy0, fy1)):
        raw = [g0 * t0[tap] + g1 * t1[tap] for tap in taps]
        mean = sum(raw[1:], raw[0]) * (1.0 / 6.0)
        for k in range(6):
            value = raw[k] - mean
            put_plane(planes, at + k, slot, value)
            sums.append(jnp.sum(jnp.where(own, value, 0.0), axis=0, keepdims=True))
    for r in head_rows:
        state_in.put_shifted(r, take_rows(planes, (r - first) * slot, 2 * slot), (1,))
    return sums


def layers(
    rows,
    cols,
    groups,
    refs,
    state_in,
    act_one,
    slope_one,
    grad_two,
    act_two,
    grad_one,
    acc_mid,
    acc_small,
    bias_acc,
):
    w_in_ref, w_mid_ref, w_mid_t_ref, w_out_t_ref, b_in_ref, b_mid_ref = refs
    width = bias_acc.shape[2]
    lane = lax.broadcasted_iota(jnp.int32, (1, width), 1)
    own_cols = (lane >= halo) & (lane < halo + cols)
    groups_one, groups_two, groups_back, groups_in = groups

    w_in = w_in_ref[...]
    b_in = b_in_ref[:, 0:1]
    for r in groups_one:
        linear = mm(w_in, state_in.window(r - 1, r + 3, (0,))) + b_in
        sigma = sigma_of(linear)
        act = linear * sigma
        act_one.put_shifted(r, act)
        slope_one.put(r, sigma + act * (1.0 - sigma))

    b_mid = b_mid_ref[:, 0:1]
    w_out_t = w_out_t_ref[...]
    w_mid = jnp.concatenate([w_mid_ref[b] for b in range(3)], axis=1)
    w_mid_t = jnp.concatenate([w_mid_t_ref[b] for b in range(3)], axis=1)
    held = []
    for r in groups_two:
        window = [act_one.get(r - 1, r + 3, (b,)) for b in range(3)]
        linear = mm(w_mid, jnp.concatenate(window, axis=0)) + b_mid
        sigma = sigma_of(linear)
        act = linear * sigma
        act_two.put(r, act.astype(bf16))
        fed = state_in.window(r - 1, r + 3, (1,))
        grad = mm(w_out_t, fed) * (sigma + act * (1.0 - sigma))
        grad_two.put_shifted(r, grad)
        if halo <= r < halo + rows:
            kept = jnp.where(own_cols, grad, 0.0)
            bias_acc[0] += kept
            kept = kept.astype(bf16)
            held.append((kept, window, fed, jnp.where(own_cols, act, 0.0).astype(bf16)))
        if held and (len(held) == 2 or r == groups_two[-1]):
            kepts, windows, feds, acts = zip(*held)
            held = []
            kepts = jnp.concatenate(kepts, axis=1)
            for b in range(3):
                acc_mid[b] += mm_nt(kepts, jnp.concatenate([w[b] for w in windows], axis=1))
            acc_small[0] += mm_nt(jnp.concatenate(feds, axis=1), jnp.concatenate(acts, axis=1))

    for r in groups_back:
        grad = mm(w_mid_t, grad_two.window(r - 1, r + 3)) * slope_one.get(r, r + 2)
        grad_one.put(r, grad.astype(bf16))
        kept = jnp.where(own_cols, grad, 0.0)
        if r < halo:
            bias_acc[1, hid:, :] += kept[hid:, :]
        elif r + 2 > halo + rows:
            bias_acc[1, :hid, :] += kept[:hid, :]
        else:
            bias_acc[1] += kept
    for r in groups_in:
        kept = jnp.where(own_cols, grad_one.get(r, r + 2), jnp.zeros((), bf16))
        acc_small[1] += mm_nt(state_in.window(r - 1, r + 3, (0,)), kept)


def inner_kernel(rows, cols, ext_ref, *refs):
    weight_refs, refs = refs[:6], refs[6:]
    act_one, slope_one, grad_two, act_two, grad_one, acc_mid, acc_small, bias_acc, *refs = refs
    stage, planes, state_in = refs
    low, high = halo, halo + rows
    state_in = Rows(slot, (low, high, state_in))
    acc_mid[...] = jnp.zeros(acc_mid.shape, f32)
    acc_small[...] = jnp.zeros(acc_small.shape, f32)
    bias_acc[...] = jnp.zeros(bias_acc.shape, f32)
    pairs = range(low, high, 2)
    prepare(low, rows, cols, ext_ref, stage, planes, state_in, pairs, pairs)
    groups = [range(low + k, high - k, 2) for k in (1, 2, 3, 4)]
    layers(
        rows,
        cols,
        groups,
        weight_refs,
        state_in,
        Rows(hid, (low + 1, high - 1, act_one)),
        Rows(hid, (low + 1, high - 1, slope_one)),
        Rows(hid, (low + 2, high - 2, grad_two)),
        Rows(hid, (low + 2, high - 2, act_two)),
        Rows(hid, (low + 3, high - 3, grad_one)),
        acc_mid,
        acc_small,
        bias_acc,
    )


def split_rows(size, first, low, high, last, lower_ref, inner_ref, upper_ref):
    return Rows(size, (first, low, lower_ref), (low, high, inner_ref), (high, last, upper_ref))


def outer_kernel(rows, cols, ext_ref, *refs):
    weight_refs, core_ref, refs = refs[:6], refs[6], refs[7:]
    act_one_in, slope_one_in, grad_two_in, grad_one_in, acc_mid_in, acc_small_in, bias_in, *refs = refs
    keep_ref, send_ref, act_two, grad_one, *refs = refs
    pay, stage, planes, state_in, act_one, slope_one, grad_two, acc_mid, acc_small, bias_acc = refs
    low, high, deep = halo, halo + rows, rows + 2 * halo
    acc_mid[...] = acc_mid_in[...]
    acc_small[...] = acc_small_in[...]
    bias_acc[...] = bias_in[...]
    state_in = Rows(slot, (0, deep, state_in))
    state_rows = [r for r in range(0, deep, 2) if r < low + 6 or r + 2 > high - 6]
    head_rows = [r for r in range(0, deep, 2) if r < low + 4 or r + 2 > high - 4]
    sums = prepare(0, rows, cols, ext_ref, stage, planes, state_in, state_rows, head_rows)
    bias_out = jnp.concatenate(sums + [jnp.zeros((128 - coef, stage.shape[2]), f32)], axis=0)
    groups = [
        [*range(k, low + k, 2), *range(high - k, deep - k, 2)] for k in (1, 2, 3)
    ]
    groups.append([low, low + 2, high - 4, high - 2])

    def both(k, edge, inner):
        edges = [edge.at[i] for i in range(2)]
        return split_rows(hid, k, low + k, high - k, deep - k, edges[0], inner, edges[1])

    layers(
        rows,
        cols,
        groups,
        weight_refs,
        state_in,
        both(1, act_one, act_one_in),
        both(1, slope_one, slope_one_in),
        both(2, grad_two, grad_two_in),
        Rows(hid, (2, low + 2, act_two.at[0]), (high - 2, deep - 2, act_two.at[1])),
        both(3, grad_one, grad_one_in),
        acc_mid,
        acc_small,
        bias_acc,
    )

    for b in range(3):
        total = acc_mid[b, :hid, : 3 * hid] + acc_mid[b, hid:, hid:]
        for a in range(3):
            t = 3 * a + b
            block = total[:, a * hid : (a + 1) * hid].astype(bf16)
            for h in range(2):
                pay[h, :, t * hid : (t + 1) * hid] = block[32 * h : 32 * h + 32]
    slots = []
    pieces = []
    for a in range(3):
        for b in range(3):
            at = (2 - b) * 4 * slot + (2 - a) * slot
            slots.append(
                acc_small[0, at : at + slot, :hid] + acc_small[0, at + slot : at + 2 * slot, hid:]
            )
            at = b * 4 * slot + a * slot
            pieces.append(
                acc_small[1, at : at + 2, :hid] + acc_small[1, at + slot : at + slot + 2, hid:]
            )
    sums_in, sums_mid = lane_sums(bias_acc[1]), lane_sums(bias_acc[0])
    pieces.append(sums_in[:, :hid] + sums_in[:, hid:])
    pieces.append(sums_mid[:, :hid] + sums_mid[:, hid:])
    pieces.append(lane_sums(bias_out)[:, :hid])
    pieces.append(jnp.zeros((11, hid), f32))
    rest = jnp.concatenate(pieces, axis=0)
    slots += [rest[:slot], rest[slot:], jnp.zeros((slot, hid), f32)]
    for h in range(2):
        for q in range(3):
            at = 6 * h + 2 * q
            block = jnp.concatenate(slots[at : at + 2], axis=0).astype(bf16)
            pay[h, :, (9 + q) * hid : (10 + q) * hid] = block
    core = core_ref[0]
    keep_ref[...] = pay[core]
    send_ref[...] = pay[1 - core]


def advance_kernel(
    rows,
    cols,
    ext_ref,
    forcing_ref,
    w_head_ref,
    b_head_ref,
    w_in_t_ref,
    act_two_in,
    act_two_edge,
    grad_one_in,
    grad_one_edge,
    new_ref,
    grad_ref,
    stage,
    head,
    back,
):
    low, high, deep = halo, halo + rows, rows + 2 * halo
    act_two, grad_one = (
        split_rows(hid, k, low + k, high - k, deep - k, edge.at[0], inner, edge.at[1])
        for k, inner, edge in ((2, act_two_in, act_two_edge), (3, grad_one_in, grad_one_edge))
    )
    stage[...] = jnp.zeros(stage.shape, f32)
    stage[:, 0:deep, 0 : cols + 2 * halo] = ext_ref[...]
    w0, w1, c0, c1 = stage[0], stage[1], stage[2], stage[3]
    head[...] = jnp.zeros(head.shape, f32)
    back[...] = jnp.zeros(back.shape, f32)
    w_head = w_head_ref[...]
    b_head = b_head_ref[:, 0:1]
    for r in range(3, deep - 3, 2):
        part = mm(w_head, act_two.get(r - 1, r + 3))
        size = 2 * slot
        out = b_head
        for b in range(3):
            out = out + shift(part[b * size : (b + 1) * size], 0, b - 1)
        put_rows(head, r * slot, out)
    w_in_t = w_in_t_ref[...]
    for r in range(halo, halo + rows, 2):
        part = mm(w_in_t, grad_one.get(r - 1, r + 3))
        out = part[16:32]
        for b in (0, 2):
            out = out + shift(part[b * 16 : (b + 1) * 16], 0, b - 1)
        put_rows(back, r * 8, out)

    coefs = [take_plane(head, k, deep, slot) for k in range(coef)]
    mean_x = sum(coefs[1:6], coefs[0]) * (1.0 / 6.0)
    mean_y = sum(coefs[7:12], coefs[6]) * (1.0 / 6.0)
    sx = [coefs[k] - mean_x + face_base[0][k] for k in range(6)]
    sy = [coefs[6 + k] - mean_y + face_base[1][k] for k in range(6)]
    normal_x, normal_y = faces(w0, w1)
    grad_x = [-advection * (c - shift(c, 1, 0)) for c in (c0, c1)]
    grad_y = [-advection * (c - shift(c, 0, 1)) for c in (c0, c1)]
    normal_grad_x, normal_grad_y = 0.0, 0.0
    for c, (w, cot) in enumerate(((w0, c0), (w1, c1))):
        table = shifted_fields(w)
        face_x = sum(s * table[tap] for s, tap in zip(sx, taps_x))
        face_y = sum(s * table[tap] for s, tap in zip(sy, taps_y))
        flux_x = normal_x * face_x
        flux_y = normal_y * face_y
        normal_grad_x = normal_grad_x + grad_x[c] * face_x
        normal_grad_y = normal_grad_y + grad_y[c] * face_y
        around = table[1, 0] + table[-1, 0] + table[0, 1] + table[0, -1]
        new = (
            w
            - advection
            * (flux_x - shift(flux_x, -1, 0) + flux_y - shift(flux_y, 0, -1))
            + viscosity * (around - 4.0 * w)
        )
        if c == 0:
            new = new + forcing_ref[...]
        new_ref[c] = new[halo : halo + rows, halo : halo + cols]
    for c, cot in enumerate((c0, c1)):
        around = shift(cot, 1, 0) + shift(cot, -1, 0) + shift(cot, 0, 1) + shift(cot, 0, -1)
        total = cot + viscosity * (around - 4.0 * cot)
        flow_x = normal_x * grad_x[c]
        flow_y = normal_y * grad_y[c]
        by_col = {-1: {}, 0: {}, 1: {}}
        for s, (a, b) in zip(sx, taps_x):
            by_col[b][a] = by_col[b].get(a, 0.0) + flow_x * s
        for s, (a, b) in zip(sy, taps_y):
            by_col[b][a] = by_col[b].get(a, 0.0) + flow_y * s
        for b, column in by_col.items():
            part = sum(shift(value, -a, 0) for a, value in column.items())
            total = total + shift(part, 0, -b)
        if c == 0:
            total = total + 0.5 * (normal_grad_x + shift(normal_grad_x, -1, 0))
        else:
            total = total + 0.5 * (normal_grad_y + shift(normal_grad_y, 0, -1))
        total = total + take_plane(back, c, deep, 8)
        grad_ref[c] = total[halo : halo + rows, halo : halo + cols]


def finish_kernel(
    scale, mine_ref, other_ref, core_ref, in_ref, b_in_ref, mid_ref, b_mid_ref, out_ref, b_out_ref
):
    mine = mine_ref[...].astype(f32) * scale
    other = other_ref[...].astype(f32) * scale
    first = core_ref[0] == 0
    halves = (jnp.where(first, mine, other), jnp.where(first, other, mine))
    slots = []
    for h, half in enumerate(halves):
        for t in range(9):
            mid_ref[t, 32 * h : 32 * h + 32, :] = half[:, t * hid : (t + 1) * hid]
        for q in range(3):
            block = half[:, (9 + q) * hid : (10 + q) * hid]
            slots += [block[:slot], block[slot:]]
    for a in range(3):
        for b in range(3):
            out_ref[:, a, b, :] = slots[3 * a + b][:coef]
    for t in range(9):
        in_ref[t] = slots[9 + t // 8][2 * t % 16 : 2 * t % 16 + 2]
    b_in_ref[...] = slots[10][2:3]
    b_mid_ref[...] = slots[10][3:4]
    b_out_ref[...] = slots[10][4:5, :coef]


def in_hbm(array):
    return pltpu.with_memory_space_constraint(array, pltpu.HBM)


def fetched(sources, targets, sems):
    copies = [
        pltpu.make_async_copy(source, target, sems.at[k])
        for k, (source, target) in enumerate(zip(sources, targets))
    ]
    for copy in copies:
        copy.start()
    for copy in copies:
        copy.wait()


def pack_kernel(even_ref, velocity_ref, cotangent_ref, fields_ref, far_ref, near_ref, sems):
    cols = fields_ref.shape[2]
    fetched(
        (velocity_ref, cotangent_ref), (fields_ref.at[0:2], fields_ref.at[2:4]), sems
    )
    first = fields_ref[:, :, 0:halo].astype(bf16)
    last = fields_ref[:, :, cols - halo : cols].astype(bf16)
    even = even_ref[0] == 1
    far_ref[...] = jnp.where(even, first, last)
    near_ref[...] = jnp.where(even, last, first)


def weights_kernel(*refs):
    sources, refs = refs[:6], refs[6:]
    outs, (*inputs, sems) = refs[:9], refs[9:]
    fetched(sources, inputs, sems)
    k_in_ref, k_mid_ref, k_out_ref, b_in_ref, b_mid_ref, b_out_ref = inputs
    w_in_ref, w_mid_ref, w_mid_t_ref, w_out_t_ref, w_head_ref, w_in_t_ref, *outs = outs
    c_in_ref, c_mid_ref, c_head_ref = outs

    def band(block, upper):
        none = jnp.zeros(block[0].shape, f32)
        return jnp.concatenate([none, *block] if upper else [*block, none], axis=1)

    def tall(block, rows):
        return jnp.concatenate(
            [block, jnp.zeros((rows - block.shape[0], block.shape[1]), f32)], axis=0
        )

    k_mid = [k_mid_ref[t].astype(f32) for t in range(9)]
    k_mid_t = [k.T for k in k_mid]
    k_out = [k_out_ref[:, t // 3, t % 3, :].astype(f32) for t in range(9)]
    k_in = [k_in_ref[t].astype(f32) for t in range(9)]
    in_rows = []
    out_rows = []
    zero = jnp.zeros((slot, hid), f32)
    for b in range(3):
        forward = [3 * a + b for a in range(3)]
        backward = [8 - t for t in forward]
        for u in range(2):
            at = slice(u * hid, (u + 1) * hid)
            w_mid_ref[b, at, :] = band([k_mid[t] for t in forward], u).astype(bf16)
            w_mid_t_ref[b, at, :] = band([k_mid_t[t] for t in backward], u).astype(bf16)
        head = [band([tall(k_out[t], slot) for t in forward], u) for u in range(2)]
        w_head_ref[2 * slot * b : 2 * slot * (b + 1), :] = jnp.concatenate(head, 0).astype(bf16)
        back = [band([tall(k_in[t], 8) for t in backward], u) for u in range(2)]
        w_in_t_ref[16 * b : 16 * (b + 1), :] = jnp.concatenate(back, 0).astype(bf16)
        for rows, blocks in (
            (in_rows, [tall(k_in[t], slot) for t in forward]),
            (out_rows, [tall(k_out[t], slot) for t in backward]),
        ):
            lower = jnp.concatenate(blocks + [zero], axis=0)
            upper = jnp.concatenate([zero] + blocks, axis=0)
            rows.append(jnp.concatenate([lower, upper], axis=1))
    w_in_ref[...] = jnp.concatenate(in_rows, axis=0).T.astype(bf16)
    w_out_t_ref[...] = jnp.concatenate(out_rows, axis=0).T.astype(bf16)
    for ref, bias in ((c_in_ref, b_in_ref[...]), (c_mid_ref, b_mid_ref[...])):
        ref[...] = jnp.broadcast_to(jnp.concatenate([bias, bias], axis=1), (128, 128)).T
    bias = jnp.concatenate([b_out_ref[...], jnp.zeros((1, slot - coef), f32)], axis=1)
    bias = jnp.concatenate([bias, bias, jnp.zeros((1, 128 - 2 * slot), f32)], axis=1)
    c_head_ref[...] = jnp.broadcast_to(bias, (128, 128)).T[: 2 * slot]


def edges(fields, axis, dim):
    size = fields.shape[dim]
    even = lax.axis_index(axis) % 2 == 0
    first = lax.slice_in_dim(fields, 0, halo, axis=dim).astype(bf16)
    last = lax.slice_in_dim(fields, size - halo, size, axis=dim).astype(bf16)
    return jnp.where(even, first, last), jnp.where(even, last, first)


def widened(fields, far, near, axis, dim):
    count = lax.axis_size(axis)
    even = lax.axis_index(axis) % 2 == 0
    far_pairs = [(i, (i + 1 if i % 2 else i - 1) % count) for i in range(count)]
    far = lax.ppermute(far, axis, far_pairs)
    near = lax.ppermute(near, axis, [(i, i ^ 1) for i in range(count)])
    low = jnp.where(even, far, near).astype(f32)
    high = jnp.where(even, near, far).astype(f32)
    return jnp.concatenate([low, fields, high], axis=dim)


def swap(value, rows, cols):
    height, width = lax.axis_size("gx"), lax.axis_size("gy")
    pairs = [
        (i * width + j, (i ^ rows) * width + (j ^ cols)) for i in range(height) for j in range(width)
    ]
    return lax.ppermute(value, ("gx", "gy"), pairs)


def added(*values):
    sums = [v.astype(f32) for v in values]
    while len(sums) > 1:
        sums = [sums[k] + sums[k + 1] for k in range(0, len(sums), 2)]
    return sums[0].astype(bf16)


def summed(keep, send, beside):
    half = added(keep, swap(send, 0, 1))
    steps = [(0, 1 << k) for k in range(1, lax.axis_size("gy").bit_length() - 1)]
    steps += [(1 << k, 0) for k in range(lax.axis_size("gx").bit_length() - 1)]
    while steps:
        if len(steps) >= 2 and steps[0][0] == 0 and steps[1][1] == 0:
            (_, cols), (rows, _) = steps[:2]
            half = added(
                half,
                swap(half, 0, cols),
                swap(half, rows, 0),
                swap(half, rows, cols),
            )
            steps = steps[2:]
        else:
            arrived = swap(half, *steps[0])
            steps = steps[1:]
            if not steps:
                arrived, beside = lax.optimization_barrier((arrived, beside))
            half = added(half, arrived)
    return half, swap(half, 0, 1), beside


def per_device(velocity, kernel_in, bias_in, kernel_mid, bias_mid, kernel_out, bias_out, cotangent):
    rows, cols = velocity.shape[1], velocity.shape[2]
    ny_total = lax.axis_size("gy") * cols
    cell_count = lax.axis_size("gx") * rows * ny_total
    deep = rows + 2 * halo
    height = deep
    width = -(-(cols + 2 * halo) // 128) * 128
    vmem = pl.BlockSpec(memory_space=pltpu.VMEM)
    params = pltpu.CompilerParams(vmem_limit_bytes=18 << 20)

    core = (lax.axis_index("gy") % 2).astype(jnp.int32).reshape(1)
    smem = pl.BlockSpec(memory_space=pltpu.SMEM)
    hbm = pl.BlockSpec(memory_space=pltpu.HBM)
    w_in, w_mid, w_mid_t, w_out_t, w_head, w_in_t, b_in, b_mid, b_head = pl.pallas_call(
        weights_kernel,
        out_shape=(
            jax.ShapeDtypeStruct((2 * hid, 12 * slot), bf16),
            jax.ShapeDtypeStruct((3, 2 * hid, 4 * hid), bf16),
            jax.ShapeDtypeStruct((3, 2 * hid, 4 * hid), bf16),
            jax.ShapeDtypeStruct((2 * hid, 12 * slot), bf16),
            jax.ShapeDtypeStruct((6 * slot, 4 * hid), bf16),
            jax.ShapeDtypeStruct((48, 4 * hid), bf16),
            jax.ShapeDtypeStruct((128, 128), f32),
            jax.ShapeDtypeStruct((128, 128), f32),
            jax.ShapeDtypeStruct((2 * slot, 128), f32),
        ),
        in_specs=[hbm] * 6,
        out_specs=(vmem,) * 9,
        scratch_shapes=[
            pltpu.VMEM((9, 2, hid), bf16),
            pltpu.VMEM((9, hid, hid), bf16),
            pltpu.VMEM((coef, 3, 3, hid), bf16),
            pltpu.VMEM((1, hid), f32),
            pltpu.VMEM((1, hid), f32),
            pltpu.VMEM((1, coef), f32),
            pltpu.SemaphoreType.DMA((6,)),
        ],
        compiler_params=params,
        name="weights",
    )(
        in_hbm(jnp.transpose(kernel_in, (2, 3, 1, 0)).reshape(9, 2, hid)),
        in_hbm(jnp.transpose(kernel_mid, (2, 3, 0, 1)).reshape(9, hid, hid)),
        in_hbm(jnp.transpose(kernel_out, (0, 2, 3, 1))),
        in_hbm(bias_in[None, :]),
        in_hbm(bias_mid[None, :]),
        in_hbm(bias_out[None, :]),
    )
    columns = lax.iota(jnp.int32, width) - halo + lax.axis_index("gy") * cols
    forcing = forcing_amp * jnp.sin(2.0 * math.pi * forcing_wave * columns.astype(f32) / ny_total)
    even = (lax.axis_index("gy") % 2 == 0).astype(jnp.int32).reshape(1)
    edge = jax.ShapeDtypeStruct((4, rows, halo), bf16)
    fields, far, near = pl.pallas_call(
        pack_kernel,
        out_shape=(jax.ShapeDtypeStruct((4, rows, cols), f32), edge, edge),
        in_specs=[smem, hbm, hbm],
        out_specs=(vmem,) * 3,
        scratch_shapes=[pltpu.SemaphoreType.DMA((2,))],
        compiler_params=params,
        name="pack",
    )(even, in_hbm(velocity), in_hbm(cotangent))
    wide = widened(fields, far, near, "gy", 2)
    maps = (w_in, w_mid, w_mid_t, w_out_t, b_in, b_mid)
    far, near = edges(wide, "gx", 1)
    near, maps = lax.optimization_barrier((near, maps))
    ext = widened(wide, far, near, "gx", 1)

    accs = (
        jax.ShapeDtypeStruct((3, 2 * hid, 4 * hid), f32),
        jax.ShapeDtypeStruct((2, 12 * slot, 2 * hid), f32),
        jax.ShapeDtypeStruct((2, 2 * hid, width), f32),
    )
    act_one, slope_one, grad_two, act_two_in, grad_one_in, *totals = pl.pallas_call(
        lambda *refs: inner_kernel(rows, cols, *refs),
        out_shape=(
            jax.ShapeDtypeStruct((3, (rows - 2) * hid, width), bf16),
            jax.ShapeDtypeStruct(((rows - 2) * hid, width), f32),
            jax.ShapeDtypeStruct((3, (rows - 4) * hid, width), bf16),
            jax.ShapeDtypeStruct(((rows - 4) * hid, width), bf16),
            jax.ShapeDtypeStruct(((rows - 6) * hid, width), bf16),
            *accs,
        ),
        in_specs=[vmem] * 7,
        out_specs=(vmem,) * 8,
        scratch_shapes=[
            pltpu.VMEM((4, rows, width), f32),
            pltpu.VMEM((width // 128, rows * slot, 128), f32),
            pltpu.VMEM((2, 3, rows * slot, width), bf16),
        ],
        compiler_params=params,
        name="inner",
    )(wide, *maps)

    keep, send, act_two_edge, grad_one_edge = pl.pallas_call(
        lambda *refs: outer_kernel(rows, cols, *refs),
        out_shape=(
            jax.ShapeDtypeStruct((hid // 2, 12 * hid), bf16),
            jax.ShapeDtypeStruct((hid // 2, 12 * hid), bf16),
            jax.ShapeDtypeStruct((2, halo * hid, width), bf16),
            jax.ShapeDtypeStruct((2, halo * hid, width), bf16),
        ),
        in_specs=[vmem] * 7 + [smem] + [vmem] * 7,
        out_specs=(vmem,) * 4,
        scratch_shapes=[
            pltpu.VMEM((2, hid // 2, 12 * hid), bf16),
            pltpu.VMEM((4, deep, width), f32),
            pltpu.VMEM((width // 128, deep * slot, 128), f32),
            pltpu.VMEM((2, 3, deep * slot, width), bf16),
            pltpu.VMEM((2, 3, halo * hid, width), bf16),
            pltpu.VMEM((2, halo * hid, width), f32),
            pltpu.VMEM((2, 3, halo * hid, width), bf16),
            *(pltpu.VMEM(acc.shape, f32) for acc in accs),
        ],
        compiler_params=params,
        name="outer",
    )(ext, *maps, core, act_one, slope_one, grad_two, grad_one_in, *totals)

    new_velocity, grad_velocity = pl.pallas_call(
        lambda *refs: advance_kernel(rows, cols, *refs),
        out_shape=(jax.ShapeDtypeStruct(velocity.shape, f32),) * 2,
        in_specs=[vmem] * 9,
        out_specs=(vmem,) * 2,
        scratch_shapes=[
            pltpu.VMEM((4, height, width), f32),
            pltpu.VMEM((width // 128, deep * slot, 128), f32),
            pltpu.VMEM((width // 128, deep * 8, 128), f32),
        ],
        compiler_params=params,
        name="advance",
    )(ext, forcing[None, :], w_head, b_head, w_in_t, act_two_in, act_two_edge, grad_one_in, grad_one_edge)

    mine, other, (new_velocity, grad_velocity) = summed(
        keep, send, (new_velocity, grad_velocity)
    )
    g_in, gb_in, g_mid, gb_mid, g_out, gb_out = pl.pallas_call(
        lambda *refs: finish_kernel(1.0 / math.sqrt(cell_count), *refs),
        out_shape=(
            jax.ShapeDtypeStruct((9, 2, hid), f32),
            jax.ShapeDtypeStruct((1, hid), f32),
            jax.ShapeDtypeStruct((9, hid, hid), f32),
            jax.ShapeDtypeStruct((1, hid), f32),
            jax.ShapeDtypeStruct((coef, 3, 3, hid), f32),
            jax.ShapeDtypeStruct((1, coef), f32),
        ),
        in_specs=[vmem] * 2 + [smem],
        out_specs=(vmem,) * 6,
        compiler_params=params,
        name="finish",
    )(mine, other, core)

    return (
        new_velocity,
        grad_velocity,
        jnp.transpose(g_in.reshape(3, 3, 2, hid), (3, 2, 0, 1)),
        gb_in.reshape(hid),
        jnp.transpose(g_mid.reshape(3, 3, hid, hid), (2, 3, 0, 1)),
        gb_mid.reshape(hid),
        jnp.transpose(g_out, (0, 3, 1, 2)),
        gb_out.reshape(coef),
    )


def solution(mesh):
    in_specs = (P("groups", "gx", "gy"), P(), P(), P(), P(), P(), P(), P("groups", "gx", "gy"))
    out_specs = (
        P("groups", "gx", "gy"),
        P("groups", "gx", "gy"),
        P("groups", None, None, None),
        P("groups"),
        P("groups", None, None, None),
        P("groups"),
        P("groups", None, None, None),
        P("groups"),
    )
    return jax.shard_map(
        per_device, mesh=mesh, in_specs=in_specs, out_specs=out_specs, check_vma=False
    )
```

```python
import math

import jax
import jax.numpy as jnp
from jax import lax
from jax.experimental import pallas as pl
from jax.experimental.pallas import tpu as pltpu
from jax.sharding import PartitionSpec as P

advection = 0.2
viscosity = 0.05
forcing_amp = 0.05
forcing_wave = 4
face_base = ((0.0, 0.5, 0.0, 0.0, 0.5, 0.0), (0.0, 0.0, 0.5, 0.5, 0.0, 0.0))
halo = 4
hid = 64
coef = 12
slot = 16
side = 2 * halo
pitch = 2 * side
left_of, right_of = halo - 1, side + halo
taps_x = [(a, b) for a in (0, 1) for b in (-1, 0, 1)]
taps_y = [(a, b) for a in (-1, 0, 1) for b in (0, 1)]
f32 = jnp.float32
bf16 = jnp.bfloat16


def shift(value, rows, cols):
    if rows:
        value = pltpu.roll(value, (-rows) % value.shape[-2], value.ndim - 2)
    if cols:
        value = pltpu.roll(value, (-cols) % value.shape[-1], value.ndim - 1)
    return value


def mm(lhs, rhs):
    return lax.dot_general(lhs, rhs, (((1,), (0,)), ((), ())), preferred_element_type=f32)


def mm_nt(lhs, rhs):
    return lax.dot_general(lhs, rhs, (((1,), (1,)), ((), ())), preferred_element_type=f32)


def sigma_of(linear):
    return 0.5 * jnp.tanh(0.5 * linear) + 0.5


def with_lane(value, at, column):
    tiles = [value[:, k : k + 128] for k in range(0, value.shape[1], 128)]
    lane = lax.broadcasted_iota(jnp.int32, (1, 128), 1)
    tiles[at // 128] = jnp.where(lane == at % 128, column, tiles[at // 128])
    return jnp.concatenate(tiles, axis=1)


def strip_column(strip, row, at, to):
    source = row * pitch + at
    tile = strip[:, source // 128 * 128 : source // 128 * 128 + 128]
    return pltpu.roll(tile, (to - source) % 128, 1) if (to - source) % 128 else tile


def beside(low, middle, high, before, after):
    return (
        with_lane(shift(low, 0, -1), 0, before),
        middle,
        with_lane(shift(high, 0, 1), high.shape[1] - 1, after),
    )


def strip_taps(strip, columns=(-1, 0, 1)):
    return jnp.concatenate(
        [shift(strip, 0, a * pitch + b) for b in columns for a in (-1, 0, 1)], axis=0
    )


def strip_of(planes, rows, cols):
    lane = lax.broadcasted_iota(jnp.int32, (1, 128), 1)
    per_tile = 128 // pitch
    tiles = []
    for start in range(0, rows, per_tile):
        tile = jnp.zeros((slot, 128), f32)
        for k in range(min(per_tile, rows - start)):
            at = slice((start + k) * slot, (start + k + 1) * slot)
            pair = jnp.where(lane < side, planes[0, at, :], pltpu.roll(planes[cols // 128, at, :], side, 1))
            pair = pltpu.roll(pair, k * pitch, 1) if k else pair
            tile = jnp.where((lane >= k * pitch) & (lane < (k + 1) * pitch), pair, tile)
        tiles.append(tile)
    return jnp.concatenate(tiles, axis=1).astype(bf16)


class Rows:
    def __init__(self, size, *pieces):
        self.size = size
        self.pieces = pieces

    def get(self, lo, hi, lead=()):
        parts = []
        for start, stop, ref in self.pieces:
            first, last = max(lo, start), min(hi, stop)
            if first < last:
                rows = slice((first - start) * self.size, (last - start) * self.size)
                parts.append((first, ref[(*lead, rows, slice(None))]))
        parts = [part for _, part in sorted(parts, key=lambda item: item[0])]
        return parts[0] if len(parts) == 1 else jnp.concatenate(parts, axis=0)

    def put(self, lo, value, lead=()):
        for start, stop, ref in self.pieces:
            if start <= lo < stop:
                rows = slice((lo - start) * self.size, (lo - start) * self.size + value.shape[0])
                ref[(*lead, rows, slice(None))] = value

    def put_shifted(self, lo, value, strip, first):
        value = value.astype(bf16)
        ends = [
            jnp.concatenate([strip_column(strip, lo + k - first, at, to) for k in range(2)], axis=0)
            for at, to in ((left_of, 0), (right_of, value.shape[1] - 1))
        ]
        for b, shifted in enumerate(beside(value, value, value, *ends)):
            self.put(lo, shifted, (b,))

    def put_cut(self, lo, value, lead):
        value = value.astype(bf16)
        cols = self.pieces[0][2].shape[-1]
        for b in range(3):
            self.put(lo, shift(value, 0, halo - 1 + b)[:, :cols], (*lead, b))

    def window(self, lo, hi, lead=()):
        return jnp.concatenate([self.get(lo, hi, (*lead, b)) for b in range(3)], axis=0)


def put_plane(planes, k, stride, value):
    for j in range(planes.shape[0]):
        planes[j, pl.ds(k, value.shape[0], stride=stride), :] = value[:, 128 * j : 128 * j + 128]


def take_plane(planes, k, count, stride):
    tiles = [planes[j, pl.ds(k, count, stride=stride), :] for j in range(planes.shape[0])]
    return jnp.concatenate(tiles, axis=1)


def take_rows(planes, at, size):
    return jnp.concatenate([planes[j, at : at + size, :] for j in range(planes.shape[0])], axis=1)


def put_rows(planes, at, value):
    for j in range(planes.shape[0]):
        planes[j, at : at + value.shape[0], :] = value[:, 128 * j : 128 * j + 128]


def faces(w0, w1):
    normal_x = 0.5 * (w0 + shift(w0, 1, 0))
    normal_y = 0.5 * (w1 + shift(w1, 0, 1))
    return normal_x, normal_y


def shifted_fields(w):
    table = {}
    for b in (-1, 0, 1):
        col = shift(w, 0, b)
        for a in (-1, 0, 1):
            table[a, b] = shift(col, a, 0)
    return table


def lane_sums(total):
    lanes = total.shape[1]
    part = total[:, :128]
    for k in range(1, lanes // 128):
        part = part + total[:, 128 * k : 128 * k + 128]
    return jnp.sum(part.T, axis=0, keepdims=True)


def prepare(first, rows, cols, ext_ref, stage, planes, state_in, state_rows, head_rows):
    count = ext_ref.shape[1]
    height, width = stage.shape[1], stage.shape[2]
    stage[...] = jnp.zeros(stage.shape, f32)
    stage[:, 0:count, 0 : cols + 2 * halo] = ext_ref[...]
    w0, w1, c0, c1 = stage[0], stage[1], stage[2], stage[3]

    planes[...] = jnp.zeros(planes.shape, f32)
    put_plane(planes, 0, slot, w0)
    put_plane(planes, 1, slot, w1)
    for r in state_rows:
        state_in.put_cut(r, take_rows(planes, (r - first) * slot, 2 * slot), (0,))
    strips = [strip_of(planes, count, cols)]

    normal_x, normal_y = faces(w0, w1)
    t0, t1 = shifted_fields(w0), shifted_fields(w1)
    fx0 = -advection * (c0 - shift(c0, 1, 0)) * normal_x
    fx1 = -advection * (c1 - shift(c1, 1, 0)) * normal_x
    fy0 = -advection * (c0 - shift(c0, 0, 1)) * normal_y
    fy1 = -advection * (c1 - shift(c1, 0, 1)) * normal_y
    lane = lax.broadcasted_iota(jnp.int32, (height, width), 1)
    row_id = lax.broadcasted_iota(jnp.int32, (height, width), 0) + first
    own = (lane >= halo) & (lane < halo + cols) & (row_id >= halo) & (row_id < halo + rows)
    sums = []
    for at, taps, g0, g1 in ((0, taps_x, fx0, fx1), (6, taps_y, fy0, fy1)):
        raw = [g0 * t0[tap] + g1 * t1[tap] for tap in taps]
        mean = sum(raw[1:], raw[0]) * (1.0 / 6.0)
        for k in range(6):
            value = raw[k] - mean
            put_plane(planes, at + k, slot, value)
            sums.append(jnp.sum(jnp.where(own, value, 0.0), axis=0, keepdims=True))
    for r in head_rows:
        state_in.put_cut(r, take_rows(planes, (r - first) * slot, 2 * slot), (1,))
    strips.append(strip_of(planes, count, cols))
    return sums, strips


class Strips:
    def __init__(self, refs, state, head):
        self.refs, self.state, self.head = refs, state, head

    def spread(self, k):
        ref = self.refs[k]
        if k in (0, 3):
            parts = [ref[:hid, 4 * slot * b : (4 * b + 3) * slot] for b in range(3)]
        else:
            parts = [ref[b, :hid, : 3 * hid] for b in range(3)]
        return jnp.concatenate(parts, axis=1)

    def first(self):
        linear = mm(self.spread(0), strip_taps(self.state)) + self.refs[4][:hid, 0:1]
        sigma = sigma_of(linear)
        act = linear * sigma
        self.slope = sigma + act * (1.0 - sigma)
        self.act_one = act.astype(bf16)

    def second(self):
        linear = mm(self.spread(1), strip_taps(self.act_one)) + self.refs[5][:hid, 0:1]
        sigma = sigma_of(linear)
        act = linear * sigma
        grad = mm(self.spread(3), strip_taps(self.head)) * (sigma + act * (1.0 - sigma))
        self.act_two = act.astype(bf16)
        self.grad_two = grad.astype(bf16)

    def back(self):
        grad = mm(self.spread(2), strip_taps(self.grad_two)) * self.slope
        self.grad_one = grad.astype(bf16)


def layers(
    rows,
    groups,
    refs,
    strips,
    with_back,
    first,
    state_in,
    act_one,
    slope_one,
    grad_two,
    act_two,
    grad_one,
    acc_mid,
    acc_small,
    bias_acc,
):
    w_in_ref, w_mid_ref, w_mid_t_ref, w_out_t_ref, b_in_ref, b_mid_ref = refs
    groups_one, groups_two, groups_back, groups_in = groups

    w_in = w_in_ref[...]
    b_in = b_in_ref[:, 0:1]
    strips.first()
    for r in groups_one:
        linear = mm(w_in, state_in.window(r - 1, r + 3, (0,))) + b_in
        sigma = sigma_of(linear)
        act = linear * sigma
        act_one.put_shifted(r, act, strips.act_one, first)
        slope_one.put(r, sigma + act * (1.0 - sigma))
        if r == groups_one[0]:
            strips.second()

    b_mid = b_mid_ref[:, 0:1]
    w_out_t = w_out_t_ref[...]
    w_mid = jnp.concatenate([w_mid_ref[b] for b in range(3)], axis=1)
    w_mid_t = jnp.concatenate([w_mid_t_ref[b] for b in range(3)], axis=1)
    held = []
    for r in groups_two:
        window = [act_one.get(r - 1, r + 3, (b,)) for b in range(3)]
        linear = mm(w_mid, jnp.concatenate(window, axis=0)) + b_mid
        sigma = sigma_of(linear)
        act = linear * sigma
        act_short = act.astype(bf16)
        act_two.put(r, act_short)
        fed = state_in.window(r - 1, r + 3, (1,))
        grad = mm(w_out_t, fed) * (sigma + act * (1.0 - sigma))
        grad_two.put_shifted(r, grad, strips.grad_two, first)
        if with_back and r == groups_two[0]:
            strips.back()
        if halo <= r < halo + rows:
            bias_acc[0] += grad
            held.append((grad.astype(bf16), window, fed, act_short))
        if held and (len(held) == 2 or r == groups_two[-1]):
            grads, windows, feds, acts = zip(*held)
            held = []
            grads = jnp.concatenate(grads, axis=1)
            for b in range(3):
                acc_mid[b] += mm_nt(grads, jnp.concatenate([w[b] for w in windows], axis=1))
            acc_small[0] += mm_nt(jnp.concatenate(feds, axis=1), jnp.concatenate(acts, axis=1))

    for r in groups_back:
        grad = mm(w_mid_t, grad_two.window(r - 1, r + 3)) * slope_one.get(r, r + 2)
        grad_one.put(r, grad.astype(bf16))
        if r < halo:
            bias_acc[1, hid:, :] += grad[hid:, :]
        elif r + 2 > halo + rows:
            bias_acc[1, :hid, :] += grad[:hid, :]
        else:
            bias_acc[1] += grad
    for r in groups_in:
        acc_small[1] += mm_nt(state_in.window(r - 1, r + 3, (0,)), grad_one.get(r, r + 2))


def inner_kernel(rows, cols, ext_ref, *refs):
    weight_refs, refs = refs[:6], refs[6:]
    act_one, slope_one, grad_two, act_two, grad_one, acc_mid, acc_small, bias_acc, *refs = refs
    stage, planes, state_in = refs
    low, high = halo, halo + rows
    state_in = Rows(slot, (low, high, state_in))
    acc_mid[...] = jnp.zeros(acc_mid.shape, f32)
    acc_small[...] = jnp.zeros(acc_small.shape, f32)
    bias_acc[...] = jnp.zeros(bias_acc.shape, f32)
    pairs = range(low, high, 2)
    _, strips = prepare(low, rows, cols, ext_ref, stage, planes, state_in, pairs, pairs)
    groups = [range(low + k, high - k, 2) for k in (1, 2, 3, 4)]
    layers(
        rows,
        groups,
        weight_refs,
        Strips(weight_refs, *strips),
        False,
        low,
        state_in,
        Rows(hid, (low + 1, high - 1, act_one)),
        Rows(hid, (low + 1, high - 1, slope_one)),
        Rows(hid, (low + 2, high - 2, grad_two)),
        Rows(hid, (low + 2, high - 2, act_two)),
        Rows(hid, (low + 3, high - 3, grad_one)),
        acc_mid,
        acc_small,
        bias_acc,
    )


def split_rows(size, first, low, high, last, lower_ref, inner_ref, upper_ref):
    return Rows(size, (first, low, lower_ref), (low, high, inner_ref), (high, last, upper_ref))


def outer_kernel(rows, cols, ext_ref, *refs):
    weight_refs, core_ref, refs = refs[:6], refs[6], refs[7:]
    act_one_in, slope_one_in, grad_two_in, grad_one_in, acc_mid_in, acc_small_in, bias_in, *refs = refs
    keep_ref, send_ref, act_two, grad_one, act_two_strip, grad_one_strip, *refs = refs
    pay, stage, planes, state_in, act_one, slope_one, grad_two, acc_mid, acc_small, bias_acc = refs
    low, high, deep = halo, halo + rows, rows + 2 * halo
    acc_mid[...] = acc_mid_in[...]
    acc_small[...] = acc_small_in[...]
    bias_acc[...] = bias_in[...]
    state_in = Rows(slot, (0, deep, state_in))
    state_rows = [r for r in range(0, deep, 2) if r < low + 6 or r + 2 > high - 6]
    head_rows = [r for r in range(0, deep, 2) if r < low + 4 or r + 2 > high - 4]
    sums, strips = prepare(0, rows, cols, ext_ref, stage, planes, state_in, state_rows, head_rows)
    bias_out = jnp.concatenate(sums + [jnp.zeros((128 - coef, stage.shape[2]), f32)], axis=0)
    groups = [
        [*range(k, low + k, 2), *range(high - k, deep - k, 2)] for k in (1, 2, 3)
    ]
    groups.append([low, low + 2, high - 4, high - 2])

    def both(k, edge, inner):
        edges = [edge.at[i] for i in range(2)]
        return split_rows(hid, k, low + k, high - k, deep - k, edges[0], inner, edges[1])

    strips = Strips(weight_refs, *strips)
    layers(
        rows,
        groups,
        weight_refs,
        strips,
        True,
        0,
        state_in,
        both(1, act_one, act_one_in),
        both(1, slope_one, slope_one_in),
        both(2, grad_two, grad_two_in),
        Rows(hid, (2, low + 2, act_two.at[0]), (high - 2, deep - 2, act_two.at[1])),
        both(3, grad_one, grad_one_in),
        acc_mid,
        acc_small,
        bias_acc,
    )

    act_two_strip[...] = strips.act_two
    grad_one_strip[...] = strips.grad_one

    for b in range(3):
        total = acc_mid[b, :hid, : 3 * hid] + acc_mid[b, hid:, hid:]
        for a in range(3):
            t = 3 * a + b
            block = total[:, a * hid : (a + 1) * hid].astype(bf16)
            for h in range(2):
                pay[h, :, t * hid : (t + 1) * hid] = block[32 * h : 32 * h + 32]
    slots = []
    pieces = []
    for a in range(3):
        for b in range(3):
            at = (2 - b) * 4 * slot + (2 - a) * slot
            slots.append(
                acc_small[0, at : at + slot, :hid] + acc_small[0, at + slot : at + 2 * slot, hid:]
            )
            at = b * 4 * slot + a * slot
            pieces.append(
                acc_small[1, at : at + 2, :hid] + acc_small[1, at + slot : at + slot + 2, hid:]
            )
    sums_in, sums_mid = lane_sums(bias_acc[1]), lane_sums(bias_acc[0])
    pieces.append(sums_in[:, :hid] + sums_in[:, hid:])
    pieces.append(sums_mid[:, :hid] + sums_mid[:, hid:])
    pieces.append(lane_sums(bias_out)[:, :hid])
    pieces.append(jnp.zeros((11, hid), f32))
    rest = jnp.concatenate(pieces, axis=0)
    slots += [rest[:slot], rest[slot:], jnp.zeros((slot, hid), f32)]
    for h in range(2):
        for q in range(3):
            at = 6 * h + 2 * q
            block = jnp.concatenate(slots[at : at + 2], axis=0).astype(bf16)
            pay[h, :, (9 + q) * hid : (10 + q) * hid] = block
    core = core_ref[0]
    keep_ref[...] = pay[core]
    send_ref[...] = pay[1 - core]


def advance_kernel(
    rows,
    cols,
    ext_ref,
    forcing_ref,
    w_head_ref,
    b_head_ref,
    w_in_t_ref,
    act_two_in,
    act_two_edge,
    grad_one_in,
    grad_one_edge,
    act_two_strip,
    grad_one_strip,
    new_ref,
    grad_ref,
    stage,
    head,
    back,
):
    low, high, deep = halo, halo + rows, rows + 2 * halo
    act_two, grad_one = (
        split_rows(hid, k, low + k, high - k, deep - k, edge.at[0], inner, edge.at[1])
        for k, inner, edge in ((2, act_two_in, act_two_edge), (3, grad_one_in, grad_one_edge))
    )
    stage[...] = jnp.zeros(stage.shape, f32)
    stage[:, 0:deep, 0 : cols + 2 * halo] = ext_ref[...]
    w0, w1, c0, c1 = stage[0], stage[1], stage[2], stage[3]
    head[...] = jnp.zeros(head.shape, f32)
    back[...] = jnp.zeros(back.shape, f32)
    b_head = b_head_ref[:, 0:1]
    width = stage.shape[2]
    blank = jnp.zeros((2 * slot, width - cols), f32)

    def weighed(weight_ref, size, strip_ref):
        weight = weight_ref[...]
        alone = [weight[2 * size * b : (2 * b + 1) * size, : 3 * hid] for b in range(3)]
        taps = strip_taps(strip_ref[...], (0,))
        ends = mm(jnp.concatenate(alone, axis=0), taps)
        ends = [ends[b * size : (b + 1) * size] for b in range(3)]

        def pair(field, r):
            part = mm(weight, field.get(r - 1, r + 3))
            part = [part[2 * size * b : 2 * size * (b + 1)] for b in range(3)]
            around = [
                jnp.concatenate([strip_column(end, r + k, at, to) for k in range(2)], axis=0)
                for end, at, to in ((ends[0], left_of, 0), (ends[2], right_of, cols - 1))
            ]
            low, middle, high = beside(*part, *around)
            return low + middle + high

        return ends, pair

    ends, pair = weighed(w_head_ref, slot, act_two_strip)
    head_strip = b_head[:slot] + ends[1] + shift(ends[0], 0, -1) + shift(ends[2], 0, 1)
    for r in range(3, deep - 3, 2):
        out = jnp.concatenate([pair(act_two, r) + b_head, blank], axis=1)
        out = pltpu.roll(out, halo, 1)
        for at, to in ((left_of, halo - 1), (right_of, halo + cols)):
            column = [strip_column(head_strip, r + k, at, to) for k in range(2)]
            out = with_lane(out, to, jnp.concatenate(column, axis=0))
        put_rows(head, r * slot, out)
    _, pair = weighed(w_in_t_ref, 8, grad_one_strip)
    for r in range(halo, halo + rows, 2):
        out = jnp.concatenate([pair(grad_one, r), blank[:16]], axis=1)
        put_rows(back, r * 8, pltpu.roll(out, halo, 1))

    coefs = [take_plane(head, k, deep, slot) for k in range(coef)]
    mean_x = sum(coefs[1:6], coefs[0]) * (1.0 / 6.0)
    mean_y = sum(coefs[7:12], coefs[6]) * (1.0 / 6.0)
    sx = [coefs[k] - mean_x + face_base[0][k] for k in range(6)]
    sy = [coefs[6 + k] - mean_y + face_base[1][k] for k in range(6)]
    normal_x, normal_y = faces(w0, w1)
    grad_x = [-advection * (c - shift(c, 1, 0)) for c in (c0, c1)]
    grad_y = [-advection * (c - shift(c, 0, 1)) for c in (c0, c1)]
    normal_grad_x, normal_grad_y = 0.0, 0.0
    for c, (w, cot) in enumerate(((w0, c0), (w1, c1))):
        table = shifted_fields(w)
        face_x = sum(s * table[tap] for s, tap in zip(sx, taps_x))
        face_y = sum(s * table[tap] for s, tap in zip(sy, taps_y))
        flux_x = normal_x * face_x
        flux_y = normal_y * face_y
        normal_grad_x = normal_grad_x + grad_x[c] * face_x
        normal_grad_y = normal_grad_y + grad_y[c] * face_y
        around = table[1, 0] + table[-1, 0] + table[0, 1] + table[0, -1]
        new = (
            w
            - advection
            * (flux_x - shift(flux_x, -1, 0) + flux_y - shift(flux_y, 0, -1))
            + viscosity * (around - 4.0 * w)
        )
        if c == 0:
            new = new + forcing_ref[...]
        new_ref[c] = new[halo : halo + rows, halo : halo + cols]
    for c, cot in enumerate((c0, c1)):
        around = shift(cot, 1, 0) + shift(cot, -1, 0) + shift(cot, 0, 1) + shift(cot, 0, -1)
        total = cot + viscosity * (around - 4.0 * cot)
        flow_x = normal_x * grad_x[c]
        flow_y = normal_y * grad_y[c]
        by_col = {-1: {}, 0: {}, 1: {}}
        for s, (a, b) in zip(sx, taps_x):
            by_col[b][a] = by_col[b].get(a, 0.0) + flow_x * s
        for s, (a, b) in zip(sy, taps_y):
            by_col[b][a] = by_col[b].get(a, 0.0) + flow_y * s
        for b, column in by_col.items():
            part = sum(shift(value, -a, 0) for a, value in column.items())
            total = total + shift(part, 0, -b)
        if c == 0:
            total = total + 0.5 * (normal_grad_x + shift(normal_grad_x, -1, 0))
        else:
            total = total + 0.5 * (normal_grad_y + shift(normal_grad_y, 0, -1))
        total = total + take_plane(back, c, deep, 8)
        grad_ref[c] = total[halo : halo + rows, halo : halo + cols]


def finish_kernel(
    scale, mine_ref, other_ref, core_ref, in_ref, b_in_ref, mid_ref, b_mid_ref, out_ref, b_out_ref
):
    mine = mine_ref[...].astype(f32) * scale
    other = other_ref[...].astype(f32) * scale
    first = core_ref[0] == 0
    halves = (jnp.where(first, mine, other), jnp.where(first, other, mine))
    slots = []
    for h, half in enumerate(halves):
        for t in range(9):
            mid_ref[t, 32 * h : 32 * h + 32, :] = half[:, t * hid : (t + 1) * hid]
        for q in range(3):
            block = half[:, (9 + q) * hid : (10 + q) * hid]
            slots += [block[:slot], block[slot:]]
    for a in range(3):
        for b in range(3):
            out_ref[:, a, b, :] = slots[3 * a + b][:coef]
    for t in range(9):
        in_ref[t] = slots[9 + t // 8][2 * t % 16 : 2 * t % 16 + 2]
    b_in_ref[...] = slots[10][2:3]
    b_mid_ref[...] = slots[10][3:4]
    b_out_ref[...] = slots[10][4:5, :coef]


def in_hbm(array):
    return pltpu.with_memory_space_constraint(array, pltpu.HBM)


def fetched(sources, targets, sems):
    copies = [
        pltpu.make_async_copy(source, target, sems.at[k])
        for k, (source, target) in enumerate(zip(sources, targets))
    ]
    for copy in copies:
        copy.start()
    for copy in copies:
        copy.wait()


def pack_kernel(even_ref, velocity_ref, cotangent_ref, fields_ref, far_ref, near_ref, sems):
    cols = fields_ref.shape[2]
    fetched(
        (velocity_ref, cotangent_ref), (fields_ref.at[0:2], fields_ref.at[2:4]), sems
    )
    first = fields_ref[:, :, 0:halo].astype(bf16)
    last = fields_ref[:, :, cols - halo : cols].astype(bf16)
    even = even_ref[0] == 1
    far_ref[...] = jnp.where(even, first, last)
    near_ref[...] = jnp.where(even, last, first)


def weights_kernel(*refs):
    sources, refs = refs[:6], refs[6:]
    outs, (*inputs, sems) = refs[:9], refs[9:]
    fetched(sources, inputs, sems)
    k_in_ref, k_mid_ref, k_out_ref, b_in_ref, b_mid_ref, b_out_ref = inputs
    w_in_ref, w_mid_ref, w_mid_t_ref, w_out_t_ref, w_head_ref, w_in_t_ref, *outs = outs
    c_in_ref, c_mid_ref, c_head_ref = outs

    def band(block, upper):
        none = jnp.zeros(block[0].shape, f32)
        return jnp.concatenate([none, *block] if upper else [*block, none], axis=1)

    def tall(block, rows):
        return jnp.concatenate(
            [block, jnp.zeros((rows - block.shape[0], block.shape[1]), f32)], axis=0
        )

    k_mid = [k_mid_ref[t].astype(f32) for t in range(9)]
    k_mid_t = [k.T for k in k_mid]
    k_out = [k_out_ref[:, t // 3, t % 3, :].astype(f32) for t in range(9)]
    k_in = [k_in_ref[t].astype(f32) for t in range(9)]
    in_rows = []
    out_rows = []
    zero = jnp.zeros((slot, hid), f32)
    for b in range(3):
        forward = [3 * a + b for a in range(3)]
        backward = [8 - t for t in forward]
        for u in range(2):
            at = slice(u * hid, (u + 1) * hid)
            w_mid_ref[b, at, :] = band([k_mid[t] for t in forward], u).astype(bf16)
            w_mid_t_ref[b, at, :] = band([k_mid_t[t] for t in backward], u).astype(bf16)
        head = [band([tall(k_out[t], slot) for t in forward], u) for u in range(2)]
        w_head_ref[2 * slot * b : 2 * slot * (b + 1), :] = jnp.concatenate(head, 0).astype(bf16)
        back = [band([tall(k_in[t], 8) for t in backward], u) for u in range(2)]
        w_in_t_ref[16 * b : 16 * (b + 1), :] = jnp.concatenate(back, 0).astype(bf16)
        for rows, blocks in (
            (in_rows, [tall(k_in[t], slot) for t in forward]),
            (out_rows, [tall(k_out[t], slot) for t in backward]),
        ):
            lower = jnp.concatenate(blocks + [zero], axis=0)
            upper = jnp.concatenate([zero] + blocks, axis=0)
            rows.append(jnp.concatenate([lower, upper], axis=1))
    w_in_ref[...] = jnp.concatenate(in_rows, axis=0).T.astype(bf16)
    w_out_t_ref[...] = jnp.concatenate(out_rows, axis=0).T.astype(bf16)
    for ref, bias in ((c_in_ref, b_in_ref[...]), (c_mid_ref, b_mid_ref[...])):
        ref[...] = jnp.broadcast_to(jnp.concatenate([bias, bias], axis=1), (128, 128)).T
    bias = jnp.concatenate([b_out_ref[...], jnp.zeros((1, slot - coef), f32)], axis=1)
    bias = jnp.concatenate([bias, bias, jnp.zeros((1, 128 - 2 * slot), f32)], axis=1)
    c_head_ref[...] = jnp.broadcast_to(bias, (128, 128)).T[: 2 * slot]


def edges(fields, axis, dim):
    size = fields.shape[dim]
    even = lax.axis_index(axis) % 2 == 0
    first = lax.slice_in_dim(fields, 0, halo, axis=dim).astype(bf16)
    last = lax.slice_in_dim(fields, size - halo, size, axis=dim).astype(bf16)
    return jnp.where(even, first, last), jnp.where(even, last, first)


def widened(fields, far, near, axis, dim):
    count = lax.axis_size(axis)
    even = lax.axis_index(axis) % 2 == 0
    far_pairs = [(i, (i + 1 if i % 2 else i - 1) % count) for i in range(count)]
    far = lax.ppermute(far, axis, far_pairs)
    near = lax.ppermute(near, axis, [(i, i ^ 1) for i in range(count)])
    low = jnp.where(even, far, near).astype(f32)
    high = jnp.where(even, near, far).astype(f32)
    return jnp.concatenate([low, fields, high], axis=dim)


def swap(value, rows, cols):
    height, width = lax.axis_size("gx"), lax.axis_size("gy")
    pairs = [
        (i * width + j, (i ^ rows) * width + (j ^ cols)) for i in range(height) for j in range(width)
    ]
    return lax.ppermute(value, ("gx", "gy"), pairs)


def added(*values):
    sums = [v.astype(f32) for v in values]
    while len(sums) > 1:
        sums = [sums[k] + sums[k + 1] for k in range(0, len(sums), 2)]
    return sums[0].astype(bf16)


def summed(keep, send, beside):
    half = added(keep, swap(send, 0, 1))
    steps = [(0, 1 << k) for k in range(1, lax.axis_size("gy").bit_length() - 1)]
    steps += [(1 << k, 0) for k in range(lax.axis_size("gx").bit_length() - 1)]
    while steps:
        if len(steps) >= 2 and steps[0][0] == 0 and steps[1][1] == 0:
            (_, cols), (rows, _) = steps[:2]
            half = added(
                half,
                swap(half, 0, cols),
                swap(half, rows, 0),
                swap(half, rows, cols),
            )
            steps = steps[2:]
        else:
            arrived = swap(half, *steps[0])
            steps = steps[1:]
            if not steps:
                arrived, beside = lax.optimization_barrier((arrived, beside))
            half = added(half, arrived)
    return half, swap(half, 0, 1), beside


def per_device(velocity, kernel_in, bias_in, kernel_mid, bias_mid, kernel_out, bias_out, cotangent):
    rows, cols = velocity.shape[1], velocity.shape[2]
    ny_total = lax.axis_size("gy") * cols
    cell_count = lax.axis_size("gx") * rows * ny_total
    deep = rows + 2 * halo
    width = -(-(cols + 2 * halo) // 128) * 128
    vmem = pl.BlockSpec(memory_space=pltpu.VMEM)
    params = pltpu.CompilerParams(vmem_limit_bytes=18 << 20)

    core = (lax.axis_index("gy") % 2).astype(jnp.int32).reshape(1)
    smem = pl.BlockSpec(memory_space=pltpu.SMEM)
    hbm = pl.BlockSpec(memory_space=pltpu.HBM)
    w_in, w_mid, w_mid_t, w_out_t, w_head, w_in_t, b_in, b_mid, b_head = pl.pallas_call(
        weights_kernel,
        out_shape=(
            jax.ShapeDtypeStruct((2 * hid, 12 * slot), bf16),
            jax.ShapeDtypeStruct((3, 2 * hid, 4 * hid), bf16),
            jax.ShapeDtypeStruct((3, 2 * hid, 4 * hid), bf16),
            jax.ShapeDtypeStruct((2 * hid, 12 * slot), bf16),
            jax.ShapeDtypeStruct((6 * slot, 4 * hid), bf16),
            jax.ShapeDtypeStruct((48, 4 * hid), bf16),
            jax.ShapeDtypeStruct((128, 128), f32),
            jax.ShapeDtypeStruct((128, 128), f32),
            jax.ShapeDtypeStruct((2 * slot, 128), f32),
        ),
        in_specs=[hbm] * 6,
        out_specs=(vmem,) * 9,
        scratch_shapes=[
            pltpu.VMEM((9, 2, hid), bf16),
            pltpu.VMEM((9, hid, hid), bf16),
            pltpu.VMEM((coef, 3, 3, hid), bf16),
            pltpu.VMEM((1, hid), f32),
            pltpu.VMEM((1, hid), f32),
            pltpu.VMEM((1, coef), f32),
            pltpu.SemaphoreType.DMA((6,)),
        ],
        compiler_params=params,
        name="weights",
    )(
        in_hbm(jnp.transpose(kernel_in, (2, 3, 1, 0)).reshape(9, 2, hid)),
        in_hbm(jnp.transpose(kernel_mid, (2, 3, 0, 1)).reshape(9, hid, hid)),
        in_hbm(jnp.transpose(kernel_out, (0, 2, 3, 1))),
        in_hbm(bias_in[None, :]),
        in_hbm(bias_mid[None, :]),
        in_hbm(bias_out[None, :]),
    )
    columns = lax.iota(jnp.int32, width) - halo + lax.axis_index("gy") * cols
    forcing = forcing_amp * jnp.sin(2.0 * math.pi * forcing_wave * columns.astype(f32) / ny_total)
    even = (lax.axis_index("gy") % 2 == 0).astype(jnp.int32).reshape(1)
    edge = jax.ShapeDtypeStruct((4, rows, halo), bf16)
    fields, far, near = pl.pallas_call(
        pack_kernel,
        out_shape=(jax.ShapeDtypeStruct((4, rows, cols), f32), edge, edge),
        in_specs=[smem, hbm, hbm],
        out_specs=(vmem,) * 3,
        scratch_shapes=[pltpu.SemaphoreType.DMA((2,))],
        compiler_params=params,
        name="pack",
    )(even, in_hbm(velocity), in_hbm(cotangent))
    wide = widened(fields, far, near, "gy", 2)
    maps = (w_in, w_mid, w_mid_t, w_out_t, b_in, b_mid)
    far, near = edges(wide, "gx", 1)
    near, maps = lax.optimization_barrier((near, maps))
    ext = widened(wide, far, near, "gx", 1)

    accs = (
        jax.ShapeDtypeStruct((3, 2 * hid, 4 * hid), f32),
        jax.ShapeDtypeStruct((2, 12 * slot, 2 * hid), f32),
        jax.ShapeDtypeStruct((2, 2 * hid, cols), f32),
    )
    strip = jax.ShapeDtypeStruct((hid, deep * pitch), bf16)
    act_one, slope_one, grad_two, act_two_in, grad_one_in, *totals = pl.pallas_call(
        lambda *refs: inner_kernel(rows, cols, *refs),
        out_shape=(
            jax.ShapeDtypeStruct((3, (rows - 2) * hid, cols), bf16),
            jax.ShapeDtypeStruct(((rows - 2) * hid, cols), f32),
            jax.ShapeDtypeStruct((3, (rows - 4) * hid, cols), bf16),
            jax.ShapeDtypeStruct(((rows - 4) * hid, cols), bf16),
            jax.ShapeDtypeStruct(((rows - 6) * hid, cols), bf16),
            *accs,
        ),
        in_specs=[vmem] * 7,
        out_specs=(vmem,) * 8,
        scratch_shapes=[
            pltpu.VMEM((4, rows, width), f32),
            pltpu.VMEM((width // 128, rows * slot, 128), f32),
            pltpu.VMEM((2, 3, rows * slot, cols), bf16),
        ],
        compiler_params=params,
        name="inner",
    )(wide, *maps)

    keep, send, act_two_edge, grad_one_edge, *strips = pl.pallas_call(
        lambda *refs: outer_kernel(rows, cols, *refs),
        out_shape=(
            jax.ShapeDtypeStruct((hid // 2, 12 * hid), bf16),
            jax.ShapeDtypeStruct((hid // 2, 12 * hid), bf16),
            jax.ShapeDtypeStruct((2, halo * hid, cols), bf16),
            jax.ShapeDtypeStruct((2, halo * hid, cols), bf16),
            strip,
            strip,
        ),
        in_specs=[vmem] * 7 + [smem] + [vmem] * 7,
        out_specs=(vmem,) * 6,
        scratch_shapes=[
            pltpu.VMEM((2, hid // 2, 12 * hid), bf16),
            pltpu.VMEM((4, deep, width), f32),
            pltpu.VMEM((width // 128, deep * slot, 128), f32),
            pltpu.VMEM((2, 3, deep * slot, cols), bf16),
            pltpu.VMEM((2, 3, halo * hid, cols), bf16),
            pltpu.VMEM((2, halo * hid, cols), f32),
            pltpu.VMEM((2, 3, halo * hid, cols), bf16),
            *(pltpu.VMEM(acc.shape, f32) for acc in accs),
        ],
        compiler_params=params,
        name="outer",
    )(ext, *maps, core, act_one, slope_one, grad_two, grad_one_in, *totals)

    new_velocity, grad_velocity = pl.pallas_call(
        lambda *refs: advance_kernel(rows, cols, *refs),
        out_shape=(jax.ShapeDtypeStruct(velocity.shape, f32),) * 2,
        in_specs=[vmem] * 11,
        out_specs=(vmem,) * 2,
        scratch_shapes=[
            pltpu.VMEM((4, deep, width), f32),
            pltpu.VMEM((width // 128, deep * slot, 128), f32),
            pltpu.VMEM((width // 128, deep * 8, 128), f32),
        ],
        compiler_params=params,
        name="advance",
    )(ext, forcing[None, :], w_head, b_head, w_in_t, act_two_in, act_two_edge, grad_one_in, grad_one_edge, *strips)

    mine, other, (new_velocity, grad_velocity) = summed(
        keep, send, (new_velocity, grad_velocity)
    )
    g_in, gb_in, g_mid, gb_mid, g_out, gb_out = pl.pallas_call(
        lambda *refs: finish_kernel(1.0 / math.sqrt(cell_count), *refs),
        out_shape=(
            jax.ShapeDtypeStruct((9, 2, hid), f32),
            jax.ShapeDtypeStruct((1, hid), f32),
            jax.ShapeDtypeStruct((9, hid, hid), f32),
            jax.ShapeDtypeStruct((1, hid), f32),
            jax.ShapeDtypeStruct((coef, 3, 3, hid), f32),
            jax.ShapeDtypeStruct((1, coef), f32),
        ),
        in_specs=[vmem] * 2 + [smem],
        out_specs=(vmem,) * 6,
        compiler_params=params,
        name="finish",
    )(mine, other, core)

    return (
        new_velocity,
        grad_velocity,
        jnp.transpose(g_in.reshape(3, 3, 2, hid), (3, 2, 0, 1)),
        gb_in.reshape(hid),
        jnp.transpose(g_mid.reshape(3, 3, hid, hid), (2, 3, 0, 1)),
        gb_mid.reshape(hid),
        jnp.transpose(g_out, (0, 3, 1, 2)),
        gb_out.reshape(coef),
    )


def solution(mesh):
    in_specs = (P("groups", "gx", "gy"), P(), P(), P(), P(), P(), P(), P("groups", "gx", "gy"))
    out_specs = (
        P("groups", "gx", "gy"),
        P("groups", "gx", "gy"),
        P("groups", None, None, None),
        P("groups"),
        P("groups", None, None, None),
        P("groups"),
        P("groups", None, None, None),
        P("groups"),
    )
    return jax.shard_map(
        per_device, mesh=mesh, in_specs=in_specs, out_specs=out_specs, check_vma=False
    )
```

```python
import math

import jax
import jax.numpy as jnp
from jax import lax
from jax.experimental import pallas as pl
from jax.experimental.pallas import tpu as pltpu
from jax.sharding import PartitionSpec as P

advection = 0.2
viscosity = 0.05
forcing_amp = 0.05
forcing_wave = 4
face_base = ((0.0, 0.5, 0.0, 0.0, 0.5, 0.0), (0.0, 0.0, 0.5, 0.5, 0.0, 0.0))
halo = 4
hid = 64
coef = 12
slot = 16
side = 2 * halo
pitch = 2 * side
left_of, right_of = halo - 1, side + halo
taps_x = [(a, b) for a in (0, 1) for b in (-1, 0, 1)]
taps_y = [(a, b) for a in (-1, 0, 1) for b in (0, 1)]
f32 = jnp.float32
bf16 = jnp.bfloat16


def shift(value, rows, cols):
    if rows:
        value = pltpu.roll(value, (-rows) % value.shape[-2], value.ndim - 2)
    if cols:
        value = pltpu.roll(value, (-cols) % value.shape[-1], value.ndim - 1)
    return value


def mm(lhs, rhs):
    return lax.dot_general(lhs, rhs, (((1,), (0,)), ((), ())), preferred_element_type=f32)


def mm_nt(lhs, rhs):
    return lax.dot_general(lhs, rhs, (((1,), (1,)), ((), ())), preferred_element_type=f32)


def sigma_of(linear):
    return 0.5 * jnp.tanh(0.5 * linear) + 0.5


def with_lane(value, at, column):
    tiles = [value[:, k : k + 128] for k in range(0, value.shape[1], 128)]
    lane = lax.broadcasted_iota(jnp.int32, (1, 128), 1)
    tiles[at // 128] = jnp.where(lane == at % 128, column, tiles[at // 128])
    return jnp.concatenate(tiles, axis=1)


def strip_column(strip, row, at, to):
    source = row * pitch + at
    tile = strip[:, source // 128 * 128 : source // 128 * 128 + 128]
    return pltpu.roll(tile, (to - source) % 128, 1) if (to - source) % 128 else tile


def beside(low, middle, high, before, after):
    return (
        with_lane(shift(low, 0, -1), 0, before),
        middle,
        with_lane(shift(high, 0, 1), high.shape[1] - 1, after),
    )


def strip_taps(strip, columns=(-1, 0, 1)):
    return jnp.concatenate(
        [shift(strip, 0, a * pitch + b) for b in columns for a in (-1, 0, 1)], axis=0
    )


def strip_of(planes, rows, cols):
    lane = lax.broadcasted_iota(jnp.int32, (1, 128), 1)
    per_tile = 128 // pitch
    tiles = []
    for start in range(0, rows, per_tile):
        tile = jnp.zeros((slot, 128), f32)
        for k in range(min(per_tile, rows - start)):
            at = slice((start + k) * slot, (start + k + 1) * slot)
            pair = jnp.where(lane < side, planes[0, at, :], pltpu.roll(planes[cols // 128, at, :], side, 1))
            pair = pltpu.roll(pair, k * pitch, 1) if k else pair
            tile = jnp.where((lane >= k * pitch) & (lane < (k + 1) * pitch), pair, tile)
        tiles.append(tile)
    return jnp.concatenate(tiles, axis=1).astype(bf16)


class Rows:
    def __init__(self, size, *pieces):
        self.size = size
        self.pieces = pieces

    def get(self, lo, hi, lead=()):
        parts = []
        for start, stop, ref in self.pieces:
            first, last = max(lo, start), min(hi, stop)
            if first < last:
                rows = slice((first - start) * self.size, (last - start) * self.size)
                parts.append((first, ref[(*lead, rows, slice(None))]))
        parts = [part for _, part in sorted(parts, key=lambda item: item[0])]
        return parts[0] if len(parts) == 1 else jnp.concatenate(parts, axis=0)

    def put(self, lo, value, lead=()):
        for start, stop, ref in self.pieces:
            if start <= lo < stop:
                rows = slice((lo - start) * self.size, (lo - start) * self.size + value.shape[0])
                ref[(*lead, rows, slice(None))] = value

    def put_shifted(self, lo, value, strip, first):
        value = value.astype(bf16)
        ends = [
            jnp.concatenate([strip_column(strip, lo + k - first, at, to) for k in range(2)], axis=0)
            for at, to in ((left_of, 0), (right_of, value.shape[1] - 1))
        ]
        for b, shifted in enumerate(beside(value, value, value, *ends)):
            self.put(lo, shifted, (b,))

    def put_cut(self, lo, value, lead):
        value = value.astype(bf16)
        cols = self.pieces[0][2].shape[-1]
        for b in range(3):
            self.put(lo, shift(value, 0, halo - 1 + b)[:, :cols], (*lead, b))

    def window(self, lo, hi, lead=()):
        return jnp.concatenate([self.get(lo, hi, (*lead, b)) for b in range(3)], axis=0)


def put_plane(planes, k, stride, value):
    for j in range(planes.shape[0]):
        planes[j, pl.ds(k, value.shape[0], stride=stride), :] = value[:, 128 * j : 128 * j + 128]


def take_plane(planes, k, count, stride):
    tiles = [planes[j, pl.ds(k, count, stride=stride), :] for j in range(planes.shape[0])]
    return jnp.concatenate(tiles, axis=1)


def take_rows(planes, at, size):
    return jnp.concatenate([planes[j, at : at + size, :] for j in range(planes.shape[0])], axis=1)


def put_rows(planes, at, value):
    for j in range(planes.shape[0]):
        planes[j, at : at + value.shape[0], :] = value[:, 128 * j : 128 * j + 128]


def faces(w0, w1):
    normal_x = 0.5 * (w0 + shift(w0, 1, 0))
    normal_y = 0.5 * (w1 + shift(w1, 0, 1))
    return normal_x, normal_y


def shifted_fields(w):
    table = {}
    for b in (-1, 0, 1):
        col = shift(w, 0, b)
        for a in (-1, 0, 1):
            table[a, b] = shift(col, a, 0)
    return table


def lane_sums(total):
    lanes = total.shape[1]
    part = total[:, :128]
    for k in range(1, lanes // 128):
        part = part + total[:, 128 * k : 128 * k + 128]
    return jnp.sum(part.T, axis=0, keepdims=True)


def prepare(first, rows, cols, ext_ref, stage, planes, state_in, state_rows, head_rows):
    count = ext_ref.shape[1]
    height, width = stage.shape[1], stage.shape[2]
    stage[...] = jnp.zeros(stage.shape, f32)
    stage[:, 0:count, 0 : cols + 2 * halo] = ext_ref[...]
    w0, w1, c0, c1 = stage[0], stage[1], stage[2], stage[3]

    planes[...] = jnp.zeros(planes.shape, f32)
    put_plane(planes, 0, slot, w0)
    put_plane(planes, 1, slot, w1)
    for r in state_rows:
        state_in.put_cut(r, take_rows(planes, (r - first) * slot, 2 * slot), (0,))
    strips = [strip_of(planes, count, cols)]

    normal_x, normal_y = faces(w0, w1)
    t0, t1 = shifted_fields(w0), shifted_fields(w1)
    fx0 = -advection * (c0 - shift(c0, 1, 0)) * normal_x
    fx1 = -advection * (c1 - shift(c1, 1, 0)) * normal_x
    fy0 = -advection * (c0 - shift(c0, 0, 1)) * normal_y
    fy1 = -advection * (c1 - shift(c1, 0, 1)) * normal_y
    lane = lax.broadcasted_iota(jnp.int32, (height, width), 1)
    row_id = lax.broadcasted_iota(jnp.int32, (height, width), 0) + first
    own = (lane >= halo) & (lane < halo + cols) & (row_id >= halo) & (row_id < halo + rows)
    sums = []
    for at, taps, g0, g1 in ((0, taps_x, fx0, fx1), (6, taps_y, fy0, fy1)):
        raw = [g0 * t0[tap] + g1 * t1[tap] for tap in taps]
        mean = sum(raw[1:], raw[0]) * (1.0 / 6.0)
        for k in range(6):
            value = raw[k] - mean
            put_plane(planes, at + k, slot, value)
            sums.append(jnp.sum(jnp.where(own, value, 0.0), axis=0, keepdims=True))
    for r in head_rows:
        state_in.put_cut(r, take_rows(planes, (r - first) * slot, 2 * slot), (1,))
    strips.append(strip_of(planes, count, cols))
    return sums, strips


class Strips:
    def __init__(self, refs, state, head):
        self.refs, self.state, self.head = refs, state, head

    def spread(self, k):
        ref = self.refs[k]
        if k in (0, 3):
            parts = [ref[:hid, 4 * slot * b : (4 * b + 3) * slot] for b in range(3)]
        else:
            parts = [ref[b, :hid, : 3 * hid] for b in range(3)]
        return jnp.concatenate(parts, axis=1)

    def first(self):
        linear = mm(self.spread(0), strip_taps(self.state)) + self.refs[4][:hid, 0:1]
        sigma = sigma_of(linear)
        act = linear * sigma
        self.slope = sigma + act * (1.0 - sigma)
        self.act_one = act.astype(bf16)

    def second(self):
        linear = mm(self.spread(1), strip_taps(self.act_one)) + self.refs[5][:hid, 0:1]
        sigma = sigma_of(linear)
        act = linear * sigma
        grad = mm(self.spread(3), strip_taps(self.head)) * (sigma + act * (1.0 - sigma))
        self.act_two = act.astype(bf16)
        self.grad_two = grad.astype(bf16)


def layers(
    rows,
    groups,
    refs,
    strips,
    first,
    state_in,
    act_one,
    slope_one,
    grad_two,
    act_two,
    grad_one,
    acc_mid,
    acc_small,
    bias_acc,
):
    w_in_ref, w_mid_ref, w_mid_t_ref, w_out_t_ref, b_in_ref, b_mid_ref = refs
    groups_one, groups_two, groups_back, groups_in = groups

    w_in = w_in_ref[...]
    b_in = b_in_ref[:, 0:1]
    strips.first()
    for r in groups_one:
        linear = mm(w_in, state_in.window(r - 1, r + 3, (0,))) + b_in
        sigma = sigma_of(linear)
        act = linear * sigma
        act_one.put_shifted(r, act, strips.act_one, first)
        slope_one.put(r, sigma + act * (1.0 - sigma))
        if r == groups_one[0]:
            strips.second()

    b_mid = b_mid_ref[:, 0:1]
    w_out_t = w_out_t_ref[...]
    w_mid = jnp.concatenate([w_mid_ref[b] for b in range(3)], axis=1)
    w_mid_t = jnp.concatenate([w_mid_t_ref[b] for b in range(3)], axis=1)
    held = []
    for r in groups_two:
        window = [act_one.get(r - 1, r + 3, (b,)) for b in range(3)]
        linear = mm(w_mid, jnp.concatenate(window, axis=0)) + b_mid
        sigma = sigma_of(linear)
        act = linear * sigma
        act_short = act.astype(bf16)
        act_two.put(r, act_short)
        fed = state_in.window(r - 1, r + 3, (1,))
        grad = mm(w_out_t, fed) * (sigma + act * (1.0 - sigma))
        grad_two.put_shifted(r, grad, strips.grad_two, first)
        if halo <= r < halo + rows:
            bias_acc[0] += grad
            held.append((grad.astype(bf16), window, fed, act_short))
        if held and (len(held) == 2 or r == groups_two[-1]):
            grads, windows, feds, acts = zip(*held)
            held = []
            grads = jnp.concatenate(grads, axis=1)
            for b in range(3):
                acc_mid[b] += mm_nt(grads, jnp.concatenate([w[b] for w in windows], axis=1))
            acc_small[0] += mm_nt(jnp.concatenate(feds, axis=1), jnp.concatenate(acts, axis=1))

    for r in groups_back:
        grad = mm(w_mid_t, grad_two.window(r - 1, r + 3)) * slope_one.get(r, r + 2)
        grad_one.put(r, grad.astype(bf16))
        if r < halo:
            bias_acc[1, hid:, :] += grad[hid:, :]
        elif r + 2 > halo + rows:
            bias_acc[1, :hid, :] += grad[:hid, :]
        else:
            bias_acc[1] += grad
    for r in groups_in:
        acc_small[1] += mm_nt(state_in.window(r - 1, r + 3, (0,)), grad_one.get(r, r + 2))


def inner_kernel(rows, cols, ext_ref, *refs):
    weight_refs, refs = refs[:6], refs[6:]
    act_one, slope_one, grad_two, act_two, grad_one, acc_mid, acc_small, bias_acc, *refs = refs
    stage, planes, state_in = refs
    low, high = halo, halo + rows
    state_in = Rows(slot, (low, high, state_in))
    acc_mid[...] = jnp.zeros(acc_mid.shape, f32)
    acc_small[...] = jnp.zeros(acc_small.shape, f32)
    bias_acc[...] = jnp.zeros(bias_acc.shape, f32)
    pairs = range(low, high, 2)
    _, strips = prepare(low, rows, cols, ext_ref, stage, planes, state_in, pairs, pairs)
    groups = [range(low + k, high - k, 2) for k in (1, 2, 3, 4)]
    layers(
        rows,
        groups,
        weight_refs,
        Strips(weight_refs, *strips),
        low,
        state_in,
        Rows(hid, (low + 1, high - 1, act_one)),
        Rows(hid, (low + 1, high - 1, slope_one)),
        Rows(hid, (low + 2, high - 2, grad_two)),
        Rows(hid, (low + 2, high - 2, act_two)),
        Rows(hid, (low + 3, high - 3, grad_one)),
        acc_mid,
        acc_small,
        bias_acc,
    )


def split_rows(size, first, low, high, last, lower_ref, inner_ref, upper_ref):
    return Rows(size, (first, low, lower_ref), (low, high, inner_ref), (high, last, upper_ref))


def outer_kernel(rows, cols, ext_ref, *refs):
    weight_refs, core_ref, refs = refs[:6], refs[6], refs[7:]
    act_one_in, slope_one_in, grad_two_in, grad_one_in, acc_mid_in, acc_small_in, bias_in, *refs = refs
    keep_ref, send_ref, act_two, grad_one, act_two_strip, grad_two_strip, slope_strip, *refs = refs
    pay, stage, planes, state_in, act_one, slope_one, grad_two, acc_mid, acc_small, bias_acc = refs
    low, high, deep = halo, halo + rows, rows + 2 * halo
    acc_mid[...] = acc_mid_in[...]
    acc_small[...] = acc_small_in[...]
    bias_acc[...] = bias_in[...]
    state_in = Rows(slot, (0, deep, state_in))
    state_rows = [r for r in range(0, deep, 2) if r < low + 6 or r + 2 > high - 6]
    head_rows = [r for r in range(0, deep, 2) if r < low + 4 or r + 2 > high - 4]
    sums, strips = prepare(0, rows, cols, ext_ref, stage, planes, state_in, state_rows, head_rows)
    bias_out = jnp.concatenate(sums + [jnp.zeros((128 - coef, stage.shape[2]), f32)], axis=0)
    groups = [
        [*range(k, low + k, 2), *range(high - k, deep - k, 2)] for k in (1, 2, 3)
    ]
    groups.append([low, low + 2, high - 4, high - 2])

    def both(k, edge, inner):
        edges = [edge.at[i] for i in range(2)]
        return split_rows(hid, k, low + k, high - k, deep - k, edges[0], inner, edges[1])

    strips = Strips(weight_refs, *strips)
    layers(
        rows,
        groups,
        weight_refs,
        strips,
        0,
        state_in,
        both(1, act_one, act_one_in),
        both(1, slope_one, slope_one_in),
        both(2, grad_two, grad_two_in),
        Rows(hid, (2, low + 2, act_two.at[0]), (high - 2, deep - 2, act_two.at[1])),
        both(3, grad_one, grad_one_in),
        acc_mid,
        acc_small,
        bias_acc,
    )

    act_two_strip[...] = strips.act_two
    grad_two_strip[...] = strips.grad_two
    slope_strip[...] = strips.slope

    for b in range(3):
        total = acc_mid[b, :hid, : 3 * hid] + acc_mid[b, hid:, hid:]
        for a in range(3):
            t = 3 * a + b
            block = total[:, a * hid : (a + 1) * hid].astype(bf16)
            for h in range(2):
                pay[h, :, t * hid : (t + 1) * hid] = block[32 * h : 32 * h + 32]
    slots = []
    pieces = []
    for a in range(3):
        for b in range(3):
            at = (2 - b) * 4 * slot + (2 - a) * slot
            slots.append(
                acc_small[0, at : at + slot, :hid] + acc_small[0, at + slot : at + 2 * slot, hid:]
            )
            at = b * 4 * slot + a * slot
            pieces.append(
                acc_small[1, at : at + 2, :hid] + acc_small[1, at + slot : at + slot + 2, hid:]
            )
    sums_in, sums_mid = lane_sums(bias_acc[1]), lane_sums(bias_acc[0])
    pieces.append(sums_in[:, :hid] + sums_in[:, hid:])
    pieces.append(sums_mid[:, :hid] + sums_mid[:, hid:])
    pieces.append(lane_sums(bias_out)[:, :hid])
    pieces.append(jnp.zeros((11, hid), f32))
    rest = jnp.concatenate(pieces, axis=0)
    slots += [rest[:slot], rest[slot:], jnp.zeros((slot, hid), f32)]
    for h in range(2):
        for q in range(3):
            at = 6 * h + 2 * q
            block = jnp.concatenate(slots[at : at + 2], axis=0).astype(bf16)
            pay[h, :, (9 + q) * hid : (10 + q) * hid] = block
    core = core_ref[0]
    keep_ref[...] = pay[core]
    send_ref[...] = pay[1 - core]


def advance_kernel(
    rows,
    cols,
    ext_ref,
    forcing_ref,
    w_head_ref,
    b_head_ref,
    w_in_t_ref,
    act_two_in,
    act_two_edge,
    grad_one_in,
    grad_one_edge,
    act_two_strip,
    grad_two_strip,
    slope_strip,
    w_mid_t_ref,
    new_ref,
    grad_ref,
    stage,
    head,
    back,
):
    low, high, deep = halo, halo + rows, rows + 2 * halo
    act_two, grad_one = (
        split_rows(hid, k, low + k, high - k, deep - k, edge.at[0], inner, edge.at[1])
        for k, inner, edge in ((2, act_two_in, act_two_edge), (3, grad_one_in, grad_one_edge))
    )
    stage[...] = jnp.zeros(stage.shape, f32)
    stage[:, 0:deep, 0 : cols + 2 * halo] = ext_ref[...]
    w0, w1, c0, c1 = stage[0], stage[1], stage[2], stage[3]
    head[...] = jnp.zeros(head.shape, f32)
    back[...] = jnp.zeros(back.shape, f32)
    b_head = b_head_ref[:, 0:1]
    width = stage.shape[2]
    blank = jnp.zeros((2 * slot, width - cols), f32)

    def weighed(weight_ref, size, strip):
        weight = weight_ref[...]
        alone = [weight[2 * size * b : (2 * b + 1) * size, : 3 * hid] for b in range(3)]
        taps = strip_taps(strip, (0,))
        ends = mm(jnp.concatenate(alone, axis=0), taps)
        ends = [ends[b * size : (b + 1) * size] for b in range(3)]

        def pair(field, r):
            part = mm(weight, field.get(r - 1, r + 3))
            part = [part[2 * size * b : 2 * size * (b + 1)] for b in range(3)]
            around = [
                jnp.concatenate([strip_column(end, r + k, at, to) for k in range(2)], axis=0)
                for end, at, to in ((ends[0], left_of, 0), (ends[2], right_of, cols - 1))
            ]
            low, middle, high = beside(*part, *around)
            return low + middle + high

        return ends, pair

    ends, pair = weighed(w_head_ref, slot, act_two_strip[...])
    head_strip = b_head[:slot] + ends[1] + shift(ends[0], 0, -1) + shift(ends[2], 0, 1)
    for r in range(3, deep - 3, 2):
        out = jnp.concatenate([pair(act_two, r) + b_head, blank], axis=1)
        out = pltpu.roll(out, halo, 1)
        for at, to in ((left_of, halo - 1), (right_of, halo + cols)):
            column = [strip_column(head_strip, r + k, at, to) for k in range(2)]
            out = with_lane(out, to, jnp.concatenate(column, axis=0))
        put_rows(head, r * slot, out)
    spread = jnp.concatenate([w_mid_t_ref[b, :hid, : 3 * hid] for b in range(3)], axis=1)
    grad_one_strip = mm(spread, strip_taps(grad_two_strip[...])) * slope_strip[...]
    _, pair = weighed(w_in_t_ref, 8, grad_one_strip.astype(bf16))
    for r in range(halo, halo + rows, 2):
        out = jnp.concatenate([pair(grad_one, r), blank[:16]], axis=1)
        put_rows(back, r * 8, pltpu.roll(out, halo, 1))

    coefs = [take_plane(head, k, deep, slot) for k in range(coef)]
    mean_x = sum(coefs[1:6], coefs[0]) * (1.0 / 6.0)
    mean_y = sum(coefs[7:12], coefs[6]) * (1.0 / 6.0)
    sx = [coefs[k] - mean_x + face_base[0][k] for k in range(6)]
    sy = [coefs[6 + k] - mean_y + face_base[1][k] for k in range(6)]
    normal_x, normal_y = faces(w0, w1)
    grad_x = [-advection * (c - shift(c, 1, 0)) for c in (c0, c1)]
    grad_y = [-advection * (c - shift(c, 0, 1)) for c in (c0, c1)]
    normal_grad_x, normal_grad_y = 0.0, 0.0
    for c, (w, cot) in enumerate(((w0, c0), (w1, c1))):
        table = shifted_fields(w)
        face_x = sum(s * table[tap] for s, tap in zip(sx, taps_x))
        face_y = sum(s * table[tap] for s, tap in zip(sy, taps_y))
        flux_x = normal_x * face_x
        flux_y = normal_y * face_y
        normal_grad_x = normal_grad_x + grad_x[c] * face_x
        normal_grad_y = normal_grad_y + grad_y[c] * face_y
        around = table[1, 0] + table[-1, 0] + table[0, 1] + table[0, -1]
        new = (
            w
            - advection
            * (flux_x - shift(flux_x, -1, 0) + flux_y - shift(flux_y, 0, -1))
            + viscosity * (around - 4.0 * w)
        )
        if c == 0:
            new = new + forcing_ref[...]
        new_ref[c] = new[halo : halo + rows, halo : halo + cols]
    for c, cot in enumerate((c0, c1)):
        around = shift(cot, 1, 0) + shift(cot, -1, 0) + shift(cot, 0, 1) + shift(cot, 0, -1)
        total = cot + viscosity * (around - 4.0 * cot)
        flow_x = normal_x * grad_x[c]
        flow_y = normal_y * grad_y[c]
        by_col = {-1: {}, 0: {}, 1: {}}
        for s, (a, b) in zip(sx, taps_x):
            by_col[b][a] = by_col[b].get(a, 0.0) + flow_x * s
        for s, (a, b) in zip(sy, taps_y):
            by_col[b][a] = by_col[b].get(a, 0.0) + flow_y * s
        for b, column in by_col.items():
            part = sum(shift(value, -a, 0) for a, value in column.items())
            total = total + shift(part, 0, -b)
        if c == 0:
            total = total + 0.5 * (normal_grad_x + shift(normal_grad_x, -1, 0))
        else:
            total = total + 0.5 * (normal_grad_y + shift(normal_grad_y, 0, -1))
        total = total + take_plane(back, c, deep, 8)
        grad_ref[c] = total[halo : halo + rows, halo : halo + cols]


def finish_kernel(
    scale, mine_ref, other_ref, core_ref, in_ref, b_in_ref, mid_ref, b_mid_ref, out_ref, b_out_ref
):
    mine = mine_ref[...].astype(f32) * scale
    other = other_ref[...].astype(f32) * scale
    first = core_ref[0] == 0
    halves = (jnp.where(first, mine, other), jnp.where(first, other, mine))
    slots = []
    for h, half in enumerate(halves):
        for t in range(9):
            mid_ref[t, 32 * h : 32 * h + 32, :] = half[:, t * hid : (t + 1) * hid]
        for q in range(3):
            block = half[:, (9 + q) * hid : (10 + q) * hid]
            slots += [block[:slot], block[slot:]]
    for a in range(3):
        for b in range(3):
            out_ref[:, a, b, :] = slots[3 * a + b][:coef]
    for t in range(9):
        in_ref[t] = slots[9 + t // 8][2 * t % 16 : 2 * t % 16 + 2]
    b_in_ref[...] = slots[10][2:3]
    b_mid_ref[...] = slots[10][3:4]
    b_out_ref[...] = slots[10][4:5, :coef]


def in_hbm(array):
    return pltpu.with_memory_space_constraint(array, pltpu.HBM)


def fetched(sources, targets, sems):
    copies = [
        pltpu.make_async_copy(source, target, sems.at[k])
        for k, (source, target) in enumerate(zip(sources, targets))
    ]
    for copy in copies:
        copy.start()
    for copy in copies:
        copy.wait()


def pack_kernel(even_ref, velocity_ref, cotangent_ref, fields_ref, far_ref, near_ref, sems):
    cols = fields_ref.shape[2]
    fetched(
        (velocity_ref, cotangent_ref), (fields_ref.at[0:2], fields_ref.at[2:4]), sems
    )
    first = fields_ref[:, :, 0:halo].astype(bf16)
    last = fields_ref[:, :, cols - halo : cols].astype(bf16)
    even = even_ref[0] == 1
    far_ref[...] = jnp.where(even, first, last)
    near_ref[...] = jnp.where(even, last, first)


def weights_kernel(*refs):
    sources, refs = refs[:6], refs[6:]
    outs, (*inputs, sems) = refs[:9], refs[9:]
    fetched(sources, inputs, sems)
    k_in_ref, k_mid_ref, k_out_ref, b_in_ref, b_mid_ref, b_out_ref = inputs
    w_in_ref, w_mid_ref, w_mid_t_ref, w_out_t_ref, w_head_ref, w_in_t_ref, *outs = outs
    c_in_ref, c_mid_ref, c_head_ref = outs

    def band(block, upper):
        none = jnp.zeros(block[0].shape, f32)
        return jnp.concatenate([none, *block] if upper else [*block, none], axis=1)

    def tall(block, rows):
        return jnp.concatenate(
            [block, jnp.zeros((rows - block.shape[0], block.shape[1]), f32)], axis=0
        )

    k_mid = [k_mid_ref[t].astype(f32) for t in range(9)]
    k_mid_t = [k.T for k in k_mid]
    k_out = [k_out_ref[:, t // 3, t % 3, :].astype(f32) for t in range(9)]
    k_in = [k_in_ref[t].astype(f32) for t in range(9)]
    in_rows = []
    out_rows = []
    zero = jnp.zeros((slot, hid), f32)
    for b in range(3):
        forward = [3 * a + b for a in range(3)]
        backward = [8 - t for t in forward]
        for u in range(2):
            at = slice(u * hid, (u + 1) * hid)
            w_mid_ref[b, at, :] = band([k_mid[t] for t in forward], u).astype(bf16)
            w_mid_t_ref[b, at, :] = band([k_mid_t[t] for t in backward], u).astype(bf16)
        head = [band([tall(k_out[t], slot) for t in forward], u) for u in range(2)]
        w_head_ref[2 * slot * b : 2 * slot * (b + 1), :] = jnp.concatenate(head, 0).astype(bf16)
        back = [band([tall(k_in[t], 8) for t in backward], u) for u in range(2)]
        w_in_t_ref[16 * b : 16 * (b + 1), :] = jnp.concatenate(back, 0).astype(bf16)
        for rows, blocks in (
            (in_rows, [tall(k_in[t], slot) for t in forward]),
            (out_rows, [tall(k_out[t], slot) for t in backward]),
        ):
            lower = jnp.concatenate(blocks + [zero], axis=0)
            upper = jnp.concatenate([zero] + blocks, axis=0)
            rows.append(jnp.concatenate([lower, upper], axis=1))
    w_in_ref[...] = jnp.concatenate(in_rows, axis=0).T.astype(bf16)
    w_out_t_ref[...] = jnp.concatenate(out_rows, axis=0).T.astype(bf16)
    for ref, bias in ((c_in_ref, b_in_ref[...]), (c_mid_ref, b_mid_ref[...])):
        ref[...] = jnp.broadcast_to(jnp.concatenate([bias, bias], axis=1), (128, 128)).T
    bias = jnp.concatenate([b_out_ref[...], jnp.zeros((1, slot - coef), f32)], axis=1)
    bias = jnp.concatenate([bias, bias, jnp.zeros((1, 128 - 2 * slot), f32)], axis=1)
    c_head_ref[...] = jnp.broadcast_to(bias, (128, 128)).T[: 2 * slot]


def edges(fields, axis, dim):
    size = fields.shape[dim]
    even = lax.axis_index(axis) % 2 == 0
    first = lax.slice_in_dim(fields, 0, halo, axis=dim).astype(bf16)
    last = lax.slice_in_dim(fields, size - halo, size, axis=dim).astype(bf16)
    return jnp.where(even, first, last), jnp.where(even, last, first)


def widened(fields, far, near, axis, dim):
    count = lax.axis_size(axis)
    even = lax.axis_index(axis) % 2 == 0
    far_pairs = [(i, (i + 1 if i % 2 else i - 1) % count) for i in range(count)]
    far = lax.ppermute(far, axis, far_pairs)
    near = lax.ppermute(near, axis, [(i, i ^ 1) for i in range(count)])
    low = jnp.where(even, far, near).astype(f32)
    high = jnp.where(even, near, far).astype(f32)
    return jnp.concatenate([low, fields, high], axis=dim)


def swap(value, rows, cols):
    height, width = lax.axis_size("gx"), lax.axis_size("gy")
    pairs = [
        (i * width + j, (i ^ rows) * width + (j ^ cols)) for i in range(height) for j in range(width)
    ]
    return lax.ppermute(value, ("gx", "gy"), pairs)


def added(*values):
    sums = [v.astype(f32) for v in values]
    while len(sums) > 1:
        sums = [sums[k] + sums[k + 1] for k in range(0, len(sums), 2)]
    return sums[0].astype(bf16)


def summed(keep, send, beside):
    half = added(keep, swap(send, 0, 1))
    steps = [(0, 1 << k) for k in range(1, lax.axis_size("gy").bit_length() - 1)]
    steps += [(1 << k, 0) for k in range(lax.axis_size("gx").bit_length() - 1)]
    while steps:
        if len(steps) >= 2 and steps[0][0] == 0 and steps[1][1] == 0:
            (_, cols), (rows, _) = steps[:2]
            half = added(
                half,
                swap(half, 0, cols),
                swap(half, rows, 0),
                swap(half, rows, cols),
            )
            steps = steps[2:]
        else:
            arrived = swap(half, *steps[0])
            steps = steps[1:]
            if not steps:
                arrived, beside = lax.optimization_barrier((arrived, beside))
            half = added(half, arrived)
    return half, swap(half, 0, 1), beside


def per_device(velocity, kernel_in, bias_in, kernel_mid, bias_mid, kernel_out, bias_out, cotangent):
    rows, cols = velocity.shape[1], velocity.shape[2]
    ny_total = lax.axis_size("gy") * cols
    cell_count = lax.axis_size("gx") * rows * ny_total
    deep = rows + 2 * halo
    width = -(-(cols + 2 * halo) // 128) * 128
    vmem = pl.BlockSpec(memory_space=pltpu.VMEM)
    params = pltpu.CompilerParams(vmem_limit_bytes=18 << 20)

    core = (lax.axis_index("gy") % 2).astype(jnp.int32).reshape(1)
    smem = pl.BlockSpec(memory_space=pltpu.SMEM)
    hbm = pl.BlockSpec(memory_space=pltpu.HBM)
    w_in, w_mid, w_mid_t, w_out_t, w_head, w_in_t, b_in, b_mid, b_head = pl.pallas_call(
        weights_kernel,
        out_shape=(
            jax.ShapeDtypeStruct((2 * hid, 12 * slot), bf16),
            jax.ShapeDtypeStruct((3, 2 * hid, 4 * hid), bf16),
            jax.ShapeDtypeStruct((3, 2 * hid, 4 * hid), bf16),
            jax.ShapeDtypeStruct((2 * hid, 12 * slot), bf16),
            jax.ShapeDtypeStruct((6 * slot, 4 * hid), bf16),
            jax.ShapeDtypeStruct((48, 4 * hid), bf16),
            jax.ShapeDtypeStruct((128, 128), f32),
            jax.ShapeDtypeStruct((128, 128), f32),
            jax.ShapeDtypeStruct((2 * slot, 128), f32),
        ),
        in_specs=[hbm] * 6,
        out_specs=(vmem,) * 9,
        scratch_shapes=[
            pltpu.VMEM((9, 2, hid), bf16),
            pltpu.VMEM((9, hid, hid), bf16),
            pltpu.VMEM((coef, 3, 3, hid), bf16),
            pltpu.VMEM((1, hid), f32),
            pltpu.VMEM((1, hid), f32),
            pltpu.VMEM((1, coef), f32),
            pltpu.SemaphoreType.DMA((6,)),
        ],
        compiler_params=params,
        name="weights",
    )(
        in_hbm(jnp.transpose(kernel_in, (2, 3, 1, 0)).reshape(9, 2, hid)),
        in_hbm(jnp.transpose(kernel_mid, (2, 3, 0, 1)).reshape(9, hid, hid)),
        in_hbm(jnp.transpose(kernel_out, (0, 2, 3, 1))),
        in_hbm(bias_in[None, :]),
        in_hbm(bias_mid[None, :]),
        in_hbm(bias_out[None, :]),
    )
    columns = lax.iota(jnp.int32, width) - halo + lax.axis_index("gy") * cols
    forcing = forcing_amp * jnp.sin(2.0 * math.pi * forcing_wave * columns.astype(f32) / ny_total)
    even = (lax.axis_index("gy") % 2 == 0).astype(jnp.int32).reshape(1)
    edge = jax.ShapeDtypeStruct((4, rows, halo), bf16)
    fields, far, near = pl.pallas_call(
        pack_kernel,
        out_shape=(jax.ShapeDtypeStruct((4, rows, cols), f32), edge, edge),
        in_specs=[smem, hbm, hbm],
        out_specs=(vmem,) * 3,
        scratch_shapes=[pltpu.SemaphoreType.DMA((2,))],
        compiler_params=params,
        name="pack",
    )(even, in_hbm(velocity), in_hbm(cotangent))
    wide = widened(fields, far, near, "gy", 2)
    maps = (w_in, w_mid, w_mid_t, w_out_t, b_in, b_mid)
    far, near = edges(wide, "gx", 1)
    near, maps = lax.optimization_barrier((near, maps))
    ext = widened(wide, far, near, "gx", 1)

    accs = (
        jax.ShapeDtypeStruct((3, 2 * hid, 4 * hid), f32),
        jax.ShapeDtypeStruct((2, 12 * slot, 2 * hid), f32),
        jax.ShapeDtypeStruct((2, 2 * hid, cols), f32),
    )
    strip = jax.ShapeDtypeStruct((hid, deep * pitch), bf16)
    act_one, slope_one, grad_two, act_two_in, grad_one_in, *totals = pl.pallas_call(
        lambda *refs: inner_kernel(rows, cols, *refs),
        out_shape=(
            jax.ShapeDtypeStruct((3, (rows - 2) * hid, cols), bf16),
            jax.ShapeDtypeStruct(((rows - 2) * hid, cols), f32),
            jax.ShapeDtypeStruct((3, (rows - 4) * hid, cols), bf16),
            jax.ShapeDtypeStruct(((rows - 4) * hid, cols), bf16),
            jax.ShapeDtypeStruct(((rows - 6) * hid, cols), bf16),
            *accs,
        ),
        in_specs=[vmem] * 7,
        out_specs=(vmem,) * 8,
        scratch_shapes=[
            pltpu.VMEM((4, rows, width), f32),
            pltpu.VMEM((width // 128, rows * slot, 128), f32),
            pltpu.VMEM((2, 3, rows * slot, cols), bf16),
        ],
        compiler_params=params,
        name="inner",
    )(wide, *maps)

    keep, send, act_two_edge, grad_one_edge, *strips = pl.pallas_call(
        lambda *refs: outer_kernel(rows, cols, *refs),
        out_shape=(
            jax.ShapeDtypeStruct((hid // 2, 12 * hid), bf16),
            jax.ShapeDtypeStruct((hid // 2, 12 * hid), bf16),
            jax.ShapeDtypeStruct((2, halo * hid, cols), bf16),
            jax.ShapeDtypeStruct((2, halo * hid, cols), bf16),
            strip,
            strip,
            jax.ShapeDtypeStruct(strip.shape, f32),
        ),
        in_specs=[vmem] * 7 + [smem] + [vmem] * 7,
        out_specs=(vmem,) * 7,
        scratch_shapes=[
            pltpu.VMEM((2, hid // 2, 12 * hid), bf16),
            pltpu.VMEM((4, deep, width), f32),
            pltpu.VMEM((width // 128, deep * slot, 128), f32),
            pltpu.VMEM((2, 3, deep * slot, cols), bf16),
            pltpu.VMEM((2, 3, halo * hid, cols), bf16),
            pltpu.VMEM((2, halo * hid, cols), f32),
            pltpu.VMEM((2, 3, halo * hid, cols), bf16),
            *(pltpu.VMEM(acc.shape, f32) for acc in accs),
        ],
        compiler_params=params,
        name="outer",
    )(ext, *maps, core, act_one, slope_one, grad_two, grad_one_in, *totals)

    new_velocity, grad_velocity = pl.pallas_call(
        lambda *refs: advance_kernel(rows, cols, *refs),
        out_shape=(jax.ShapeDtypeStruct(velocity.shape, f32),) * 2,
        in_specs=[vmem] * 13,
        out_specs=(vmem,) * 2,
        scratch_shapes=[
            pltpu.VMEM((4, deep, width), f32),
            pltpu.VMEM((width // 128, deep * slot, 128), f32),
            pltpu.VMEM((width // 128, deep * 8, 128), f32),
        ],
        compiler_params=params,
        name="advance",
    )(ext, forcing[None, :], w_head, b_head, w_in_t, act_two_in, act_two_edge, grad_one_in, grad_one_edge, *strips, w_mid_t)

    mine, other, (new_velocity, grad_velocity) = summed(
        keep, send, (new_velocity, grad_velocity)
    )
    g_in, gb_in, g_mid, gb_mid, g_out, gb_out = pl.pallas_call(
        lambda *refs: finish_kernel(1.0 / math.sqrt(cell_count), *refs),
        out_shape=(
            jax.ShapeDtypeStruct((9, 2, hid), f32),
            jax.ShapeDtypeStruct((1, hid), f32),
            jax.ShapeDtypeStruct((9, hid, hid), f32),
            jax.ShapeDtypeStruct((1, hid), f32),
            jax.ShapeDtypeStruct((coef, 3, 3, hid), f32),
            jax.ShapeDtypeStruct((1, coef), f32),
        ),
        in_specs=[vmem] * 2 + [smem],
        out_specs=(vmem,) * 6,
        compiler_params=params,
        name="finish",
    )(mine, other, core)

    return (
        new_velocity,
        grad_velocity,
        jnp.transpose(g_in.reshape(3, 3, 2, hid), (3, 2, 0, 1)),
        gb_in.reshape(hid),
        jnp.transpose(g_mid.reshape(3, 3, hid, hid), (2, 3, 0, 1)),
        gb_mid.reshape(hid),
        jnp.transpose(g_out, (0, 3, 1, 2)),
        gb_out.reshape(coef),
    )


def solution(mesh):
    in_specs = (P("groups", "gx", "gy"), P(), P(), P(), P(), P(), P(), P("groups", "gx", "gy"))
    out_specs = (
        P("groups", "gx", "gy"),
        P("groups", "gx", "gy"),
        P("groups", None, None, None),
        P("groups"),
        P("groups", None, None, None),
        P("groups"),
        P("groups", None, None, None),
        P("groups"),
    )
    return jax.shard_map(
        per_device, mesh=mesh, in_specs=in_specs, out_specs=out_specs, check_vma=False
    )
```

```python
import math

import jax
import jax.numpy as jnp
from jax import lax
from jax.experimental import pallas as pl
from jax.experimental.pallas import tpu as pltpu
from jax.sharding import PartitionSpec as P

advection = 0.2
viscosity = 0.05
forcing_amp = 0.05
forcing_wave = 4
face_base = ((0.0, 0.5, 0.0, 0.0, 0.5, 0.0), (0.0, 0.0, 0.5, 0.5, 0.0, 0.0))
halo = 4
hid = 64
coef = 12
slot = 16
side = 2 * halo
pitch = 2 * side
left_of, right_of = halo - 1, side + halo
taps_x = [(a, b) for a in (0, 1) for b in (-1, 0, 1)]
taps_y = [(a, b) for a in (-1, 0, 1) for b in (0, 1)]
f32 = jnp.float32
bf16 = jnp.bfloat16


def shift(value, rows, cols):
    if rows:
        value = pltpu.roll(value, (-rows) % value.shape[-2], value.ndim - 2)
    if cols:
        value = pltpu.roll(value, (-cols) % value.shape[-1], value.ndim - 1)
    return value


def mm(lhs, rhs):
    return lax.dot_general(lhs, rhs, (((1,), (0,)), ((), ())), preferred_element_type=f32)


def mm_nt(lhs, rhs):
    return lax.dot_general(lhs, rhs, (((1,), (1,)), ((), ())), preferred_element_type=f32)


def sigma_of(linear):
    return 0.5 * jnp.tanh(0.5 * linear) + 0.5


def with_lane(value, at, column):
    tiles = [value[:, k : k + 128] for k in range(0, value.shape[1], 128)]
    lane = lax.broadcasted_iota(jnp.int32, (1, 128), 1)
    tiles[at // 128] = jnp.where(lane == at % 128, column, tiles[at // 128])
    return jnp.concatenate(tiles, axis=1)


def strip_column(strip, row, at, to):
    source = row * pitch + at
    tile = strip[:, source // 128 * 128 : source // 128 * 128 + 128]
    return pltpu.roll(tile, (to - source) % 128, 1) if (to - source) % 128 else tile


def beside(low, middle, high, before, after):
    return (
        with_lane(shift(low, 0, -1), 0, before),
        middle,
        with_lane(shift(high, 0, 1), high.shape[1] - 1, after),
    )


def strip_taps(strip, columns=(-1, 0, 1)):
    return jnp.concatenate(
        [shift(strip, 0, a * pitch + b) for b in columns for a in (-1, 0, 1)], axis=0
    )


def strip_of(planes, rows, cols):
    lane = lax.broadcasted_iota(jnp.int32, (1, 128), 1)
    per_tile = 128 // pitch
    tiles = []
    for start in range(0, rows, per_tile):
        tile = jnp.zeros((slot, 128), f32)
        for k in range(min(per_tile, rows - start)):
            at = slice((start + k) * slot, (start + k + 1) * slot)
            pair = jnp.where(lane < side, planes[0, at, :], pltpu.roll(planes[cols // 128, at, :], side, 1))
            pair = pltpu.roll(pair, k * pitch, 1) if k else pair
            tile = jnp.where((lane >= k * pitch) & (lane < (k + 1) * pitch), pair, tile)
        tiles.append(tile)
    return jnp.concatenate(tiles, axis=1).astype(bf16)


class Rows:
    def __init__(self, size, *pieces):
        self.size = size
        self.pieces = pieces

    def get(self, lo, hi, lead=()):
        parts = []
        for start, stop, ref in self.pieces:
            first, last = max(lo, start), min(hi, stop)
            if first < last:
                rows = slice((first - start) * self.size, (last - start) * self.size)
                parts.append((first, ref[(*lead, rows, slice(None))]))
        parts = [part for _, part in sorted(parts, key=lambda item: item[0])]
        return parts[0] if len(parts) == 1 else jnp.concatenate(parts, axis=0)

    def put(self, lo, value, lead=()):
        for start, stop, ref in self.pieces:
            if start <= lo < stop:
                rows = slice((lo - start) * self.size, (lo - start) * self.size + value.shape[0])
                ref[(*lead, rows, slice(None))] = value

    def put_shifted(self, lo, value, strip, first):
        value = value.astype(bf16)
        ends = [
            jnp.concatenate([strip_column(strip, lo + k - first, at, to) for k in range(2)], axis=0)
            for at, to in ((left_of, 0), (right_of, value.shape[1] - 1))
        ]
        for b, shifted in enumerate(beside(value, value, value, *ends)):
            self.put(lo, shifted, (b,))

    def put_cut(self, lo, value, lead):
        value = value.astype(bf16)
        cols = self.pieces[0][2].shape[-1]
        for b in range(3):
            self.put(lo, shift(value, 0, halo - 1 + b)[:, :cols], (*lead, b))

    def window(self, lo, hi, lead=()):
        return jnp.concatenate([self.get(lo, hi, (*lead, b)) for b in range(3)], axis=0)


def put_plane(planes, k, stride, value):
    for j in range(planes.shape[0]):
        planes[j, pl.ds(k, value.shape[0], stride=stride), :] = value[:, 128 * j : 128 * j + 128]


def take_plane(planes, k, count, stride):
    tiles = [planes[j, pl.ds(k, count, stride=stride), :] for j in range(planes.shape[0])]
    return jnp.concatenate(tiles, axis=1)


def take_rows(planes, at, size):
    return jnp.concatenate([planes[j, at : at + size, :] for j in range(planes.shape[0])], axis=1)


def put_rows(planes, at, value):
    for j in range(planes.shape[0]):
        planes[j, at : at + value.shape[0], :] = value[:, 128 * j : 128 * j + 128]


def faces(w0, w1):
    normal_x = 0.5 * (w0 + shift(w0, 1, 0))
    normal_y = 0.5 * (w1 + shift(w1, 0, 1))
    return normal_x, normal_y


def shifted_fields(w):
    table = {}
    for b in (-1, 0, 1):
        col = shift(w, 0, b)
        for a in (-1, 0, 1):
            table[a, b] = shift(col, a, 0)
    return table


def lane_sums(total):
    lanes = total.shape[1]
    part = total[:, :128]
    for k in range(1, lanes // 128):
        part = part + total[:, 128 * k : 128 * k + 128]
    return jnp.sum(part.T, axis=0, keepdims=True)


def prepare(first, rows, cols, ext_ref, stage, planes, state_in, state_rows, head_rows):
    count = ext_ref.shape[1]
    height, width = stage.shape[1], stage.shape[2]
    stage[...] = jnp.zeros(stage.shape, f32)
    stage[:, 0:count, 0 : cols + 2 * halo] = ext_ref[...]
    w0, w1, c0, c1 = stage[0], stage[1], stage[2], stage[3]

    planes[...] = jnp.zeros(planes.shape, f32)
    put_plane(planes, 0, slot, w0)
    put_plane(planes, 1, slot, w1)
    for r in state_rows:
        state_in.put_cut(r, take_rows(planes, (r - first) * slot, 2 * slot), (0,))
    strips = [strip_of(planes, count, cols)]

    normal_x, normal_y = faces(w0, w1)
    t0, t1 = shifted_fields(w0), shifted_fields(w1)
    fx0 = -advection * (c0 - shift(c0, 1, 0)) * normal_x
    fx1 = -advection * (c1 - shift(c1, 1, 0)) * normal_x
    fy0 = -advection * (c0 - shift(c0, 0, 1)) * normal_y
    fy1 = -advection * (c1 - shift(c1, 0, 1)) * normal_y
    lane = lax.broadcasted_iota(jnp.int32, (height, width), 1)
    row_id = lax.broadcasted_iota(jnp.int32, (height, width), 0) + first
    own = (lane >= halo) & (lane < halo + cols) & (row_id >= halo) & (row_id < halo + rows)
    sums = []
    for at, taps, g0, g1 in ((0, taps_x, fx0, fx1), (6, taps_y, fy0, fy1)):
        raw = [g0 * t0[tap] + g1 * t1[tap] for tap in taps]
        mean = sum(raw[1:], raw[0]) * (1.0 / 6.0)
        for k in range(6):
            value = raw[k] - mean
            put_plane(planes, at + k, slot, value)
            sums.append(jnp.sum(jnp.where(own, value, 0.0), axis=0, keepdims=True))
    for r in head_rows:
        state_in.put_cut(r, take_rows(planes, (r - first) * slot, 2 * slot), (1,))
    strips.append(strip_of(planes, count, cols))
    return sums, strips


class Strips:
    def __init__(self, refs, state, head):
        self.refs, self.state, self.head = refs, state, head

    def spread(self, k):
        ref = self.refs[k]
        if k in (0, 3):
            parts = [ref[:hid, 4 * slot * b : (4 * b + 3) * slot] for b in range(3)]
        else:
            parts = [ref[b, :hid, : 3 * hid] for b in range(3)]
        return jnp.concatenate(parts, axis=1)

    def first(self):
        linear = mm(self.spread(0), strip_taps(self.state)) + self.refs[4][:hid, 0:1]
        sigma = sigma_of(linear)
        act = linear * sigma
        self.slope = sigma + act * (1.0 - sigma)
        self.act_one = act.astype(bf16)

    def second(self):
        linear = mm(self.spread(1), strip_taps(self.act_one)) + self.refs[5][:hid, 0:1]
        sigma = sigma_of(linear)
        act = linear * sigma
        grad = mm(self.spread(3), strip_taps(self.head)) * (sigma + act * (1.0 - sigma))
        self.act_two = act.astype(bf16)
        self.grad_two = grad.astype(bf16)


def layers(
    rows,
    groups,
    refs,
    strips,
    first,
    state_in,
    act_one,
    slope_one,
    grad_two,
    act_two,
    grad_one,
    acc_mid,
    acc_small,
    bias_acc,
):
    w_in_ref, w_mid_ref, w_mid_t_ref, w_out_t_ref, b_in_ref, b_mid_ref = refs
    groups_one, groups_two, groups_back, groups_in = groups

    w_in = w_in_ref[...]
    b_in = b_in_ref[:, 0:1]
    strips.first()
    for r in groups_one:
        linear = mm(w_in, state_in.window(r - 1, r + 3, (0,))) + b_in
        sigma = sigma_of(linear)
        act = linear * sigma
        act_one.put_shifted(r, act, strips.act_one, first)
        slope_one.put(r, sigma + act * (1.0 - sigma))
        if r == groups_one[0]:
            strips.second()

    b_mid = b_mid_ref[:, 0:1]
    w_out_t = w_out_t_ref[...]
    w_mid = jnp.concatenate([w_mid_ref[b] for b in range(3)], axis=1)
    w_mid_t = jnp.concatenate([w_mid_t_ref[b] for b in range(3)], axis=1)
    held = []
    for r in groups_two:
        window = [act_one.get(r - 1, r + 3, (b,)) for b in range(3)]
        linear = mm(w_mid, jnp.concatenate(window, axis=0)) + b_mid
        sigma = sigma_of(linear)
        act = linear * sigma
        act_short = act.astype(bf16)
        act_two.put(r, act_short)
        fed = state_in.window(r - 1, r + 3, (1,))
        grad = mm(w_out_t, fed) * (sigma + act * (1.0 - sigma))
        grad_two.put_shifted(r, grad, strips.grad_two, first)
        if halo <= r < halo + rows:
            bias_acc[0] += grad
            held.append((grad.astype(bf16), window, fed, act_short))
        if held and (len(held) == 3 or r == groups_two[-1]):
            grads, windows, feds, acts = zip(*held)
            held = []
            grads = jnp.concatenate(grads, axis=1)
            for b in range(3):
                acc_mid[b] += mm_nt(grads, jnp.concatenate([w[b] for w in windows], axis=1))
            acc_small[0] += mm_nt(jnp.concatenate(feds, axis=1), jnp.concatenate(acts, axis=1))

    for r in groups_back:
        grad = mm(w_mid_t, grad_two.window(r - 1, r + 3)) * slope_one.get(r, r + 2)
        grad_one.put(r, grad.astype(bf16))
        if r < halo:
            bias_acc[1, hid:, :] += grad[hid:, :]
        elif r + 2 > halo + rows:
            bias_acc[1, :hid, :] += grad[:hid, :]
        else:
            bias_acc[1] += grad
    fed = jnp.concatenate([state_in.window(r - 1, r + 3, (0,)) for r in groups_in], axis=1)
    grads = jnp.concatenate([grad_one.get(r, r + 2) for r in groups_in], axis=1)
    acc_small[1] += mm_nt(fed, grads)


def inner_kernel(rows, cols, ext_ref, *refs):
    weight_refs, refs = refs[:6], refs[6:]
    act_one, slope_one, grad_two, act_two, grad_one, acc_mid, acc_small, bias_acc, *refs = refs
    stage, planes, state_in = refs
    low, high = halo, halo + rows
    state_in = Rows(slot, (low, high, state_in))
    acc_mid[...] = jnp.zeros(acc_mid.shape, f32)
    acc_small[...] = jnp.zeros(acc_small.shape, f32)
    bias_acc[...] = jnp.zeros(bias_acc.shape, f32)
    pairs = range(low, high, 2)
    _, strips = prepare(low, rows, cols, ext_ref, stage, planes, state_in, pairs, pairs)
    groups = [range(low + k, high - k, 2) for k in (1, 2, 3, 4)]
    layers(
        rows,
        groups,
        weight_refs,
        Strips(weight_refs, *strips),
        low,
        state_in,
        Rows(hid, (low + 1, high - 1, act_one)),
        Rows(hid, (low + 1, high - 1, slope_one)),
        Rows(hid, (low + 2, high - 2, grad_two)),
        Rows(hid, (low + 2, high - 2, act_two)),
        Rows(hid, (low + 3, high - 3, grad_one)),
        acc_mid,
        acc_small,
        bias_acc,
    )


def split_rows(size, first, low, high, last, lower_ref, inner_ref, upper_ref):
    return Rows(size, (first, low, lower_ref), (low, high, inner_ref), (high, last, upper_ref))


def outer_kernel(rows, cols, ext_ref, *refs):
    weight_refs, core_ref, refs = refs[:6], refs[6], refs[7:]
    act_one_in, slope_one_in, grad_two_in, grad_one_in, acc_mid_in, acc_small_in, bias_in, *refs = refs
    keep_ref, send_ref, act_two, grad_one, act_two_strip, grad_two_strip, slope_strip, *refs = refs
    pay, stage, planes, state_in, act_one, slope_one, grad_two, acc_mid, acc_small, bias_acc = refs
    low, high, deep = halo, halo + rows, rows + 2 * halo
    acc_mid[...] = acc_mid_in[...]
    acc_small[...] = acc_small_in[...]
    bias_acc[...] = bias_in[...]
    state_in = Rows(slot, (0, deep, state_in))
    state_rows = [r for r in range(0, deep, 2) if r < low + 6 or r + 2 > high - 6]
    head_rows = [r for r in range(0, deep, 2) if r < low + 4 or r + 2 > high - 4]
    sums, strips = prepare(0, rows, cols, ext_ref, stage, planes, state_in, state_rows, head_rows)
    bias_out = jnp.concatenate(sums + [jnp.zeros((128 - coef, stage.shape[2]), f32)], axis=0)
    groups = [
        [*range(k, low + k, 2), *range(high - k, deep - k, 2)] for k in (1, 2, 3)
    ]
    groups.append([low, low + 2, high - 4, high - 2])

    def both(k, edge, inner):
        edges = [edge.at[i] for i in range(2)]
        return split_rows(hid, k, low + k, high - k, deep - k, edges[0], inner, edges[1])

    strips = Strips(weight_refs, *strips)
    layers(
        rows,
        groups,
        weight_refs,
        strips,
        0,
        state_in,
        both(1, act_one, act_one_in),
        both(1, slope_one, slope_one_in),
        both(2, grad_two, grad_two_in),
        Rows(hid, (2, low + 2, act_two.at[0]), (high - 2, deep - 2, act_two.at[1])),
        both(3, grad_one, grad_one_in),
        acc_mid,
        acc_small,
        bias_acc,
    )

    act_two_strip[...] = strips.act_two
    grad_two_strip[...] = strips.grad_two
    slope_strip[...] = strips.slope

    for b in range(3):
        total = acc_mid[b, :hid, : 3 * hid] + acc_mid[b, hid:, hid:]
        for a in range(3):
            t = 3 * a + b
            block = total[:, a * hid : (a + 1) * hid].astype(bf16)
            for h in range(2):
                pay[h, :, t * hid : (t + 1) * hid] = block[32 * h : 32 * h + 32]
    slots = []
    pieces = []
    for a in range(3):
        for b in range(3):
            at = (2 - b) * 4 * slot + (2 - a) * slot
            slots.append(
                acc_small[0, at : at + slot, :hid] + acc_small[0, at + slot : at + 2 * slot, hid:]
            )
            at = b * 4 * slot + a * slot
            pieces.append(
                acc_small[1, at : at + 2, :hid] + acc_small[1, at + slot : at + slot + 2, hid:]
            )
    sums_in, sums_mid = lane_sums(bias_acc[1]), lane_sums(bias_acc[0])
    pieces.append(sums_in[:, :hid] + sums_in[:, hid:])
    pieces.append(sums_mid[:, :hid] + sums_mid[:, hid:])
    pieces.append(lane_sums(bias_out)[:, :hid])
    pieces.append(jnp.zeros((11, hid), f32))
    rest = jnp.concatenate(pieces, axis=0)
    slots += [rest[:slot], rest[slot:], jnp.zeros((slot, hid), f32)]
    for h in range(2):
        for q in range(3):
            at = 6 * h + 2 * q
            block = jnp.concatenate(slots[at : at + 2], axis=0).astype(bf16)
            pay[h, :, (9 + q) * hid : (10 + q) * hid] = block
    core = core_ref[0]
    keep_ref[...] = pay[core]
    send_ref[...] = pay[1 - core]


def advance_kernel(
    rows,
    cols,
    ext_ref,
    forcing_ref,
    w_head_ref,
    b_head_ref,
    w_in_t_ref,
    act_two_in,
    act_two_edge,
    grad_one_in,
    grad_one_edge,
    act_two_strip,
    grad_two_strip,
    slope_strip,
    w_mid_t_ref,
    new_ref,
    grad_ref,
    stage,
    head,
    back,
):
    low, high, deep = halo, halo + rows, rows + 2 * halo
    act_two, grad_one = (
        split_rows(hid, k, low + k, high - k, deep - k, edge.at[0], inner, edge.at[1])
        for k, inner, edge in ((2, act_two_in, act_two_edge), (3, grad_one_in, grad_one_edge))
    )
    stage[...] = jnp.zeros(stage.shape, f32)
    stage[:, 0:deep, 0 : cols + 2 * halo] = ext_ref[...]
    w0, w1, c0, c1 = stage[0], stage[1], stage[2], stage[3]
    head[...] = jnp.zeros(head.shape, f32)
    back[...] = jnp.zeros(back.shape, f32)
    b_head = b_head_ref[:, 0:1]
    width = stage.shape[2]
    blank = jnp.zeros((2 * slot, width - cols), f32)

    def weighed(weight_ref, size, strip):
        weight = weight_ref[...]
        alone = [weight[2 * size * b : (2 * b + 1) * size, : 3 * hid] for b in range(3)]
        taps = strip_taps(strip, (0,))
        ends = mm(jnp.concatenate(alone, axis=0), taps)
        ends = [ends[b * size : (b + 1) * size] for b in range(3)]

        def pair(field, r):
            part = mm(weight, field.get(r - 1, r + 3))
            part = [part[2 * size * b : 2 * size * (b + 1)] for b in range(3)]
            around = [
                jnp.concatenate([strip_column(end, r + k, at, to) for k in range(2)], axis=0)
                for end, at, to in ((ends[0], left_of, 0), (ends[2], right_of, cols - 1))
            ]
            low, middle, high = beside(*part, *around)
            return low + middle + high

        return ends, pair

    ends, pair = weighed(w_head_ref, slot, act_two_strip[...])
    head_strip = b_head[:slot] + ends[1] + shift(ends[0], 0, -1) + shift(ends[2], 0, 1)
    for r in range(3, deep - 3, 2):
        out = jnp.concatenate([pair(act_two, r) + b_head, blank], axis=1)
        out = pltpu.roll(out, halo, 1)
        for at, to in ((left_of, halo - 1), (right_of, halo + cols)):
            column = [strip_column(head_strip, r + k, at, to) for k in range(2)]
            out = with_lane(out, to, jnp.concatenate(column, axis=0))
        put_rows(head, r * slot, out)
    spread = jnp.concatenate([w_mid_t_ref[b, :hid, : 3 * hid] for b in range(3)], axis=1)
    grad_one_strip = mm(spread, strip_taps(grad_two_strip[...])) * slope_strip[...]
    _, pair = weighed(w_in_t_ref, 8, grad_one_strip.astype(bf16))
    for r in range(halo, halo + rows, 2):
        out = jnp.concatenate([pair(grad_one, r), blank[:16]], axis=1)
        put_rows(back, r * 8, pltpu.roll(out, halo, 1))

    coefs = [take_plane(head, k, deep, slot) for k in range(coef)]
    mean_x = sum(coefs[1:6], coefs[0]) * (1.0 / 6.0)
    mean_y = sum(coefs[7:12], coefs[6]) * (1.0 / 6.0)
    sx = [coefs[k] - mean_x + face_base[0][k] for k in range(6)]
    sy = [coefs[6 + k] - mean_y + face_base[1][k] for k in range(6)]
    normal_x, normal_y = faces(w0, w1)
    grad_x = [-advection * (c - shift(c, 1, 0)) for c in (c0, c1)]
    grad_y = [-advection * (c - shift(c, 0, 1)) for c in (c0, c1)]
    normal_grad_x, normal_grad_y = 0.0, 0.0
    for c, (w, cot) in enumerate(((w0, c0), (w1, c1))):
        table = shifted_fields(w)
        face_x = sum(s * table[tap] for s, tap in zip(sx, taps_x))
        face_y = sum(s * table[tap] for s, tap in zip(sy, taps_y))
        flux_x = normal_x * face_x
        flux_y = normal_y * face_y
        normal_grad_x = normal_grad_x + grad_x[c] * face_x
        normal_grad_y = normal_grad_y + grad_y[c] * face_y
        around = table[1, 0] + table[-1, 0] + table[0, 1] + table[0, -1]
        new = (
            w
            - advection
            * (flux_x - shift(flux_x, -1, 0) + flux_y - shift(flux_y, 0, -1))
            + viscosity * (around - 4.0 * w)
        )
        if c == 0:
            new = new + forcing_ref[...]
        new_ref[c] = new[halo : halo + rows, halo : halo + cols]
    for c, cot in enumerate((c0, c1)):
        around = shift(cot, 1, 0) + shift(cot, -1, 0) + shift(cot, 0, 1) + shift(cot, 0, -1)
        total = cot + viscosity * (around - 4.0 * cot)
        flow_x = normal_x * grad_x[c]
        flow_y = normal_y * grad_y[c]
        by_col = {-1: {}, 0: {}, 1: {}}
        for s, (a, b) in zip(sx, taps_x):
            by_col[b][a] = by_col[b].get(a, 0.0) + flow_x * s
        for s, (a, b) in zip(sy, taps_y):
            by_col[b][a] = by_col[b].get(a, 0.0) + flow_y * s
        for b, column in by_col.items():
            part = sum(shift(value, -a, 0) for a, value in column.items())
            total = total + shift(part, 0, -b)
        if c == 0:
            total = total + 0.5 * (normal_grad_x + shift(normal_grad_x, -1, 0))
        else:
            total = total + 0.5 * (normal_grad_y + shift(normal_grad_y, 0, -1))
        total = total + take_plane(back, c, deep, 8)
        grad_ref[c] = total[halo : halo + rows, halo : halo + cols]


def finish_kernel(
    scale, mine_ref, other_ref, core_ref, in_ref, b_in_ref, mid_ref, b_mid_ref, out_ref, b_out_ref
):
    mine = mine_ref[...].astype(f32) * scale
    other = other_ref[...].astype(f32) * scale
    first = core_ref[0] == 0
    halves = (jnp.where(first, mine, other), jnp.where(first, other, mine))
    slots = []
    for h, half in enumerate(halves):
        for t in range(9):
            mid_ref[t, 32 * h : 32 * h + 32, :] = half[:, t * hid : (t + 1) * hid]
        for q in range(3):
            block = half[:, (9 + q) * hid : (10 + q) * hid]
            slots += [block[:slot], block[slot:]]
    for a in range(3):
        for b in range(3):
            out_ref[:, a, b, :] = slots[3 * a + b][:coef]
    for t in range(9):
        in_ref[t] = slots[9 + t // 8][2 * t % 16 : 2 * t % 16 + 2]
    b_in_ref[...] = slots[10][2:3]
    b_mid_ref[...] = slots[10][3:4]
    b_out_ref[...] = slots[10][4:5, :coef]


def in_hbm(array):
    return pltpu.with_memory_space_constraint(array, pltpu.HBM)


def fetched(sources, targets, sems):
    copies = [
        pltpu.make_async_copy(source, target, sems.at[k])
        for k, (source, target) in enumerate(zip(sources, targets))
    ]
    for copy in copies:
        copy.start()
    for copy in copies:
        copy.wait()


def pack_kernel(even_ref, velocity_ref, cotangent_ref, fields_ref, far_ref, near_ref, sems):
    cols = fields_ref.shape[2]
    fetched(
        (velocity_ref, cotangent_ref), (fields_ref.at[0:2], fields_ref.at[2:4]), sems
    )
    first = fields_ref[:, :, 0:halo].astype(bf16)
    last = fields_ref[:, :, cols - halo : cols].astype(bf16)
    even = even_ref[0] == 1
    far_ref[...] = jnp.where(even, first, last)
    near_ref[...] = jnp.where(even, last, first)


def weights_kernel(*refs):
    sources, refs = refs[:6], refs[6:]
    outs, (*inputs, sems) = refs[:9], refs[9:]
    fetched(sources, inputs, sems)
    k_in_ref, k_mid_ref, k_out_ref, b_in_ref, b_mid_ref, b_out_ref = inputs
    w_in_ref, w_mid_ref, w_mid_t_ref, w_out_t_ref, w_head_ref, w_in_t_ref, *outs = outs
    c_in_ref, c_mid_ref, c_head_ref = outs

    def band(block, upper):
        none = jnp.zeros(block[0].shape, f32)
        return jnp.concatenate([none, *block] if upper else [*block, none], axis=1)

    def tall(block, rows):
        return jnp.concatenate(
            [block, jnp.zeros((rows - block.shape[0], block.shape[1]), f32)], axis=0
        )

    k_mid = [k_mid_ref[t].astype(f32) for t in range(9)]
    k_mid_t = [k.T for k in k_mid]
    k_out = [k_out_ref[:, t // 3, t % 3, :].astype(f32) for t in range(9)]
    k_in = [k_in_ref[t].astype(f32) for t in range(9)]
    in_rows = []
    out_rows = []
    zero = jnp.zeros((slot, hid), f32)
    for b in range(3):
        forward = [3 * a + b for a in range(3)]
        backward = [8 - t for t in forward]
        for u in range(2):
            at = slice(u * hid, (u + 1) * hid)
            w_mid_ref[b, at, :] = band([k_mid[t] for t in forward], u).astype(bf16)
            w_mid_t_ref[b, at, :] = band([k_mid_t[t] for t in backward], u).astype(bf16)
        head = [band([tall(k_out[t], slot) for t in forward], u) for u in range(2)]
        w_head_ref[2 * slot * b : 2 * slot * (b + 1), :] = jnp.concatenate(head, 0).astype(bf16)
        back = [band([tall(k_in[t], 8) for t in backward], u) for u in range(2)]
        w_in_t_ref[16 * b : 16 * (b + 1), :] = jnp.concatenate(back, 0).astype(bf16)
        for rows, blocks in (
            (in_rows, [tall(k_in[t], slot) for t in forward]),
            (out_rows, [tall(k_out[t], slot) for t in backward]),
        ):
            lower = jnp.concatenate(blocks + [zero], axis=0)
            upper = jnp.concatenate([zero] + blocks, axis=0)
            rows.append(jnp.concatenate([lower, upper], axis=1))
    w_in_ref[...] = jnp.concatenate(in_rows, axis=0).T.astype(bf16)
    w_out_t_ref[...] = jnp.concatenate(out_rows, axis=0).T.astype(bf16)
    for ref, bias in ((c_in_ref, b_in_ref[...]), (c_mid_ref, b_mid_ref[...])):
        ref[...] = jnp.broadcast_to(jnp.concatenate([bias, bias], axis=1), (128, 128)).T
    bias = jnp.concatenate([b_out_ref[...], jnp.zeros((1, slot - coef), f32)], axis=1)
    bias = jnp.concatenate([bias, bias, jnp.zeros((1, 128 - 2 * slot), f32)], axis=1)
    c_head_ref[...] = jnp.broadcast_to(bias, (128, 128)).T[: 2 * slot]


def edges(fields, axis, dim):
    size = fields.shape[dim]
    even = lax.axis_index(axis) % 2 == 0
    first = lax.slice_in_dim(fields, 0, halo, axis=dim).astype(bf16)
    last = lax.slice_in_dim(fields, size - halo, size, axis=dim).astype(bf16)
    return jnp.where(even, first, last), jnp.where(even, last, first)


def widened(fields, far, near, axis, dim):
    count = lax.axis_size(axis)
    even = lax.axis_index(axis) % 2 == 0
    far_pairs = [(i, (i + 1 if i % 2 else i - 1) % count) for i in range(count)]
    far = lax.ppermute(far, axis, far_pairs)
    near = lax.ppermute(near, axis, [(i, i ^ 1) for i in range(count)])
    low = jnp.where(even, far, near).astype(f32)
    high = jnp.where(even, near, far).astype(f32)
    return jnp.concatenate([low, fields, high], axis=dim)


def swap(value, rows, cols):
    height, width = lax.axis_size("gx"), lax.axis_size("gy")
    pairs = [
        (i * width + j, (i ^ rows) * width + (j ^ cols)) for i in range(height) for j in range(width)
    ]
    return lax.ppermute(value, ("gx", "gy"), pairs)


def added(*values):
    sums = [v.astype(f32) for v in values]
    while len(sums) > 1:
        sums = [sums[k] + sums[k + 1] for k in range(0, len(sums), 2)]
    return sums[0].astype(bf16)


def summed(keep, send, beside):
    half = added(keep, swap(send, 0, 1))
    steps = [(0, 1 << k) for k in range(1, lax.axis_size("gy").bit_length() - 1)]
    steps += [(1 << k, 0) for k in range(lax.axis_size("gx").bit_length() - 1)]
    while steps:
        if len(steps) >= 2 and steps[0][0] == 0 and steps[1][1] == 0:
            (_, cols), (rows, _) = steps[:2]
            half = added(
                half,
                swap(half, 0, cols),
                swap(half, rows, 0),
                swap(half, rows, cols),
            )
            steps = steps[2:]
        else:
            arrived = swap(half, *steps[0])
            steps = steps[1:]
            if not steps:
                arrived, beside = lax.optimization_barrier((arrived, beside))
            half = added(half, arrived)
    return half, swap(half, 0, 1), beside


def per_device(velocity, kernel_in, bias_in, kernel_mid, bias_mid, kernel_out, bias_out, cotangent):
    rows, cols = velocity.shape[1], velocity.shape[2]
    ny_total = lax.axis_size("gy") * cols
    cell_count = lax.axis_size("gx") * rows * ny_total
    deep = rows + 2 * halo
    width = -(-(cols + 2 * halo) // 128) * 128
    vmem = pl.BlockSpec(memory_space=pltpu.VMEM)
    params = pltpu.CompilerParams(vmem_limit_bytes=18 << 20)

    core = (lax.axis_index("gy") % 2).astype(jnp.int32).reshape(1)
    smem = pl.BlockSpec(memory_space=pltpu.SMEM)
    hbm = pl.BlockSpec(memory_space=pltpu.HBM)
    w_in, w_mid, w_mid_t, w_out_t, w_head, w_in_t, b_in, b_mid, b_head = pl.pallas_call(
        weights_kernel,
        out_shape=(
            jax.ShapeDtypeStruct((2 * hid, 12 * slot), bf16),
            jax.ShapeDtypeStruct((3, 2 * hid, 4 * hid), bf16),
            jax.ShapeDtypeStruct((3, 2 * hid, 4 * hid), bf16),
            jax.ShapeDtypeStruct((2 * hid, 12 * slot), bf16),
            jax.ShapeDtypeStruct((6 * slot, 4 * hid), bf16),
            jax.ShapeDtypeStruct((48, 4 * hid), bf16),
            jax.ShapeDtypeStruct((128, 128), f32),
            jax.ShapeDtypeStruct((128, 128), f32),
            jax.ShapeDtypeStruct((2 * slot, 128), f32),
        ),
        in_specs=[hbm] * 6,
        out_specs=(vmem,) * 9,
        scratch_shapes=[
            pltpu.VMEM((9, 2, hid), bf16),
            pltpu.VMEM((9, hid, hid), bf16),
            pltpu.VMEM((coef, 3, 3, hid), bf16),
            pltpu.VMEM((1, hid), f32),
            pltpu.VMEM((1, hid), f32),
            pltpu.VMEM((1, coef), f32),
            pltpu.SemaphoreType.DMA((6,)),
        ],
        compiler_params=params,
        name="weights",
    )(
        in_hbm(jnp.transpose(kernel_in, (2, 3, 1, 0)).reshape(9, 2, hid)),
        in_hbm(jnp.transpose(kernel_mid, (2, 3, 0, 1)).reshape(9, hid, hid)),
        in_hbm(jnp.transpose(kernel_out, (0, 2, 3, 1))),
        in_hbm(bias_in[None, :]),
        in_hbm(bias_mid[None, :]),
        in_hbm(bias_out[None, :]),
    )
    columns = lax.iota(jnp.int32, width) - halo + lax.axis_index("gy") * cols
    forcing = forcing_amp * jnp.sin(2.0 * math.pi * forcing_wave * columns.astype(f32) / ny_total)
    even = (lax.axis_index("gy") % 2 == 0).astype(jnp.int32).reshape(1)
    edge = jax.ShapeDtypeStruct((4, rows, halo), bf16)
    fields, far, near = pl.pallas_call(
        pack_kernel,
        out_shape=(jax.ShapeDtypeStruct((4, rows, cols), f32), edge, edge),
        in_specs=[smem, hbm, hbm],
        out_specs=(vmem,) * 3,
        scratch_shapes=[pltpu.SemaphoreType.DMA((2,))],
        compiler_params=params,
        name="pack",
    )(even, in_hbm(velocity), in_hbm(cotangent))
    wide = widened(fields, far, near, "gy", 2)
    maps = (w_in, w_mid, w_mid_t, w_out_t, b_in, b_mid)
    far, near = edges(wide, "gx", 1)
    near, maps = lax.optimization_barrier((near, maps))
    ext = widened(wide, far, near, "gx", 1)

    accs = (
        jax.ShapeDtypeStruct((3, 2 * hid, 4 * hid), f32),
        jax.ShapeDtypeStruct((2, 12 * slot, 2 * hid), f32),
        jax.ShapeDtypeStruct((2, 2 * hid, cols), f32),
    )
    strip = jax.ShapeDtypeStruct((hid, deep * pitch), bf16)
    act_one, slope_one, grad_two, act_two_in, grad_one_in, *totals = pl.pallas_call(
        lambda *refs: inner_kernel(rows, cols, *refs),
        out_shape=(
            jax.ShapeDtypeStruct((3, (rows - 2) * hid, cols), bf16),
            jax.ShapeDtypeStruct(((rows - 2) * hid, cols), f32),
            jax.ShapeDtypeStruct((3, (rows - 4) * hid, cols), bf16),
            jax.ShapeDtypeStruct(((rows - 4) * hid, cols), bf16),
            jax.ShapeDtypeStruct(((rows - 6) * hid, cols), bf16),
            *accs,
        ),
        in_specs=[vmem] * 7,
        out_specs=(vmem,) * 8,
        scratch_shapes=[
            pltpu.VMEM((4, rows, width), f32),
            pltpu.VMEM((width // 128, rows * slot, 128), f32),
            pltpu.VMEM((2, 3, rows * slot, cols), bf16),
        ],
        compiler_params=params,
        name="inner",
    )(wide, *maps)

    keep, send, act_two_edge, grad_one_edge, *strips = pl.pallas_call(
        lambda *refs: outer_kernel(rows, cols, *refs),
        out_shape=(
            jax.ShapeDtypeStruct((hid // 2, 12 * hid), bf16),
            jax.ShapeDtypeStruct((hid // 2, 12 * hid), bf16),
            jax.ShapeDtypeStruct((2, halo * hid, cols), bf16),
            jax.ShapeDtypeStruct((2, halo * hid, cols), bf16),
            strip,
            strip,
            jax.ShapeDtypeStruct(strip.shape, f32),
        ),
        in_specs=[vmem] * 7 + [smem] + [vmem] * 7,
        out_specs=(vmem,) * 7,
        scratch_shapes=[
            pltpu.VMEM((2, hid // 2, 12 * hid), bf16),
            pltpu.VMEM((4, deep, width), f32),
            pltpu.VMEM((width // 128, deep * slot, 128), f32),
            pltpu.VMEM((2, 3, deep * slot, cols), bf16),
            pltpu.VMEM((2, 3, halo * hid, cols), bf16),
            pltpu.VMEM((2, halo * hid, cols), f32),
            pltpu.VMEM((2, 3, halo * hid, cols), bf16),
            *(pltpu.VMEM(acc.shape, f32) for acc in accs),
        ],
        compiler_params=params,
        name="outer",
    )(ext, *maps, core, act_one, slope_one, grad_two, grad_one_in, *totals)

    new_velocity, grad_velocity = pl.pallas_call(
        lambda *refs: advance_kernel(rows, cols, *refs),
        out_shape=(jax.ShapeDtypeStruct(velocity.shape, f32),) * 2,
        in_specs=[vmem] * 13,
        out_specs=(vmem,) * 2,
        scratch_shapes=[
            pltpu.VMEM((4, deep, width), f32),
            pltpu.VMEM((width // 128, deep * slot, 128), f32),
            pltpu.VMEM((width // 128, deep * 8, 128), f32),
        ],
        compiler_params=params,
        name="advance",
    )(ext, forcing[None, :], w_head, b_head, w_in_t, act_two_in, act_two_edge, grad_one_in, grad_one_edge, *strips, w_mid_t)

    mine, other, (new_velocity, grad_velocity) = summed(
        keep, send, (new_velocity, grad_velocity)
    )
    g_in, gb_in, g_mid, gb_mid, g_out, gb_out = pl.pallas_call(
        lambda *refs: finish_kernel(1.0 / math.sqrt(cell_count), *refs),
        out_shape=(
            jax.ShapeDtypeStruct((9, 2, hid), f32),
            jax.ShapeDtypeStruct((1, hid), f32),
            jax.ShapeDtypeStruct((9, hid, hid), f32),
            jax.ShapeDtypeStruct((1, hid), f32),
            jax.ShapeDtypeStruct((coef, 3, 3, hid), f32),
            jax.ShapeDtypeStruct((1, coef), f32),
        ),
        in_specs=[vmem] * 2 + [smem],
        out_specs=(vmem,) * 6,
        compiler_params=params,
        name="finish",
    )(mine, other, core)

    return (
        new_velocity,
        grad_velocity,
        jnp.transpose(g_in.reshape(3, 3, 2, hid), (3, 2, 0, 1)),
        gb_in.reshape(hid),
        jnp.transpose(g_mid.reshape(3, 3, hid, hid), (2, 3, 0, 1)),
        gb_mid.reshape(hid),
        jnp.transpose(g_out, (0, 3, 1, 2)),
        gb_out.reshape(coef),
    )


def solution(mesh):
    in_specs = (P("groups", "gx", "gy"), P(), P(), P(), P(), P(), P(), P("groups", "gx", "gy"))
    out_specs = (
        P("groups", "gx", "gy"),
        P("groups", "gx", "gy"),
        P("groups", None, None, None),
        P("groups"),
        P("groups", None, None, None),
        P("groups"),
        P("groups", None, None, None),
        P("groups"),
    )
    return jax.shard_map(
        per_device, mesh=mesh, in_specs=in_specs, out_specs=out_specs, check_vma=False
    )
```

```python
import math

import jax
import jax.numpy as jnp
from jax import lax
from jax.experimental import pallas as pl
from jax.experimental.pallas import tpu as pltpu
from jax.sharding import PartitionSpec as P

advection = 0.2
viscosity = 0.05
forcing_amp = 0.05
forcing_wave = 4
face_base = ((0.0, 0.5, 0.0, 0.0, 0.5, 0.0), (0.0, 0.0, 0.5, 0.5, 0.0, 0.0))
halo = 4
hid = 64
coef = 12
slot = 16
side = 2 * halo
pitch = 2 * side
left_of, right_of = halo - 1, side + halo
taps_x = [(a, b) for a in (0, 1) for b in (-1, 0, 1)]
taps_y = [(a, b) for a in (-1, 0, 1) for b in (0, 1)]
f32 = jnp.float32
bf16 = jnp.bfloat16


def shift(value, rows, cols):
    if rows:
        value = pltpu.roll(value, (-rows) % value.shape[-2], value.ndim - 2)
    if cols:
        value = pltpu.roll(value, (-cols) % value.shape[-1], value.ndim - 1)
    return value


def mm(lhs, rhs):
    return lax.dot_general(lhs, rhs, (((1,), (0,)), ((), ())), preferred_element_type=f32)


def mm_nt(lhs, rhs):
    return lax.dot_general(lhs, rhs, (((1,), (1,)), ((), ())), preferred_element_type=f32)


def sigma_of(linear):
    return 0.5 * jnp.tanh(0.5 * linear) + 0.5


def with_lane(value, at, column):
    tiles = [value[:, k : k + 128] for k in range(0, value.shape[1], 128)]
    lane = lax.broadcasted_iota(jnp.int32, (1, 128), 1)
    tiles[at // 128] = jnp.where(lane == at % 128, column, tiles[at // 128])
    return jnp.concatenate(tiles, axis=1)


def strip_column(strip, row, at, to):
    source = row * pitch + at
    tile = strip[:, source // 128 * 128 : source // 128 * 128 + 128]
    return pltpu.roll(tile, (to - source) % 128, 1) if (to - source) % 128 else tile


def beside(low, middle, high, before, after):
    return (
        with_lane(shift(low, 0, -1), 0, before),
        middle,
        with_lane(shift(high, 0, 1), high.shape[1] - 1, after),
    )


def strip_taps(strip, columns=(-1, 0, 1)):
    return jnp.concatenate(
        [shift(strip, 0, a * pitch + b) for b in columns for a in (-1, 0, 1)], axis=0
    )


def strip_of(planes, rows, cols):
    lane = lax.broadcasted_iota(jnp.int32, (1, 128), 1)
    per_tile = 128 // pitch
    tiles = []
    for start in range(0, rows, per_tile):
        tile = jnp.zeros((slot, 128), f32)
        for k in range(min(per_tile, rows - start)):
            at = slice((start + k) * slot, (start + k + 1) * slot)
            pair = jnp.where(lane < side, planes[0, at, :], pltpu.roll(planes[cols // 128, at, :], side, 1))
            pair = pltpu.roll(pair, k * pitch, 1) if k else pair
            tile = jnp.where((lane >= k * pitch) & (lane < (k + 1) * pitch), pair, tile)
        tiles.append(tile)
    return jnp.concatenate(tiles, axis=1).astype(bf16)


class Rows:
    def __init__(self, size, *pieces):
        self.size = size
        self.pieces = pieces

    def get(self, lo, hi, lead=()):
        parts = []
        for start, stop, ref in self.pieces:
            first, last = max(lo, start), min(hi, stop)
            if first < last:
                rows = slice((first - start) * self.size, (last - start) * self.size)
                parts.append((first, ref[(*lead, rows, slice(None))]))
        parts = [part for _, part in sorted(parts, key=lambda item: item[0])]
        return parts[0] if len(parts) == 1 else jnp.concatenate(parts, axis=0)

    def put(self, lo, value, lead=()):
        for start, stop, ref in self.pieces:
            if start <= lo < stop:
                rows = slice((lo - start) * self.size, (lo - start) * self.size + value.shape[0])
                ref[(*lead, rows, slice(None))] = value

    def put_shifted(self, lo, value, strip, place):
        value = value.astype(bf16)
        ends = [
            jnp.concatenate([strip_column(strip, place(lo + k), at, to) for k in range(2)], axis=0)
            for at, to in ((left_of, 0), (right_of, value.shape[1] - 1))
        ]
        for b, shifted in enumerate(beside(value, value, value, *ends)):
            self.put(lo, shifted, (b,))

    def put_cut(self, lo, value, lead):
        value = value.astype(bf16)
        cols = self.pieces[0][2].shape[-1]
        for b in range(3):
            self.put(lo, shift(value, 0, halo - 1 + b)[:, :cols], (*lead, b))

    def window(self, lo, hi, lead=()):
        return jnp.concatenate([self.get(lo, hi, (*lead, b)) for b in range(3)], axis=0)


def put_plane(planes, k, stride, value):
    for j in range(planes.shape[0]):
        planes[j, pl.ds(k, value.shape[0], stride=stride), :] = value[:, 128 * j : 128 * j + 128]


def take_plane(planes, k, count, stride):
    tiles = [planes[j, pl.ds(k, count, stride=stride), :] for j in range(planes.shape[0])]
    return jnp.concatenate(tiles, axis=1)


def take_rows(planes, at, size):
    return jnp.concatenate([planes[j, at : at + size, :] for j in range(planes.shape[0])], axis=1)


def put_rows(planes, at, value):
    for j in range(planes.shape[0]):
        planes[j, at : at + value.shape[0], :] = value[:, 128 * j : 128 * j + 128]


def faces(w0, w1):
    normal_x = 0.5 * (w0 + shift(w0, 1, 0))
    normal_y = 0.5 * (w1 + shift(w1, 0, 1))
    return normal_x, normal_y


def shifted_fields(w):
    table = {}
    for b in (-1, 0, 1):
        col = shift(w, 0, b)
        for a in (-1, 0, 1):
            table[a, b] = shift(col, a, 0)
    return table


def lane_sums(total):
    lanes = total.shape[1]
    part = total[:, :128]
    for k in range(1, lanes // 128):
        part = part + total[:, 128 * k : 128 * k + 128]
    return jnp.sum(part.T, axis=0, keepdims=True)


def fill(stage, parts):
    stage[...] = jnp.zeros(stage.shape, f32)
    for at, part in parts:
        stage[:, at : at + part.shape[1], 0 : part.shape[2]] = part.astype(f32)


def prepare(place, cols, parts, stage, planes, state_in, state_rows, head_rows, sum_rows):
    height, width = stage.shape[1], stage.shape[2]
    count = height
    fill(stage, parts)
    w0, w1, c0, c1 = stage[0], stage[1], stage[2], stage[3]

    planes[...] = jnp.zeros(planes.shape, f32)
    put_plane(planes, 0, slot, w0)
    put_plane(planes, 1, slot, w1)
    for r in state_rows:
        state_in.put_cut(r, take_rows(planes, place(r) * slot, 2 * slot), (0,))
    strips = [strip_of(planes, count, cols)]

    normal_x, normal_y = faces(w0, w1)
    t0, t1 = shifted_fields(w0), shifted_fields(w1)
    fx0 = -advection * (c0 - shift(c0, 1, 0)) * normal_x
    fx1 = -advection * (c1 - shift(c1, 1, 0)) * normal_x
    fy0 = -advection * (c0 - shift(c0, 0, 1)) * normal_y
    fy1 = -advection * (c1 - shift(c1, 0, 1)) * normal_y
    lane = lax.broadcasted_iota(jnp.int32, (height, width), 1)
    row_id = lax.broadcasted_iota(jnp.int32, (height, width), 0)
    own = (lane >= halo) & (lane < halo + cols)
    inside = row_id < 0
    for lo, hi in sum_rows:
        inside = inside | ((row_id >= place(lo)) & (row_id <= place(hi - 1)))
    own = own & inside
    sums = []
    for at, taps, g0, g1 in ((0, taps_x, fx0, fx1), (6, taps_y, fy0, fy1)):
        raw = [g0 * t0[tap] + g1 * t1[tap] for tap in taps]
        mean = sum(raw[1:], raw[0]) * (1.0 / 6.0)
        for k in range(6):
            value = raw[k] - mean
            put_plane(planes, at + k, slot, value)
            sums.append(jnp.sum(jnp.where(own, value, 0.0), axis=0, keepdims=True))
    for r in head_rows:
        state_in.put_cut(r, take_rows(planes, place(r) * slot, 2 * slot), (1,))
    strips.append(strip_of(planes, count, cols))
    sums = jnp.concatenate(sums + [jnp.zeros((slot - coef, width), f32)], axis=0)
    return sums, strips


class Strips:
    def __init__(self, refs, state, head):
        self.refs, self.state, self.head = refs, state, head

    def spread(self, k):
        ref = self.refs[k]
        if k in (0, 3):
            parts = [ref[:hid, 4 * slot * b : (4 * b + 3) * slot] for b in range(3)]
        else:
            parts = [ref[b, :hid, : 3 * hid] for b in range(3)]
        return jnp.concatenate(parts, axis=1)

    def first(self):
        linear = mm(self.spread(0), strip_taps(self.state)) + self.refs[4][:hid, 0:1]
        sigma = sigma_of(linear)
        act = linear * sigma
        self.slope = sigma + act * (1.0 - sigma)
        self.act_one = act.astype(bf16)

    def second(self):
        linear = mm(self.spread(1), strip_taps(self.act_one)) + self.refs[5][:hid, 0:1]
        sigma = sigma_of(linear)
        act = linear * sigma
        grad = mm(self.spread(3), strip_taps(self.head)) * (sigma + act * (1.0 - sigma))
        self.act_two = act.astype(bf16)
        self.grad_two = grad.astype(bf16)

    def put(self, refs):
        for ref, value in zip(refs, (self.act_two, self.grad_two, self.slope), strict=True):
            ref[...] = value


def layers(
    rows,
    groups,
    refs,
    strips,
    place,
    state_in,
    act_one,
    slope_one,
    grad_two,
    act_two,
    grad_one,
    acc_mid,
    acc_small,
    bias_acc,
):
    w_in_ref, w_mid_ref, w_mid_t_ref, w_out_t_ref, b_in_ref, b_mid_ref = refs
    groups_one, groups_two, groups_back, groups_in = groups

    w_in = w_in_ref[...]
    b_in = b_in_ref[:, 0:1]
    strips.first()
    for r in groups_one:
        linear = mm(w_in, state_in.window(r - 1, r + 3, (0,))) + b_in
        sigma = sigma_of(linear)
        act = linear * sigma
        act_one.put_shifted(r, act, strips.act_one, place)
        slope_one.put(r, sigma + act * (1.0 - sigma))
        if r == groups_one[0]:
            strips.second()

    b_mid = b_mid_ref[:, 0:1]
    w_out_t = w_out_t_ref[...]
    w_mid = jnp.concatenate([w_mid_ref[b] for b in range(3)], axis=1)
    w_mid_t = jnp.concatenate([w_mid_t_ref[b] for b in range(3)], axis=1)
    held = []
    for r in groups_two:
        window = [act_one.get(r - 1, r + 3, (b,)) for b in range(3)]
        linear = mm(w_mid, jnp.concatenate(window, axis=0)) + b_mid
        sigma = sigma_of(linear)
        act = linear * sigma
        act_short = act.astype(bf16)
        act_two.put(r, act_short)
        fed = state_in.window(r - 1, r + 3, (1,))
        grad = mm(w_out_t, fed) * (sigma + act * (1.0 - sigma))
        grad_two.put_shifted(r, grad, strips.grad_two, place)
        if halo <= r < halo + rows:
            bias_acc[0] += grad
            held.append((grad.astype(bf16), window, fed, act_short))
        if held and (len(held) == 3 or r == groups_two[-1]):
            grads, windows, feds, acts = zip(*held)
            held = []
            grads = jnp.concatenate(grads, axis=1)
            for b in range(3):
                acc_mid[b] += mm_nt(grads, jnp.concatenate([w[b] for w in windows], axis=1))
            acc_small[0] += mm_nt(jnp.concatenate(feds, axis=1), jnp.concatenate(acts, axis=1))

    for r in groups_back:
        grad = mm(w_mid_t, grad_two.window(r - 1, r + 3)) * slope_one.get(r, r + 2)
        grad_one.put(r, grad.astype(bf16))
        if r < halo:
            bias_acc[1, hid:, :] += grad[hid:, :]
        elif r + 2 > halo + rows:
            bias_acc[1, :hid, :] += grad[:hid, :]
        else:
            bias_acc[1] += grad
    fed = jnp.concatenate([state_in.window(r - 1, r + 3, (0,)) for r in groups_in], axis=1)
    grads = jnp.concatenate([grad_one.get(r, r + 2) for r in groups_in], axis=1)
    acc_small[1] += mm_nt(fed, grads)


def inner_kernel(rows, cols, wide_ref, *refs):
    weight_refs, refs = refs[:6], refs[6:]
    act_one, slope_one, grad_two, act_two, grad_one, *refs = refs
    acc_mid, acc_small, bias_acc, state_ref, sums_ref, *strip_refs, stage, planes = refs
    low, high = halo, halo + rows
    state_in = Rows(slot, (low, high, state_ref))
    acc_mid[...] = jnp.zeros(acc_mid.shape, f32)
    acc_small[...] = jnp.zeros(acc_small.shape, f32)
    bias_acc[...] = jnp.zeros(bias_acc.shape, f32)
    pairs = range(low, high, 2)
    sums_ref[...], strips = prepare(
        lambda r: r - low,
        cols,
        [(0, wide_ref[...])],
        stage,
        planes,
        state_in,
        pairs,
        pairs,
        [(low + 2, high - 2)],
    )
    strips = Strips(weight_refs, *strips)
    layers(
        rows,
        [range(low + k, high - k, 2) for k in (1, 2, 3, 4)],
        weight_refs,
        strips,
        lambda r: r - low,
        state_in,
        Rows(hid, (low + 1, high - 1, act_one)),
        Rows(hid, (low + 1, high - 1, slope_one)),
        Rows(hid, (low + 2, high - 2, grad_two)),
        Rows(hid, (low + 2, high - 2, act_two)),
        Rows(hid, (low + 3, high - 3, grad_one)),
        acc_mid,
        acc_small,
        bias_acc,
    )
    strips.put(strip_refs)


def sides(far_ref, near_ref, even_ref):
    far, near = far_ref[...].astype(f32), near_ref[...].astype(f32)
    even = even_ref[0] == 1
    return jnp.where(even, far, near), jnp.where(even, near, far)


def outer_kernel(rows, cols, wide_ref, far_ref, near_ref, even_ref, core_ref, *refs):
    weight_refs, refs = refs[:6], refs[6:]
    act_one_in, slope_one_in, grad_two_in, grad_one_in, state_inner, *refs = refs
    acc_mid_in, acc_small_in, bias_in, sums_in, *refs = refs
    keep_ref, send_ref, act_two, grad_one, *refs = refs
    strip_refs, refs = refs[:3], refs[3:]
    acc_mid, acc_small, bias_acc, pay, stage, planes, state_edge, act_one, slope_one, grad_two = refs
    low, high, deep = halo, halo + rows, rows + 2 * halo
    acc_mid[...] = acc_mid_in[...]
    acc_small[...] = acc_small_in[...]
    bias_acc[...] = bias_in[...]
    edge, used = 2 * halo, 2 * halo - 2

    def place(r):
        return r if r < edge else r - (deep - 2 * edge)

    def both(k, edge_ref, inner_ref):
        return split_rows(
            hid, k, low + k, high - k, deep - k, edge_ref.at[0], inner_ref, edge_ref.at[1]
        )

    state_in = split_rows(
        slot,
        0,
        used,
        deep - used,
        deep,
        state_edge.at[:, :, 0 : used * slot, :],
        state_inner.at[:, :, 2 * slot : (rows - 2) * slot, :],
        state_edge.at[:, :, (2 * edge - used) * slot : 2 * edge * slot, :],
    )
    lower, upper = sides(far_ref, near_ref, even_ref)
    pairs = [*range(0, used, 2), *range(deep - used, deep, 2)]
    sums, strips = prepare(
        place,
        cols,
        [
            (0, lower),
            (halo, wide_ref[:, 0:halo, :]),
            (edge, wide_ref[:, rows - halo : rows, :]),
            (edge + halo, upper),
        ],
        stage,
        planes,
        state_in,
        pairs,
        pairs,
        [(low, low + 2), (high - 2, high)],
    )
    strips = Strips(weight_refs, *strips)
    layers(
        rows,
        [[*range(k, low + k, 2), *range(high - k, deep - k, 2)] for k in (1, 2, 3)]
        + [[low, low + 2, high - 4, high - 2]],
        weight_refs,
        strips,
        place,
        state_in,
        both(1, act_one, act_one_in),
        both(1, slope_one, slope_one_in),
        both(2, grad_two, grad_two_in),
        Rows(hid, (2, low + 2, act_two.at[0]), (high - 2, deep - 2, act_two.at[1])),
        both(3, grad_one, grad_one_in),
        acc_mid,
        acc_small,
        bias_acc,
    )
    strips.put(strip_refs)
    sums = sums + sums_in[...]
    bias_out = jnp.concatenate([sums, jnp.zeros((128 - slot, sums.shape[1]), f32)], axis=0)

    for b in range(3):
        total = acc_mid[b, :hid, : 3 * hid] + acc_mid[b, hid:, hid:]
        for a in range(3):
            t = 3 * a + b
            block = total[:, a * hid : (a + 1) * hid].astype(bf16)
            for h in range(2):
                pay[h, :, t * hid : (t + 1) * hid] = block[32 * h : 32 * h + 32]
    slots = []
    pieces = []
    for a in range(3):
        for b in range(3):
            at = (2 - b) * 4 * slot + (2 - a) * slot
            slots.append(
                acc_small[0, at : at + slot, :hid] + acc_small[0, at + slot : at + 2 * slot, hid:]
            )
            at = b * 4 * slot + a * slot
            pieces.append(
                acc_small[1, at : at + 2, :hid] + acc_small[1, at + slot : at + slot + 2, hid:]
            )
    sums_in, sums_mid = lane_sums(bias_acc[1]), lane_sums(bias_acc[0])
    pieces.append(sums_in[:, :hid] + sums_in[:, hid:])
    pieces.append(sums_mid[:, :hid] + sums_mid[:, hid:])
    pieces.append(lane_sums(bias_out)[:, :hid])
    pieces.append(jnp.zeros((11, hid), f32))
    rest = jnp.concatenate(pieces, axis=0)
    slots += [rest[:slot], rest[slot:], jnp.zeros((slot, hid), f32)]
    for h in range(2):
        for q in range(3):
            at = 6 * h + 2 * q
            block = jnp.concatenate(slots[at : at + 2], axis=0).astype(bf16)
            pay[h, :, (9 + q) * hid : (10 + q) * hid] = block
    core = core_ref[0]
    keep_ref[...] = pay[core]
    send_ref[...] = pay[1 - core]


def split_rows(size, first, low, high, last, lower_ref, inner_ref, upper_ref):
    return Rows(size, (first, low, lower_ref), (low, high, inner_ref), (high, last, upper_ref))


def advance_kernel(
    rows,
    cols,
    wide_ref,
    far_ref,
    near_ref,
    even_ref,
    forcing_ref,
    w_head_ref,
    b_head_ref,
    w_in_t_ref,
    w_mid_t_ref,
    *refs,
):
    inner, outer, (new_ref, grad_ref, stage, head, back) = refs[0:5], refs[5:10], refs[10:]
    act_two_in, grad_one_in = inner[:2]
    act_two_edge, grad_one_edge = outer[:2]
    edge = 2 * halo

    def whole(k):
        skip = 2 * pitch
        parts = [
            outer[k][:, : edge * pitch - skip],
            inner[k][:, skip : rows * pitch - skip],
            outer[k][:, edge * pitch + skip :],
        ]
        return jnp.concatenate(parts, axis=1)

    low, high, deep = halo, halo + rows, rows + 2 * halo
    act_two, grad_one = (
        split_rows(hid, k, low + k, high - k, deep - k, edge.at[0], inner, edge.at[1])
        for k, inner, edge in ((2, act_two_in, act_two_edge), (3, grad_one_in, grad_one_edge))
    )
    lower, upper = sides(far_ref, near_ref, even_ref)
    fill(stage, [(0, lower), (halo, wide_ref[...]), (halo + rows, upper)])
    w0, w1, c0, c1 = stage[0], stage[1], stage[2], stage[3]
    head[...] = jnp.zeros(head.shape, f32)
    back[...] = jnp.zeros(back.shape, f32)
    b_head = b_head_ref[:, 0:1]
    width = stage.shape[2]
    blank = jnp.zeros((2 * slot, width - cols), f32)

    def weighed(weight_ref, size, strip):
        weight = weight_ref[...]
        alone = [weight[2 * size * b : (2 * b + 1) * size, : 3 * hid] for b in range(3)]
        taps = strip_taps(strip, (0,))
        ends = mm(jnp.concatenate(alone, axis=0), taps)
        ends = [ends[b * size : (b + 1) * size] for b in range(3)]

        def pair(field, r):
            part = mm(weight, field.get(r - 1, r + 3))
            part = [part[2 * size * b : 2 * size * (b + 1)] for b in range(3)]
            around = [
                jnp.concatenate([strip_column(end, r + k, at, to) for k in range(2)], axis=0)
                for end, at, to in ((ends[0], left_of, 0), (ends[2], right_of, cols - 1))
            ]
            low, middle, high = beside(*part, *around)
            return low + middle + high

        return ends, pair

    ends, pair = weighed(w_head_ref, slot, whole(2))
    head_strip = b_head[:slot] + ends[1] + shift(ends[0], 0, -1) + shift(ends[2], 0, 1)
    for r in range(3, deep - 3, 2):
        out = jnp.concatenate([pair(act_two, r) + b_head, blank], axis=1)
        out = pltpu.roll(out, halo, 1)
        for at, to in ((left_of, halo - 1), (right_of, halo + cols)):
            column = [strip_column(head_strip, r + k, at, to) for k in range(2)]
            out = with_lane(out, to, jnp.concatenate(column, axis=0))
        put_rows(head, r * slot, out)
    spread = jnp.concatenate([w_mid_t_ref[b, :hid, : 3 * hid] for b in range(3)], axis=1)
    grad_one_strip = mm(spread, strip_taps(whole(3))) * whole(4)
    _, pair = weighed(w_in_t_ref, 8, grad_one_strip.astype(bf16))
    for r in range(halo, halo + rows, 2):
        out = jnp.concatenate([pair(grad_one, r), blank[:16]], axis=1)
        put_rows(back, r * 8, pltpu.roll(out, halo, 1))

    coefs = [take_plane(head, k, deep, slot) for k in range(coef)]
    mean_x = sum(coefs[1:6], coefs[0]) * (1.0 / 6.0)
    mean_y = sum(coefs[7:12], coefs[6]) * (1.0 / 6.0)
    sx = [coefs[k] - mean_x + face_base[0][k] for k in range(6)]
    sy = [coefs[6 + k] - mean_y + face_base[1][k] for k in range(6)]
    normal_x, normal_y = faces(w0, w1)
    grad_x = [-advection * (c - shift(c, 1, 0)) for c in (c0, c1)]
    grad_y = [-advection * (c - shift(c, 0, 1)) for c in (c0, c1)]
    normal_grad_x, normal_grad_y = 0.0, 0.0
    for c, (w, cot) in enumerate(((w0, c0), (w1, c1))):
        table = shifted_fields(w)
        face_x = sum(s * table[tap] for s, tap in zip(sx, taps_x))
        face_y = sum(s * table[tap] for s, tap in zip(sy, taps_y))
        flux_x = normal_x * face_x
        flux_y = normal_y * face_y
        normal_grad_x = normal_grad_x + grad_x[c] * face_x
        normal_grad_y = normal_grad_y + grad_y[c] * face_y
        around = table[1, 0] + table[-1, 0] + table[0, 1] + table[0, -1]
        new = (
            w
            - advection
            * (flux_x - shift(flux_x, -1, 0) + flux_y - shift(flux_y, 0, -1))
            + viscosity * (around - 4.0 * w)
        )
        if c == 0:
            new = new + forcing_ref[...]
        new_ref[c] = new[halo : halo + rows, halo : halo + cols]
    for c, cot in enumerate((c0, c1)):
        around = shift(cot, 1, 0) + shift(cot, -1, 0) + shift(cot, 0, 1) + shift(cot, 0, -1)
        total = cot + viscosity * (around - 4.0 * cot)
        flow_x = normal_x * grad_x[c]
        flow_y = normal_y * grad_y[c]
        by_col = {-1: {}, 0: {}, 1: {}}
        for s, (a, b) in zip(sx, taps_x):
            by_col[b][a] = by_col[b].get(a, 0.0) + flow_x * s
        for s, (a, b) in zip(sy, taps_y):
            by_col[b][a] = by_col[b].get(a, 0.0) + flow_y * s
        for b, column in by_col.items():
            part = sum(shift(value, -a, 0) for a, value in column.items())
            total = total + shift(part, 0, -b)
        if c == 0:
            total = total + 0.5 * (normal_grad_x + shift(normal_grad_x, -1, 0))
        else:
            total = total + 0.5 * (normal_grad_y + shift(normal_grad_y, 0, -1))
        total = total + take_plane(back, c, deep, 8)
        grad_ref[c] = total[halo : halo + rows, halo : halo + cols]


def finish_kernel(
    scale, mine_ref, other_ref, core_ref, in_ref, b_in_ref, mid_ref, b_mid_ref, out_ref, b_out_ref
):
    mine = mine_ref[...].astype(f32) * scale
    other = other_ref[...].astype(f32) * scale
    first = core_ref[0] == 0
    halves = (jnp.where(first, mine, other), jnp.where(first, other, mine))
    slots = []
    for h, half in enumerate(halves):
        for t in range(9):
            mid_ref[t, 32 * h : 32 * h + 32, :] = half[:, t * hid : (t + 1) * hid]
        for q in range(3):
            block = half[:, (9 + q) * hid : (10 + q) * hid]
            slots += [block[:slot], block[slot:]]
    for a in range(3):
        for b in range(3):
            out_ref[:, a, b, :] = slots[3 * a + b][:coef]
    for t in range(9):
        in_ref[t] = slots[9 + t // 8][2 * t % 16 : 2 * t % 16 + 2]
    b_in_ref[...] = slots[10][2:3]
    b_mid_ref[...] = slots[10][3:4]
    b_out_ref[...] = slots[10][4:5, :coef]


def in_hbm(array):
    return pltpu.with_memory_space_constraint(array, pltpu.HBM)


def fetched(sources, targets, sems):
    copies = [
        pltpu.make_async_copy(source, target, sems.at[k])
        for k, (source, target) in enumerate(zip(sources, targets))
    ]
    for copy in copies:
        copy.start()
    for copy in copies:
        copy.wait()


def pack_kernel(even_ref, velocity_ref, cotangent_ref, fields_ref, far_ref, near_ref, sems):
    cols = fields_ref.shape[2]
    fetched(
        (velocity_ref, cotangent_ref), (fields_ref.at[0:2], fields_ref.at[2:4]), sems
    )
    first = fields_ref[:, :, 0:halo].astype(bf16)
    last = fields_ref[:, :, cols - halo : cols].astype(bf16)
    even = even_ref[0] == 1
    far_ref[...] = jnp.where(even, first, last)
    near_ref[...] = jnp.where(even, last, first)


def weights_kernel(*refs):
    sources, refs = refs[:6], refs[6:]
    outs, (*inputs, sems) = refs[:9], refs[9:]
    fetched(sources, inputs, sems)
    k_in_ref, k_mid_ref, k_out_ref, b_in_ref, b_mid_ref, b_out_ref = inputs
    w_in_ref, w_mid_ref, w_mid_t_ref, w_out_t_ref, w_head_ref, w_in_t_ref, *outs = outs
    c_in_ref, c_mid_ref, c_head_ref = outs

    def band(block, upper):
        none = jnp.zeros(block[0].shape, f32)
        return jnp.concatenate([none, *block] if upper else [*block, none], axis=1)

    def tall(block, rows):
        return jnp.concatenate(
            [block, jnp.zeros((rows - block.shape[0], block.shape[1]), f32)], axis=0
        )

    k_mid = [k_mid_ref[t].astype(f32) for t in range(9)]
    k_mid_t = [k.T for k in k_mid]
    k_out = [k_out_ref[:, t // 3, t % 3, :].astype(f32) for t in range(9)]
    k_in = [k_in_ref[t].astype(f32) for t in range(9)]
    in_rows = []
    out_rows = []
    zero = jnp.zeros((slot, hid), f32)
    for b in range(3):
        forward = [3 * a + b for a in range(3)]
        backward = [8 - t for t in forward]
        for u in range(2):
            at = slice(u * hid, (u + 1) * hid)
            w_mid_ref[b, at, :] = band([k_mid[t] for t in forward], u).astype(bf16)
            w_mid_t_ref[b, at, :] = band([k_mid_t[t] for t in backward], u).astype(bf16)
        head = [band([tall(k_out[t], slot) for t in forward], u) for u in range(2)]
        w_head_ref[2 * slot * b : 2 * slot * (b + 1), :] = jnp.concatenate(head, 0).astype(bf16)
        back = [band([tall(k_in[t], 8) for t in backward], u) for u in range(2)]
        w_in_t_ref[16 * b : 16 * (b + 1), :] = jnp.concatenate(back, 0).astype(bf16)
        for rows, blocks in (
            (in_rows, [tall(k_in[t], slot) for t in forward]),
            (out_rows, [tall(k_out[t], slot) for t in backward]),
        ):
            lower = jnp.concatenate(blocks + [zero], axis=0)
            upper = jnp.concatenate([zero] + blocks, axis=0)
            rows.append(jnp.concatenate([lower, upper], axis=1))
    w_in_ref[...] = jnp.concatenate(in_rows, axis=0).T.astype(bf16)
    w_out_t_ref[...] = jnp.concatenate(out_rows, axis=0).T.astype(bf16)
    for ref, bias in ((c_in_ref, b_in_ref[...]), (c_mid_ref, b_mid_ref[...])):
        ref[...] = jnp.broadcast_to(jnp.concatenate([bias, bias], axis=1), (128, 128)).T
    bias = jnp.concatenate([b_out_ref[...], jnp.zeros((1, slot - coef), f32)], axis=1)
    bias = jnp.concatenate([bias, bias, jnp.zeros((1, 128 - 2 * slot), f32)], axis=1)
    c_head_ref[...] = jnp.broadcast_to(bias, (128, 128)).T[: 2 * slot]


def paired(axis, first, last):
    even = lax.axis_index(axis) % 2 == 0
    return jnp.where(even, first, last), jnp.where(even, last, first)


def met(far, near, axis):
    count = lax.axis_size(axis)
    far_pairs = [(i, (i + 1 if i % 2 else i - 1) % count) for i in range(count)]
    near_pairs = [(i, i ^ 1) for i in range(count)]
    return lax.ppermute(far, axis, far_pairs), lax.ppermute(near, axis, near_pairs)


def swap(value, rows, cols):
    height, width = lax.axis_size("gx"), lax.axis_size("gy")
    pairs = [
        (i * width + j, (i ^ rows) * width + (j ^ cols)) for i in range(height) for j in range(width)
    ]
    return lax.ppermute(value, ("gx", "gy"), pairs)


def added(*values):
    sums = [v.astype(f32) for v in values]
    while len(sums) > 1:
        sums = [sums[k] + sums[k + 1] for k in range(0, len(sums), 2)]
    return sums[0].astype(bf16)


def summed(keep, send, beside):
    half = added(keep, swap(send, 0, 1))
    steps = [(0, 1 << k) for k in range(1, lax.axis_size("gy").bit_length() - 1)]
    steps += [(1 << k, 0) for k in range(lax.axis_size("gx").bit_length() - 1)]
    while steps:
        if len(steps) >= 2 and steps[0][0] == 0 and steps[1][1] == 0:
            (_, cols), (rows, _) = steps[:2]
            half = added(
                half,
                swap(half, 0, cols),
                swap(half, rows, 0),
                swap(half, rows, cols),
            )
            steps = steps[2:]
        else:
            arrived = swap(half, *steps[0])
            steps = steps[1:]
            if not steps:
                arrived, beside = lax.optimization_barrier((arrived, beside))
            half = added(half, arrived)
    return half, swap(half, 0, 1), beside


def per_device(velocity, kernel_in, bias_in, kernel_mid, bias_mid, kernel_out, bias_out, cotangent):
    rows, cols = velocity.shape[1], velocity.shape[2]
    ny_total = lax.axis_size("gy") * cols
    cell_count = lax.axis_size("gx") * rows * ny_total
    deep = rows + 2 * halo
    width = -(-(cols + 2 * halo) // 128) * 128
    vmem = pl.BlockSpec(memory_space=pltpu.VMEM)
    params = pltpu.CompilerParams(vmem_limit_bytes=18 << 20)

    core = (lax.axis_index("gy") % 2).astype(jnp.int32).reshape(1)
    smem = pl.BlockSpec(memory_space=pltpu.SMEM)
    hbm = pl.BlockSpec(memory_space=pltpu.HBM)
    w_in, w_mid, w_mid_t, w_out_t, w_head, w_in_t, b_in, b_mid, b_head = pl.pallas_call(
        weights_kernel,
        out_shape=(
            jax.ShapeDtypeStruct((2 * hid, 12 * slot), bf16),
            jax.ShapeDtypeStruct((3, 2 * hid, 4 * hid), bf16),
            jax.ShapeDtypeStruct((3, 2 * hid, 4 * hid), bf16),
            jax.ShapeDtypeStruct((2 * hid, 12 * slot), bf16),
            jax.ShapeDtypeStruct((6 * slot, 4 * hid), bf16),
            jax.ShapeDtypeStruct((48, 4 * hid), bf16),
            jax.ShapeDtypeStruct((128, 128), f32),
            jax.ShapeDtypeStruct((128, 128), f32),
            jax.ShapeDtypeStruct((2 * slot, 128), f32),
        ),
        in_specs=[hbm] * 6,
        out_specs=(vmem,) * 9,
        scratch_shapes=[
            pltpu.VMEM((9, 2, hid), bf16),
            pltpu.VMEM((9, hid, hid), bf16),
            pltpu.VMEM((coef, 3, 3, hid), bf16),
            pltpu.VMEM((1, hid), f32),
            pltpu.VMEM((1, hid), f32),
            pltpu.VMEM((1, coef), f32),
            pltpu.SemaphoreType.DMA((6,)),
        ],
        compiler_params=params,
        name="weights",
    )(
        in_hbm(jnp.transpose(kernel_in, (2, 3, 1, 0)).reshape(9, 2, hid)),
        in_hbm(jnp.transpose(kernel_mid, (2, 3, 0, 1)).reshape(9, hid, hid)),
        in_hbm(jnp.transpose(kernel_out, (0, 2, 3, 1))),
        in_hbm(bias_in[None, :]),
        in_hbm(bias_mid[None, :]),
        in_hbm(bias_out[None, :]),
    )
    columns = lax.iota(jnp.int32, width) - halo + lax.axis_index("gy") * cols
    forcing = forcing_amp * jnp.sin(2.0 * math.pi * forcing_wave * columns.astype(f32) / ny_total)
    even = (lax.axis_index("gy") % 2 == 0).astype(jnp.int32).reshape(1)
    edge = jax.ShapeDtypeStruct((4, rows, halo), bf16)
    fields, far, near = pl.pallas_call(
        pack_kernel,
        out_shape=(jax.ShapeDtypeStruct((4, rows, cols), f32), edge, edge),
        in_specs=[smem, hbm, hbm],
        out_specs=(vmem,) * 3,
        scratch_shapes=[pltpu.SemaphoreType.DMA((2,))],
        compiler_params=params,
        name="pack",
    )(even, in_hbm(velocity), in_hbm(cotangent))
    far, near = met(far, near, "gy")
    low, high = paired("gy", far, near)[0], paired("gy", near, far)[0]
    wide = jnp.concatenate([low.astype(f32), fields, high.astype(f32)], axis=2)
    first, last = (
        jnp.concatenate([low[:, at], fields[:, at].astype(bf16), high[:, at]], axis=2)
        for at in (slice(0, halo), slice(rows - halo, rows))
    )
    maps = (w_in, w_mid, w_mid_t, w_out_t, b_in, b_mid)
    far, near = paired("gx", first, last)
    near, maps = lax.optimization_barrier((near, maps))
    far, near = met(far, near, "gx")
    row_even = (lax.axis_index("gx") % 2 == 0).astype(jnp.int32).reshape(1)

    accs = (
        jax.ShapeDtypeStruct((3, 2 * hid, 4 * hid), f32),
        jax.ShapeDtypeStruct((2, 12 * slot, 2 * hid), f32),
        jax.ShapeDtypeStruct((2, 2 * hid, cols), f32),
    )
    edge = 2 * halo
    state = jax.ShapeDtypeStruct((2, 3, rows * slot, cols), bf16)
    sums = jax.ShapeDtypeStruct((slot, width), f32)

    def strips(count):
        return [jax.ShapeDtypeStruct((hid, count * pitch), kind) for kind in (bf16, bf16, f32)]

    act_one, slope_one, grad_two, act_two, grad_one, *totals = pl.pallas_call(
        lambda *refs: inner_kernel(rows, cols, *refs),
        out_shape=(
            jax.ShapeDtypeStruct((3, (rows - 2) * hid, cols), bf16),
            jax.ShapeDtypeStruct(((rows - 2) * hid, cols), f32),
            jax.ShapeDtypeStruct((3, (rows - 4) * hid, cols), bf16),
            jax.ShapeDtypeStruct(((rows - 4) * hid, cols), bf16),
            jax.ShapeDtypeStruct(((rows - 6) * hid, cols), bf16),
            *accs,
            state,
            sums,
            *strips(rows),
        ),
        in_specs=[vmem] * 7,
        out_specs=(vmem,) * 13,
        scratch_shapes=[
            pltpu.VMEM((4, rows, width), f32),
            pltpu.VMEM((width // 128, rows * slot, 128), f32),
        ],
        compiler_params=params,
        name="inner",
    )(wide, *maps)
    *totals, state_in, sums_in, strip_a, strip_b, strip_c = totals
    inner = (act_two, grad_one, strip_a, strip_b, strip_c)
    short = jax.ShapeDtypeStruct((hid // 2, 12 * hid), bf16)
    ends = jax.ShapeDtypeStruct((2, halo * hid, cols), bf16)
    keep, send, *outer = pl.pallas_call(
        lambda *refs: outer_kernel(rows, cols, *refs),
        out_shape=(short, short, ends, ends, *strips(2 * edge)),
        in_specs=[vmem] * 3 + [smem] * 2 + [vmem] * 15,
        out_specs=(vmem,) * 7,
        scratch_shapes=[
            *(pltpu.VMEM(acc.shape, f32) for acc in accs),
            pltpu.VMEM((2, *short.shape), bf16),
            pltpu.VMEM((4, 2 * edge, width), f32),
            pltpu.VMEM((width // 128, 2 * edge * slot, 128), f32),
            pltpu.VMEM((2, 3, 2 * edge * slot, cols), bf16),
            pltpu.VMEM((2, 3, halo * hid, cols), bf16),
            pltpu.VMEM((2, halo * hid, cols), f32),
            pltpu.VMEM((2, 3, halo * hid, cols), bf16),
        ],
        compiler_params=params,
        name="outer",
    )(
        wide,
        far,
        near,
        row_even,
        core,
        *maps,
        act_one,
        slope_one,
        grad_two,
        grad_one,
        state_in,
        *totals,
        sums_in,
    )

    new_velocity, grad_velocity = pl.pallas_call(
        lambda *refs: advance_kernel(rows, cols, *refs),
        out_shape=(jax.ShapeDtypeStruct(velocity.shape, f32),) * 2,
        in_specs=[vmem] * 3 + [smem] + [vmem] * 15,
        out_specs=(vmem,) * 2,
        scratch_shapes=[
            pltpu.VMEM((4, deep, width), f32),
            pltpu.VMEM((width // 128, deep * slot, 128), f32),
            pltpu.VMEM((width // 128, deep * 8, 128), f32),
        ],
        compiler_params=params,
        name="advance",
    )(
        wide,
        far,
        near,
        row_even,
        forcing[None, :],
        w_head,
        b_head,
        w_in_t,
        w_mid_t,
        *inner,
        *outer,
    )

    mine, other, (new_velocity, grad_velocity) = summed(
        keep, send, (new_velocity, grad_velocity)
    )
    g_in, gb_in, g_mid, gb_mid, g_out, gb_out = pl.pallas_call(
        lambda *refs: finish_kernel(1.0 / math.sqrt(cell_count), *refs),
        out_shape=(
            jax.ShapeDtypeStruct((9, 2, hid), f32),
            jax.ShapeDtypeStruct((1, hid), f32),
            jax.ShapeDtypeStruct((9, hid, hid), f32),
            jax.ShapeDtypeStruct((1, hid), f32),
            jax.ShapeDtypeStruct((coef, 3, 3, hid), f32),
            jax.ShapeDtypeStruct((1, coef), f32),
        ),
        in_specs=[vmem] * 2 + [smem],
        out_specs=(vmem,) * 6,
        compiler_params=params,
        name="finish",
    )(mine, other, core)

    return (
        new_velocity,
        grad_velocity,
        jnp.transpose(g_in.reshape(3, 3, 2, hid), (3, 2, 0, 1)),
        gb_in.reshape(hid),
        jnp.transpose(g_mid.reshape(3, 3, hid, hid), (2, 3, 0, 1)),
        gb_mid.reshape(hid),
        jnp.transpose(g_out, (0, 3, 1, 2)),
        gb_out.reshape(coef),
    )


def solution(mesh):
    in_specs = (P("groups", "gx", "gy"), P(), P(), P(), P(), P(), P(), P("groups", "gx", "gy"))
    out_specs = (
        P("groups", "gx", "gy"),
        P("groups", "gx", "gy"),
        P("groups", None, None, None),
        P("groups"),
        P("groups", None, None, None),
        P("groups"),
        P("groups", None, None, None),
        P("groups"),
    )
    return jax.shard_map(
        per_device, mesh=mesh, in_specs=in_specs, out_specs=out_specs, check_vma=False
    )
```

```python
import math

import jax
import jax.numpy as jnp
from jax import lax
from jax.experimental import pallas as pl
from jax.experimental.pallas import tpu as pltpu
from jax.sharding import PartitionSpec as P

advection = 0.2
viscosity = 0.05
forcing_amp = 0.05
forcing_wave = 4
face_base = ((0.0, 0.5, 0.0, 0.0, 0.5, 0.0), (0.0, 0.0, 0.5, 0.5, 0.0, 0.0))
halo = 4
hid = 64
coef = 12
slot = 16
side = 2 * halo
pitch = 2 * side
left_of, right_of = halo - 1, side + halo
taps_x = [(a, b) for a in (0, 1) for b in (-1, 0, 1)]
taps_y = [(a, b) for a in (-1, 0, 1) for b in (0, 1)]
f32 = jnp.float32
bf16 = jnp.bfloat16


def shift(value, rows, cols):
    if rows:
        value = pltpu.roll(value, (-rows) % value.shape[-2], value.ndim - 2)
    if cols:
        value = pltpu.roll(value, (-cols) % value.shape[-1], value.ndim - 1)
    return value


def mm(lhs, rhs):
    return lax.dot_general(lhs, rhs, (((1,), (0,)), ((), ())), preferred_element_type=f32)


def mm_nt(lhs, rhs):
    return lax.dot_general(lhs, rhs, (((1,), (1,)), ((), ())), preferred_element_type=f32)


def sigma_of(linear):
    return 0.5 * jnp.tanh(0.5 * linear) + 0.5


def with_lane(value, at, column):
    tiles = [value[:, k : k + 128] for k in range(0, value.shape[1], 128)]
    lane = lax.broadcasted_iota(jnp.int32, (1, 128), 1)
    tiles[at // 128] = jnp.where(lane == at % 128, column, tiles[at // 128])
    return jnp.concatenate(tiles, axis=1)


def strip_column(strip, row, at, to):
    source = row * pitch + at
    tile = strip[:, source // 128 * 128 : source // 128 * 128 + 128]
    return pltpu.roll(tile, (to - source) % 128, 1) if (to - source) % 128 else tile


def beside(low, middle, high, before, after):
    return (
        with_lane(shift(low, 0, -1), 0, before),
        middle,
        with_lane(shift(high, 0, 1), high.shape[1] - 1, after),
    )


def strip_taps(strip, columns=(-1, 0, 1)):
    return jnp.concatenate(
        [shift(strip, 0, a * pitch + b) for b in columns for a in (-1, 0, 1)], axis=0
    )


def strip_of(planes, rows, cols):
    lane = lax.broadcasted_iota(jnp.int32, (1, 128), 1)
    per_tile = 128 // pitch
    tiles = []
    for start in range(0, rows, per_tile):
        tile = jnp.zeros((slot, 128), f32)
        for k in range(min(per_tile, rows - start)):
            at = slice((start + k) * slot, (start + k + 1) * slot)
            pair = jnp.where(lane < side, planes[0, at, :], pltpu.roll(planes[cols // 128, at, :], side, 1))
            pair = pltpu.roll(pair, k * pitch, 1) if k else pair
            tile = jnp.where((lane >= k * pitch) & (lane < (k + 1) * pitch), pair, tile)
        tiles.append(tile)
    return jnp.concatenate(tiles, axis=1).astype(bf16)


class Rows:
    def __init__(self, size, *pieces):
        self.size = size
        self.pieces = pieces

    def get(self, lo, hi, lead=()):
        parts = []
        for start, stop, ref in self.pieces:
            first, last = max(lo, start), min(hi, stop)
            if first < last:
                rows = slice((first - start) * self.size, (last - start) * self.size)
                parts.append((first, ref[(*lead, rows, slice(None))]))
        parts = [part for _, part in sorted(parts, key=lambda item: item[0])]
        return parts[0] if len(parts) == 1 else jnp.concatenate(parts, axis=0)

    def put(self, lo, value, lead=()):
        for start, stop, ref in self.pieces:
            if start <= lo < stop:
                rows = slice((lo - start) * self.size, (lo - start) * self.size + value.shape[0])
                ref[(*lead, rows, slice(None))] = value

    def put_shifted(self, lo, value, strip, place):
        value = value.astype(bf16)
        ends = [
            jnp.concatenate([strip_column(strip, place(lo + k), at, to) for k in range(2)], axis=0)
            for at, to in ((left_of, 0), (right_of, value.shape[1] - 1))
        ]
        for b, shifted in enumerate(beside(value, value, value, *ends)):
            self.put(lo, shifted, (b,))

    def put_cut(self, lo, value, lead):
        value = value.astype(bf16)
        cols = self.pieces[0][2].shape[-1]
        for b in range(3):
            self.put(lo, shift(value, 0, halo - 1 + b)[:, :cols], (*lead, b))

    def window(self, lo, hi, lead=()):
        return jnp.concatenate([self.get(lo, hi, (*lead, b)) for b in range(3)], axis=0)


def put_plane(planes, k, stride, value):
    for j in range(planes.shape[0]):
        planes[j, pl.ds(k, value.shape[0], stride=stride), :] = value[:, 128 * j : 128 * j + 128]


def take_plane(planes, k, count, stride):
    tiles = [planes[j, pl.ds(k, count, stride=stride), :] for j in range(planes.shape[0])]
    return jnp.concatenate(tiles, axis=1)


def take_rows(planes, at, size):
    return jnp.concatenate([planes[j, at : at + size, :] for j in range(planes.shape[0])], axis=1)


def put_rows(planes, at, value):
    for j in range(planes.shape[0]):
        planes[j, at : at + value.shape[0], :] = value[:, 128 * j : 128 * j + 128]


def faces(w0, w1):
    normal_x = 0.5 * (w0 + shift(w0, 1, 0))
    normal_y = 0.5 * (w1 + shift(w1, 0, 1))
    return normal_x, normal_y


def shifted_fields(w):
    table = {}
    for b in (-1, 0, 1):
        col = shift(w, 0, b)
        for a in (-1, 0, 1):
            table[a, b] = shift(col, a, 0)
    return table


def lane_sums(total):
    lanes = total.shape[1]
    part = total[:, :128]
    for k in range(1, lanes // 128):
        part = part + total[:, 128 * k : 128 * k + 128]
    return jnp.sum(part.T, axis=0, keepdims=True)


def fill(stage, parts):
    stage[...] = jnp.zeros(stage.shape, f32)
    for at, part in parts:
        stage[:, at : at + part.shape[1], 0 : part.shape[2]] = part.astype(f32)


def prepare(place, cols, parts, stage, planes, state_in, state_rows, head_rows, sum_rows):
    height, width = stage.shape[1], stage.shape[2]
    count = height
    fill(stage, parts)
    w0, w1, c0, c1 = stage[0], stage[1], stage[2], stage[3]

    planes[...] = jnp.zeros(planes.shape, f32)
    put_plane(planes, 0, slot, w0)
    put_plane(planes, 1, slot, w1)
    for r in state_rows:
        state_in.put_cut(r, take_rows(planes, place(r) * slot, 2 * slot), (0,))
    strips = [strip_of(planes, count, cols)]

    normal_x, normal_y = faces(w0, w1)
    t0, t1 = shifted_fields(w0), shifted_fields(w1)
    fx0 = -advection * (c0 - shift(c0, 1, 0)) * normal_x
    fx1 = -advection * (c1 - shift(c1, 1, 0)) * normal_x
    fy0 = -advection * (c0 - shift(c0, 0, 1)) * normal_y
    fy1 = -advection * (c1 - shift(c1, 0, 1)) * normal_y
    lane = lax.broadcasted_iota(jnp.int32, (height, width), 1)
    row_id = lax.broadcasted_iota(jnp.int32, (height, width), 0)
    own = (lane >= halo) & (lane < halo + cols)
    inside = row_id < 0
    for lo, hi in sum_rows:
        inside = inside | ((row_id >= place(lo)) & (row_id <= place(hi - 1)))
    own = own & inside
    sums = []
    for at, taps, g0, g1 in ((0, taps_x, fx0, fx1), (6, taps_y, fy0, fy1)):
        raw = [g0 * t0[tap] + g1 * t1[tap] for tap in taps]
        mean = sum(raw[1:], raw[0]) * (1.0 / 6.0)
        for k in range(6):
            value = raw[k] - mean
            put_plane(planes, at + k, slot, value)
            sums.append(jnp.sum(jnp.where(own, value, 0.0), axis=0, keepdims=True))
    for r in head_rows:
        state_in.put_cut(r, take_rows(planes, place(r) * slot, 2 * slot), (1,))
    strips.append(strip_of(planes, count, cols))
    sums = jnp.concatenate(sums + [jnp.zeros((slot - coef, width), f32)], axis=0)
    return sums, strips


class Strips:
    def __init__(self, refs, state, head):
        self.refs, self.state, self.head = refs, state, head

    def spread(self, k):
        ref = self.refs[k]
        if k in (0, 3):
            parts = [ref[:hid, 4 * slot * b : (4 * b + 3) * slot] for b in range(3)]
        else:
            parts = [ref[b, :hid, : 3 * hid] for b in range(3)]
        return jnp.concatenate(parts, axis=1)

    def first(self):
        linear = mm(self.spread(0), strip_taps(self.state)) + self.refs[4][:hid, 0:1]
        sigma = sigma_of(linear)
        act = linear * sigma
        self.slope = sigma + act * (1.0 - sigma)
        self.act_one = act.astype(bf16)

    def second(self):
        linear = mm(self.spread(1), strip_taps(self.act_one)) + self.refs[5][:hid, 0:1]
        sigma = sigma_of(linear)
        act = linear * sigma
        grad = mm(self.spread(3), strip_taps(self.head)) * (sigma + act * (1.0 - sigma))
        self.act_two = act.astype(bf16)
        self.grad_two = grad.astype(bf16)

    def put(self, refs):
        for ref, value in zip(refs, (self.act_two, self.grad_two, self.slope), strict=True):
            ref[...] = value


def layers(
    rows,
    groups,
    refs,
    strips,
    place,
    state_in,
    act_one,
    slope_one,
    grad_two,
    act_two,
    grad_one,
    acc_mid,
    acc_small,
    bias_acc,
):
    w_in_ref, w_mid_ref, w_mid_t_ref, w_out_t_ref, b_in_ref, b_mid_ref = refs
    groups_one, groups_two, groups_back, groups_in = groups

    w_in = w_in_ref[...]
    b_in = b_in_ref[:, 0:1]
    strips.first()
    for r in groups_one:
        linear = mm(w_in, state_in.window(r - 1, r + 3, (0,))) + b_in
        sigma = sigma_of(linear)
        act = linear * sigma
        act_one.put_shifted(r, act, strips.act_one, place)
        slope_one.put(r, sigma + act * (1.0 - sigma))
        if r == groups_one[0]:
            strips.second()

    b_mid = b_mid_ref[:, 0:1]
    w_out_t = w_out_t_ref[...]
    w_mid = jnp.concatenate([w_mid_ref[b] for b in range(3)], axis=1)
    w_mid_t = jnp.concatenate([w_mid_t_ref[b] for b in range(3)], axis=1)
    held = []
    for r in groups_two:
        window = [act_one.get(r - 1, r + 3, (b,)) for b in range(3)]
        linear = mm(w_mid, jnp.concatenate(window, axis=0)) + b_mid
        sigma = sigma_of(linear)
        act = linear * sigma
        act_short = act.astype(bf16)
        act_two.put(r, act_short)
        fed = state_in.window(r - 1, r + 3, (1,))
        grad = mm(w_out_t, fed) * (sigma + act * (1.0 - sigma))
        grad_two.put_shifted(r, grad, strips.grad_two, place)
        if halo <= r < halo + rows:
            bias_acc[0] += grad
            held.append((grad.astype(bf16), window, fed, act_short))
        if held and (len(held) == 3 or r == groups_two[-1]):
            grads, windows, feds, acts = zip(*held)
            held = []
            grads = jnp.concatenate(grads, axis=1)
            for b in range(3):
                acc_mid[b] += mm_nt(grads, jnp.concatenate([w[b] for w in windows], axis=1))
            acc_small[0] += mm_nt(jnp.concatenate(feds, axis=1), jnp.concatenate(acts, axis=1))

    for r in groups_back:
        grad = mm(w_mid_t, grad_two.window(r - 1, r + 3)) * slope_one.get(r, r + 2)
        grad_one.put(r, grad.astype(bf16))
        if r < halo:
            bias_acc[1, hid:, :] += grad[hid:, :]
        elif r + 2 > halo + rows:
            bias_acc[1, :hid, :] += grad[:hid, :]
        else:
            bias_acc[1] += grad
    fed = jnp.concatenate([state_in.window(r - 1, r + 3, (0,)) for r in groups_in], axis=1)
    grads = jnp.concatenate([grad_one.get(r, r + 2) for r in groups_in], axis=1)
    acc_small[1] += mm_nt(fed, grads)


def inner_kernel(rows, cols, wide_ref, *refs):
    weight_refs, refs = refs[:6], refs[6:]
    act_one, slope_one, grad_two, act_two, grad_one, *refs = refs
    acc_mid, acc_small, bias_acc, state_ref, sums_ref, *strip_refs, stage, planes = refs
    low, high = halo, halo + rows
    state_in = Rows(slot, (low, high, state_ref))
    acc_mid[...] = jnp.zeros(acc_mid.shape, f32)
    acc_small[...] = jnp.zeros(acc_small.shape, f32)
    bias_acc[...] = jnp.zeros(bias_acc.shape, f32)
    pairs = range(low, high, 2)
    sums_ref[...], strips = prepare(
        lambda r: r - low,
        cols,
        [(0, wide_ref[...])],
        stage,
        planes,
        state_in,
        pairs,
        pairs,
        [(low + 2, high - 2)],
    )
    strips = Strips(weight_refs, *strips)
    layers(
        rows,
        [range(low + k, high - k, 2) for k in (1, 2, 3, 4)],
        weight_refs,
        strips,
        lambda r: r - low,
        state_in,
        Rows(hid, (low + 1, high - 1, act_one)),
        Rows(hid, (low + 1, high - 1, slope_one)),
        Rows(hid, (low + 2, high - 2, grad_two)),
        Rows(hid, (low + 2, high - 2, act_two)),
        Rows(hid, (low + 3, high - 3, grad_one)),
        acc_mid,
        acc_small,
        bias_acc,
    )
    strips.put(strip_refs)


def sides(far_ref, near_ref, even_ref):
    far, near = far_ref[...].astype(f32), near_ref[...].astype(f32)
    even = even_ref[0] == 1
    return jnp.where(even, far, near), jnp.where(even, near, far)


def outer_kernel(rows, cols, wide_ref, far_ref, near_ref, even_ref, core_ref, *refs):
    weight_refs, refs = refs[:6], refs[6:]
    act_one_in, slope_one_in, grad_two_in, grad_one_in, state_inner, *refs = refs
    acc_mid_in, acc_small_in, bias_in, sums_in, *refs = refs
    keep_ref, send_ref, act_two, grad_one, *refs = refs
    strip_refs, refs = refs[:3], refs[3:]
    acc_mid, acc_small, bias_acc, pay, stage, planes, state_edge, act_one, slope_one, grad_two = refs
    low, high, deep = halo, halo + rows, rows + 2 * halo
    acc_mid[...] = acc_mid_in[...]
    acc_small[...] = acc_small_in[...]
    bias_acc[...] = bias_in[...]
    edge, used = 2 * halo, 2 * halo - 2

    def place(r):
        return r if r < edge else r - (deep - 2 * edge)

    def both(k, edge_ref, inner_ref):
        return split_rows(
            hid, k, low + k, high - k, deep - k, edge_ref.at[0], inner_ref, edge_ref.at[1]
        )

    state_in = split_rows(
        slot,
        0,
        used,
        deep - used,
        deep,
        state_edge.at[:, :, 0 : used * slot, :],
        state_inner.at[:, :, 2 * slot : (rows - 2) * slot, :],
        state_edge.at[:, :, (2 * edge - used) * slot : 2 * edge * slot, :],
    )
    lower, upper = sides(far_ref, near_ref, even_ref)
    pairs = [*range(0, used, 2), *range(deep - used, deep, 2)]
    sums, strips = prepare(
        place,
        cols,
        [
            (0, lower),
            (halo, wide_ref[:, 0:halo, :]),
            (edge, wide_ref[:, rows - halo : rows, :]),
            (edge + halo, upper),
        ],
        stage,
        planes,
        state_in,
        pairs,
        pairs,
        [(low, low + 2), (high - 2, high)],
    )
    strips = Strips(weight_refs, *strips)
    layers(
        rows,
        [[*range(k, low + k, 2), *range(high - k, deep - k, 2)] for k in (1, 2, 3)]
        + [[low, low + 2, high - 4, high - 2]],
        weight_refs,
        strips,
        place,
        state_in,
        both(1, act_one, act_one_in),
        both(1, slope_one, slope_one_in),
        both(2, grad_two, grad_two_in),
        Rows(hid, (2, low + 2, act_two.at[0]), (high - 2, deep - 2, act_two.at[1])),
        both(3, grad_one, grad_one_in),
        acc_mid,
        acc_small,
        bias_acc,
    )
    strips.put(strip_refs)
    sums = sums + sums_in[...]
    bias_out = jnp.concatenate([sums, jnp.zeros((128 - slot, sums.shape[1]), f32)], axis=0)

    for b in range(3):
        total = acc_mid[b, :hid, : 3 * hid] + acc_mid[b, hid:, hid:]
        for a in range(3):
            t = 3 * a + b
            block = total[:, a * hid : (a + 1) * hid].astype(bf16)
            for h in range(2):
                pay[h, :, t * hid : (t + 1) * hid] = block[32 * h : 32 * h + 32]
    slots = []
    pieces = []
    for a in range(3):
        for b in range(3):
            at = (2 - b) * 4 * slot + (2 - a) * slot
            slots.append(
                acc_small[0, at : at + slot, :hid] + acc_small[0, at + slot : at + 2 * slot, hid:]
            )
            at = b * 4 * slot + a * slot
            pieces.append(
                acc_small[1, at : at + 2, :hid] + acc_small[1, at + slot : at + slot + 2, hid:]
            )
    sums_in, sums_mid = lane_sums(bias_acc[1]), lane_sums(bias_acc[0])
    pieces.append(sums_in[:, :hid] + sums_in[:, hid:])
    pieces.append(sums_mid[:, :hid] + sums_mid[:, hid:])
    pieces.append(lane_sums(bias_out)[:, :hid])
    pieces.append(jnp.zeros((11, hid), f32))
    rest = jnp.concatenate(pieces, axis=0)
    slots += [rest[:slot], rest[slot:], jnp.zeros((slot, hid), f32)]
    for h in range(2):
        for q in range(3):
            at = 6 * h + 2 * q
            block = jnp.concatenate(slots[at : at + 2], axis=0).astype(bf16)
            pay[h, :, (9 + q) * hid : (10 + q) * hid] = block
    core = core_ref[0]
    keep_ref[...] = pay[core]
    send_ref[...] = pay[1 - core]


def split_rows(size, first, low, high, last, lower_ref, inner_ref, upper_ref):
    return Rows(size, (first, low, lower_ref), (low, high, inner_ref), (high, last, upper_ref))


def advance_kernel(
    rows,
    cols,
    wide_ref,
    far_ref,
    near_ref,
    even_ref,
    forcing_ref,
    w_head_ref,
    b_head_ref,
    w_in_t_ref,
    w_mid_t_ref,
    *refs,
):
    inner, outer, (new_ref, grad_ref, stage, head, back) = refs[0:5], refs[5:10], refs[10:]
    act_two_in, grad_one_in = inner[:2]
    act_two_edge, grad_one_edge = outer[:2]
    edge = 2 * halo

    def whole(k):
        skip = 2 * pitch
        parts = [
            outer[k][:, : edge * pitch - skip],
            inner[k][:, skip : rows * pitch - skip],
            outer[k][:, edge * pitch + skip :],
        ]
        return jnp.concatenate(parts, axis=1)

    low, high, deep = halo, halo + rows, rows + 2 * halo
    act_two, grad_one = (
        split_rows(hid, k, low + k, high - k, deep - k, edge.at[0], inner, edge.at[1])
        for k, inner, edge in ((2, act_two_in, act_two_edge), (3, grad_one_in, grad_one_edge))
    )
    lower, upper = sides(far_ref, near_ref, even_ref)
    fill(stage, [(0, lower), (halo, wide_ref[...]), (halo + rows, upper)])
    w0, w1, c0, c1 = stage[0], stage[1], stage[2], stage[3]
    head[...] = jnp.zeros(head.shape, f32)
    back[...] = jnp.zeros(back.shape, f32)
    b_head = b_head_ref[:, 0:1]
    width = stage.shape[2]
    blank = jnp.zeros((2 * slot, width - cols), f32)

    def weighed(weight_ref, size, strip):
        weight = weight_ref[...]
        alone = [weight[2 * size * b : (2 * b + 1) * size, : 3 * hid] for b in range(3)]
        taps = strip_taps(strip, (0,))
        ends = mm(jnp.concatenate(alone, axis=0), taps)
        ends = [ends[b * size : (b + 1) * size] for b in range(3)]

        def pair(field, r):
            part = mm(weight, field.get(r - 1, r + 3))
            part = [part[2 * size * b : 2 * size * (b + 1)] for b in range(3)]
            around = [
                jnp.concatenate([strip_column(end, r + k, at, to) for k in range(2)], axis=0)
                for end, at, to in ((ends[0], left_of, 0), (ends[2], right_of, cols - 1))
            ]
            low, middle, high = beside(*part, *around)
            return low + middle + high

        return ends, pair

    ends, pair = weighed(w_head_ref, slot, whole(2))
    head_strip = b_head[:slot] + ends[1] + shift(ends[0], 0, -1) + shift(ends[2], 0, 1)
    for r in range(3, deep - 3, 2):
        out = jnp.concatenate([pair(act_two, r) + b_head, blank], axis=1)
        out = pltpu.roll(out, halo, 1)
        for at, to in ((left_of, halo - 1), (right_of, halo + cols)):
            column = [strip_column(head_strip, r + k, at, to) for k in range(2)]
            out = with_lane(out, to, jnp.concatenate(column, axis=0))
        put_rows(head, r * slot, out)
    spread = jnp.concatenate([w_mid_t_ref[b, :hid, : 3 * hid] for b in range(3)], axis=1)
    grad_one_strip = mm(spread, strip_taps(whole(3))) * whole(4)
    _, pair = weighed(w_in_t_ref, 8, grad_one_strip.astype(bf16))
    for r in range(halo, halo + rows, 2):
        out = jnp.concatenate([pair(grad_one, r), blank[:16]], axis=1)
        put_rows(back, r * 8, pltpu.roll(out, halo, 1))

    coefs = [take_plane(head, k, deep, slot) for k in range(coef)]
    mean_x = sum(coefs[1:6], coefs[0]) * (1.0 / 6.0)
    mean_y = sum(coefs[7:12], coefs[6]) * (1.0 / 6.0)
    sx = [coefs[k] - mean_x + face_base[0][k] for k in range(6)]
    sy = [coefs[6 + k] - mean_y + face_base[1][k] for k in range(6)]
    normal_x, normal_y = faces(w0, w1)
    grad_x = [-advection * (c - shift(c, 1, 0)) for c in (c0, c1)]
    grad_y = [-advection * (c - shift(c, 0, 1)) for c in (c0, c1)]
    normal_grad_x, normal_grad_y = 0.0, 0.0
    for c, (w, cot) in enumerate(((w0, c0), (w1, c1))):
        table = shifted_fields(w)
        face_x = sum(s * table[tap] for s, tap in zip(sx, taps_x))
        face_y = sum(s * table[tap] for s, tap in zip(sy, taps_y))
        flux_x = normal_x * face_x
        flux_y = normal_y * face_y
        normal_grad_x = normal_grad_x + grad_x[c] * face_x
        normal_grad_y = normal_grad_y + grad_y[c] * face_y
        around = table[1, 0] + table[-1, 0] + table[0, 1] + table[0, -1]
        new = (
            w
            - advection
            * (flux_x - shift(flux_x, -1, 0) + flux_y - shift(flux_y, 0, -1))
            + viscosity * (around - 4.0 * w)
        )
        if c == 0:
            new = new + forcing_ref[...]
        new_ref[c] = new[halo : halo + rows, halo : halo + cols]
    for c, cot in enumerate((c0, c1)):
        around = shift(cot, 1, 0) + shift(cot, -1, 0) + shift(cot, 0, 1) + shift(cot, 0, -1)
        total = cot + viscosity * (around - 4.0 * cot)
        flow_x = normal_x * grad_x[c]
        flow_y = normal_y * grad_y[c]
        by_col = {-1: {}, 0: {}, 1: {}}
        for s, (a, b) in zip(sx, taps_x):
            by_col[b][a] = by_col[b].get(a, 0.0) + flow_x * s
        for s, (a, b) in zip(sy, taps_y):
            by_col[b][a] = by_col[b].get(a, 0.0) + flow_y * s
        for b, column in by_col.items():
            part = sum(shift(value, -a, 0) for a, value in column.items())
            total = total + shift(part, 0, -b)
        if c == 0:
            total = total + 0.5 * (normal_grad_x + shift(normal_grad_x, -1, 0))
        else:
            total = total + 0.5 * (normal_grad_y + shift(normal_grad_y, 0, -1))
        total = total + take_plane(back, c, deep, 8)
        grad_ref[c] = total[halo : halo + rows, halo : halo + cols]


def finish_kernel(
    scale, mine_ref, other_ref, core_ref, in_ref, b_in_ref, mid_ref, b_mid_ref, out_ref, b_out_ref
):
    mine = mine_ref[...].astype(f32) * scale
    other = other_ref[...].astype(f32) * scale
    first = core_ref[0] == 0
    halves = (jnp.where(first, mine, other), jnp.where(first, other, mine))
    slots = []
    for h, half in enumerate(halves):
        for t in range(9):
            mid_ref[t, 32 * h : 32 * h + 32, :] = half[:, t * hid : (t + 1) * hid]
        for q in range(3):
            block = half[:, (9 + q) * hid : (10 + q) * hid]
            slots += [block[:slot], block[slot:]]
    for a in range(3):
        for b in range(3):
            out_ref[:, a, b, :] = slots[3 * a + b][:coef]
    for t in range(9):
        in_ref[t] = slots[9 + t // 8][2 * t % 16 : 2 * t % 16 + 2]
    b_in_ref[...] = slots[10][2:3]
    b_mid_ref[...] = slots[10][3:4]
    b_out_ref[...] = slots[10][4:5, :coef]


def in_hbm(array):
    return pltpu.with_memory_space_constraint(array, pltpu.HBM)


def fetched(sources, targets, sems):
    copies = [
        pltpu.make_async_copy(source, target, sems.at[k])
        for k, (source, target) in enumerate(zip(sources, targets))
    ]
    for copy in copies:
        copy.start()
    for copy in copies:
        copy.wait()


def pack_kernel(even_ref, velocity_ref, cotangent_ref, fields_ref, far_ref, near_ref, sems):
    cols = fields_ref.shape[2]
    fetched(
        (velocity_ref, cotangent_ref), (fields_ref.at[0:2], fields_ref.at[2:4]), sems
    )
    first = fields_ref[:, :, 0:halo].astype(bf16)
    last = fields_ref[:, :, cols - halo : cols].astype(bf16)
    even = even_ref[0] == 1
    far_ref[...] = jnp.where(even, first, last)
    near_ref[...] = jnp.where(even, last, first)


def weights_kernel(*refs):
    sources, refs = refs[:6], refs[6:]
    outs, (*inputs, sems) = refs[:9], refs[9:]
    fetched(sources, inputs, sems)
    k_in_ref, k_mid_ref, k_out_ref, b_in_ref, b_mid_ref, b_out_ref = inputs
    w_in_ref, w_mid_ref, w_mid_t_ref, w_out_t_ref, w_head_ref, w_in_t_ref, *outs = outs
    c_in_ref, c_mid_ref, c_head_ref = outs

    def band(block, upper):
        none = jnp.zeros(block[0].shape, f32)
        return jnp.concatenate([none, *block] if upper else [*block, none], axis=1)

    def tall(block, rows):
        return jnp.concatenate(
            [block, jnp.zeros((rows - block.shape[0], block.shape[1]), f32)], axis=0
        )

    k_mid = [k_mid_ref[t].astype(f32) for t in range(9)]
    k_mid_t = [k.T for k in k_mid]
    k_out = [k_out_ref[:, t // 3, t % 3, :].astype(f32) for t in range(9)]
    k_in = [k_in_ref[t].astype(f32) for t in range(9)]
    in_rows = []
    out_rows = []
    zero = jnp.zeros((slot, hid), f32)
    for b in range(3):
        forward = [3 * a + b for a in range(3)]
        backward = [8 - t for t in forward]
        for u in range(2):
            at = slice(u * hid, (u + 1) * hid)
            w_mid_ref[b, at, :] = band([k_mid[t] for t in forward], u).astype(bf16)
            w_mid_t_ref[b, at, :] = band([k_mid_t[t] for t in backward], u).astype(bf16)
        head = [band([tall(k_out[t], slot) for t in forward], u) for u in range(2)]
        w_head_ref[2 * slot * b : 2 * slot * (b + 1), :] = jnp.concatenate(head, 0).astype(bf16)
        back = [band([tall(k_in[t], 8) for t in backward], u) for u in range(2)]
        w_in_t_ref[16 * b : 16 * (b + 1), :] = jnp.concatenate(back, 0).astype(bf16)
        for rows, blocks in (
            (in_rows, [tall(k_in[t], slot) for t in forward]),
            (out_rows, [tall(k_out[t], slot) for t in backward]),
        ):
            lower = jnp.concatenate(blocks + [zero], axis=0)
            upper = jnp.concatenate([zero] + blocks, axis=0)
            rows.append(jnp.concatenate([lower, upper], axis=1))
    w_in_ref[...] = jnp.concatenate(in_rows, axis=0).T.astype(bf16)
    w_out_t_ref[...] = jnp.concatenate(out_rows, axis=0).T.astype(bf16)
    for ref, bias in ((c_in_ref, b_in_ref[...]), (c_mid_ref, b_mid_ref[...])):
        ref[...] = jnp.broadcast_to(jnp.concatenate([bias, bias], axis=1), (128, 128)).T
    bias = jnp.concatenate([b_out_ref[...], jnp.zeros((1, slot - coef), f32)], axis=1)
    bias = jnp.concatenate([bias, bias, jnp.zeros((1, 128 - 2 * slot), f32)], axis=1)
    c_head_ref[...] = jnp.broadcast_to(bias, (128, 128)).T[: 2 * slot]


def paired(axis, first, last):
    even = lax.axis_index(axis) % 2 == 0
    return jnp.where(even, first, last), jnp.where(even, last, first)


def met(far, near, axis):
    count = lax.axis_size(axis)
    far_pairs = [(i, (i + 1 if i % 2 else i - 1) % count) for i in range(count)]
    near_pairs = [(i, i ^ 1) for i in range(count)]
    return lax.ppermute(far, axis, far_pairs), lax.ppermute(near, axis, near_pairs)


def swap(value, rows, cols):
    height, width = lax.axis_size("gx"), lax.axis_size("gy")
    pairs = [
        (i * width + j, (i ^ rows) * width + (j ^ cols)) for i in range(height) for j in range(width)
    ]
    return lax.ppermute(value, ("gx", "gy"), pairs)


def added(*values):
    sums = [v.astype(f32) for v in values]
    while len(sums) > 1:
        sums = [sums[k] + sums[k + 1] for k in range(0, len(sums), 2)]
    return sums[0].astype(bf16)


def summed(keep, send, beside):
    half = added(keep, swap(send, 0, 1))
    steps = [(0, 1 << k) for k in range(1, lax.axis_size("gy").bit_length() - 1)]
    steps += [(1 << k, 0) for k in range(lax.axis_size("gx").bit_length() - 1)]
    while steps:
        if len(steps) >= 2 and steps[0][0] == 0 and steps[1][1] == 0:
            (_, cols), (rows, _) = steps[:2]
            tied, keep = lax.optimization_barrier((half, keep))
            half = added(
                half,
                swap(half, 0, cols),
                swap(half, rows, 0),
                swap(tied, rows, cols),
            )
            steps = steps[2:]
        else:
            arrived = swap(half, *steps[0])
            steps = steps[1:]
            if not steps:
                arrived, beside = lax.optimization_barrier((arrived, beside))
            half = added(half, arrived)
    return half, swap(half, 0, 1), beside


def per_device(velocity, kernel_in, bias_in, kernel_mid, bias_mid, kernel_out, bias_out, cotangent):
    rows, cols = velocity.shape[1], velocity.shape[2]
    ny_total = lax.axis_size("gy") * cols
    cell_count = lax.axis_size("gx") * rows * ny_total
    deep = rows + 2 * halo
    width = -(-(cols + 2 * halo) // 128) * 128
    vmem = pl.BlockSpec(memory_space=pltpu.VMEM)
    params = pltpu.CompilerParams(vmem_limit_bytes=18 << 20)

    core = (lax.axis_index("gy") % 2).astype(jnp.int32).reshape(1)
    smem = pl.BlockSpec(memory_space=pltpu.SMEM)
    hbm = pl.BlockSpec(memory_space=pltpu.HBM)
    w_in, w_mid, w_mid_t, w_out_t, w_head, w_in_t, b_in, b_mid, b_head = pl.pallas_call(
        weights_kernel,
        out_shape=(
            jax.ShapeDtypeStruct((2 * hid, 12 * slot), bf16),
            jax.ShapeDtypeStruct((3, 2 * hid, 4 * hid), bf16),
            jax.ShapeDtypeStruct((3, 2 * hid, 4 * hid), bf16),
            jax.ShapeDtypeStruct((2 * hid, 12 * slot), bf16),
            jax.ShapeDtypeStruct((6 * slot, 4 * hid), bf16),
            jax.ShapeDtypeStruct((48, 4 * hid), bf16),
            jax.ShapeDtypeStruct((128, 128), f32),
            jax.ShapeDtypeStruct((128, 128), f32),
            jax.ShapeDtypeStruct((2 * slot, 128), f32),
        ),
        in_specs=[hbm] * 6,
        out_specs=(vmem,) * 9,
        scratch_shapes=[
            pltpu.VMEM((9, 2, hid), bf16),
            pltpu.VMEM((9, hid, hid), bf16),
            pltpu.VMEM((coef, 3, 3, hid), bf16),
            pltpu.VMEM((1, hid), f32),
            pltpu.VMEM((1, hid), f32),
            pltpu.VMEM((1, coef), f32),
            pltpu.SemaphoreType.DMA((6,)),
        ],
        compiler_params=params,
        name="weights",
    )(
        in_hbm(jnp.transpose(kernel_in, (2, 3, 1, 0)).reshape(9, 2, hid)),
        in_hbm(jnp.transpose(kernel_mid, (2, 3, 0, 1)).reshape(9, hid, hid)),
        in_hbm(jnp.transpose(kernel_out, (0, 2, 3, 1))),
        in_hbm(bias_in[None, :]),
        in_hbm(bias_mid[None, :]),
        in_hbm(bias_out[None, :]),
    )
    columns = lax.iota(jnp.int32, width) - halo + lax.axis_index("gy") * cols
    forcing = forcing_amp * jnp.sin(2.0 * math.pi * forcing_wave * columns.astype(f32) / ny_total)
    even = (lax.axis_index("gy") % 2 == 0).astype(jnp.int32).reshape(1)
    edge = jax.ShapeDtypeStruct((4, rows, halo), bf16)
    fields, far, near = pl.pallas_call(
        pack_kernel,
        out_shape=(jax.ShapeDtypeStruct((4, rows, cols), f32), edge, edge),
        in_specs=[smem, hbm, hbm],
        out_specs=(vmem,) * 3,
        scratch_shapes=[pltpu.SemaphoreType.DMA((2,))],
        compiler_params=params,
        name="pack",
    )(even, in_hbm(velocity), in_hbm(cotangent))
    near, even = lax.optimization_barrier((near, even))
    far, near = met(far, near, "gy")
    low, high = paired("gy", far, near)[0], paired("gy", near, far)[0]
    wide = jnp.concatenate([low.astype(f32), fields, high.astype(f32)], axis=2)
    first, last = (
        jnp.concatenate([low[:, at], fields[:, at].astype(bf16), high[:, at]], axis=2)
        for at in (slice(0, halo), slice(rows - halo, rows))
    )
    maps = (w_in, w_mid, w_mid_t, w_out_t, b_in, b_mid)
    count = lax.axis_size("gx")
    last, maps = lax.optimization_barrier((last, maps))
    far = lax.ppermute(last, "gx", [(i, (i + 1) % count) for i in range(count)])
    near = lax.ppermute(first, "gx", [(i, (i - 1) % count) for i in range(count)])
    row_even = jnp.ones((1,), jnp.int32)

    accs = (
        jax.ShapeDtypeStruct((3, 2 * hid, 4 * hid), f32),
        jax.ShapeDtypeStruct((2, 12 * slot, 2 * hid), f32),
        jax.ShapeDtypeStruct((2, 2 * hid, cols), f32),
    )
    edge = 2 * halo
    state = jax.ShapeDtypeStruct((2, 3, rows * slot, cols), bf16)
    sums = jax.ShapeDtypeStruct((slot, width), f32)

    def strips(count):
        return [jax.ShapeDtypeStruct((hid, count * pitch), kind) for kind in (bf16, bf16, f32)]

    act_one, slope_one, grad_two, act_two, grad_one, *totals = pl.pallas_call(
        lambda *refs: inner_kernel(rows, cols, *refs),
        out_shape=(
            jax.ShapeDtypeStruct((3, (rows - 2) * hid, cols), bf16),
            jax.ShapeDtypeStruct(((rows - 2) * hid, cols), f32),
            jax.ShapeDtypeStruct((3, (rows - 4) * hid, cols), bf16),
            jax.ShapeDtypeStruct(((rows - 4) * hid, cols), bf16),
            jax.ShapeDtypeStruct(((rows - 6) * hid, cols), bf16),
            *accs,
            state,
            sums,
            *strips(rows),
        ),
        in_specs=[vmem] * 7,
        out_specs=(vmem,) * 13,
        scratch_shapes=[
            pltpu.VMEM((4, rows, width), f32),
            pltpu.VMEM((width // 128, rows * slot, 128), f32),
        ],
        compiler_params=params,
        name="inner",
    )(wide, *maps)
    *totals, state_in, sums_in, strip_a, strip_b, strip_c = totals
    inner = (act_two, grad_one, strip_a, strip_b, strip_c)
    short = jax.ShapeDtypeStruct((hid // 2, 12 * hid), bf16)
    ends = jax.ShapeDtypeStruct((2, halo * hid, cols), bf16)
    keep, send, *outer = pl.pallas_call(
        lambda *refs: outer_kernel(rows, cols, *refs),
        out_shape=(short, short, ends, ends, *strips(2 * edge)),
        in_specs=[vmem] * 3 + [smem] * 2 + [vmem] * 15,
        out_specs=(vmem,) * 7,
        scratch_shapes=[
            *(pltpu.VMEM(acc.shape, f32) for acc in accs),
            pltpu.VMEM((2, *short.shape), bf16),
            pltpu.VMEM((4, 2 * edge, width), f32),
            pltpu.VMEM((width // 128, 2 * edge * slot, 128), f32),
            pltpu.VMEM((2, 3, 2 * edge * slot, cols), bf16),
            pltpu.VMEM((2, 3, halo * hid, cols), bf16),
            pltpu.VMEM((2, halo * hid, cols), f32),
            pltpu.VMEM((2, 3, halo * hid, cols), bf16),
        ],
        compiler_params=params,
        name="outer",
    )(
        wide,
        far,
        near,
        row_even,
        core,
        *maps,
        act_one,
        slope_one,
        grad_two,
        grad_one,
        state_in,
        *totals,
        sums_in,
    )

    new_velocity, grad_velocity = pl.pallas_call(
        lambda *refs: advance_kernel(rows, cols, *refs),
        out_shape=(jax.ShapeDtypeStruct(velocity.shape, f32),) * 2,
        in_specs=[vmem] * 3 + [smem] + [vmem] * 15,
        out_specs=(vmem,) * 2,
        scratch_shapes=[
            pltpu.VMEM((4, deep, width), f32),
            pltpu.VMEM((width // 128, deep * slot, 128), f32),
            pltpu.VMEM((width // 128, deep * 8, 128), f32),
        ],
        compiler_params=params,
        name="advance",
    )(
        wide,
        far,
        near,
        row_even,
        forcing[None, :],
        w_head,
        b_head,
        w_in_t,
        w_mid_t,
        *inner,
        *outer,
    )

    mine, other, (new_velocity, grad_velocity) = summed(
        keep, send, (new_velocity, grad_velocity)
    )
    g_in, gb_in, g_mid, gb_mid, g_out, gb_out = pl.pallas_call(
        lambda *refs: finish_kernel(1.0 / math.sqrt(cell_count), *refs),
        out_shape=(
            jax.ShapeDtypeStruct((9, 2, hid), f32),
            jax.ShapeDtypeStruct((1, hid), f32),
            jax.ShapeDtypeStruct((9, hid, hid), f32),
            jax.ShapeDtypeStruct((1, hid), f32),
            jax.ShapeDtypeStruct((coef, 3, 3, hid), f32),
            jax.ShapeDtypeStruct((1, coef), f32),
        ),
        in_specs=[vmem] * 2 + [smem],
        out_specs=(vmem,) * 6,
        compiler_params=params,
        name="finish",
    )(mine, other, core)

    return (
        new_velocity,
        grad_velocity,
        jnp.transpose(g_in.reshape(3, 3, 2, hid), (3, 2, 0, 1)),
        gb_in.reshape(hid),
        jnp.transpose(g_mid.reshape(3, 3, hid, hid), (2, 3, 0, 1)),
        gb_mid.reshape(hid),
        jnp.transpose(g_out, (0, 3, 1, 2)),
        gb_out.reshape(coef),
    )


def solution(mesh):
    in_specs = (P("groups", "gx", "gy"), P(), P(), P(), P(), P(), P(), P("groups", "gx", "gy"))
    out_specs = (
        P("groups", "gx", "gy"),
        P("groups", "gx", "gy"),
        P("groups", None, None, None),
        P("groups"),
        P("groups", None, None, None),
        P("groups"),
        P("groups", None, None, None),
        P("groups"),
    )
    return jax.shard_map(
        per_device, mesh=mesh, in_specs=in_specs, out_specs=out_specs, check_vma=False
    )
```
